128 devices in a mesh: azim: 32 (over z, x_hi, y), rad: 4 (over x_lo, core).
Axes of the slice: x: 4 (x_hi: 2, x_lo: 2; x = x_hi * 2 + x_lo), y: 4, z: 4, core: 2. Of those that a mesh axis runs over, the one named last changes fastest.
Arguments:
- perturbation_in: float32 [512, 512, 256], P('azim', 'rad'), may hold values from -6 to 6
- coefficients: float32 [4, 29, 512, 512], P(None, None, 'azim', 'rad'), may hold values from -0.4 to 0.4
- wall_cells: int32 [131072], P(('azim', 'rad')), may hold values from 0 to 2047
- wall_count: int32 [128], P(('azim', 'rad')), may hold values from 1 to 1024, as said below
- mode_row: int32 [131072], P(('azim', 'rad')), may hold values from 0 to 4095
- mode_table: bfloat16 [4096, 512], replicated, may hold values from -0.03125 to 0.03125
Outputs:
- perturbation: float32 [512, 512, 256], P('azim', 'rad')
- markov: float32 [512, 256], P(('azim', 'rad'))
The draws below stay inside these ranges and needn't reach their ends.
Inputs may be any that keep to these rules, and one draw needn't show every extreme that they name: wall_count[t] counts the live slots of tile t; tiles in the azimuthal sectors nearest the 4 blades hold far more wall cells than the others, and some tile holds exactly 1024.
All inputs are finite; a program needn't handle non-finite values.
Results may differ from the reference program's by a relative error of at most 0.0004.
Values sent between devices are 32-bit elements; how exact they have to be, the bound alone decides.
No kernel may reach another device: no remote copies, remote signals or barrier semaphores. Data moves between devices by JAX's collectives and lax.ppermute only.
A program may use at most 320 MiB of HBM per device.

```python
import jax
import jax.numpy as jnp
from jax import lax

CA = 16
CR = 128
V = 4
C = 64
MODES = 512
SLOTS = 1024
PANELS = 4096
BLADES = 4
STEPS = 2
NA = 512
NR = 512
TILES = 128
N_AZIM = 32
N_RAD = 4


def draw_wall_count(key, part):
    key = jax.random.fold_in(key, 11)
    key_a, key_b, key_c, key_d = jax.random.split(key, 4)
    tiles = N_AZIM * N_RAD
    sector = jnp.arange(tiles, dtype=jnp.int32) // N_RAD
    spacing = max(N_AZIM // BLADES, 1)
    offset = jax.random.randint(key_a, (), 0, spacing)
    near = sector % spacing == offset
    light = jax.random.randint(key_b, (tiles,), max(SLOTS // 8, 1), max(SLOTS // 4, 1) + 1)
    heavy = jax.random.randint(key_c, (tiles,), max(SLOTS // 2, 1), SLOTS + 1)
    counts = jnp.where(near, heavy, light)
    top = jax.random.randint(key_d, (), 0, tiles)
    return counts.at[top].set(SLOTS).astype(jnp.int32)


def place_ends(array, rng, smallest, top_value):
    index_at = [jax.random.randint(jax.random.fold_in(rng, axis), (), 0, length) for axis, length in enumerate(array.shape)]
    main_axis = array.shape.index(max(array.shape))
    beside = index_at[:main_axis] + [(index_at[main_axis] + 1) % array.shape[main_axis]] + index_at[main_axis + 1:]
    return array.at[tuple(index_at)].set(smallest).at[tuple(beside)].set(top_value)


def levels(stream_key, extent, pieces, low, largest):
    def one(dim, parts):
        steps = jax.random.uniform(jax.random.fold_in(jax.random.fold_in(stream_key, 6), dim), (parts,), jnp.float32, low / len(pieces), largest / len(pieces))
        return jnp.repeat(jnp.exp(steps), extent[dim] // parts).reshape((-1,) + (1,) * (len(extent) - dim - 1))

    gain = one(*pieces[0])
    for cut in pieces[1:]:
        gain = gain * one(*cut)
    return gain


def centred(own_key, dims, scale, bound, pieces=(), kind=jnp.bfloat16):
    drawn = scale * jax.random.normal(own_key, dims, jnp.float32)
    if pieces:
        drawn = drawn * levels(own_key, dims, pieces, -0.22, 0.18)
    return jnp.clip(drawn, -bound, bound).astype(kind)


def setup_inputs(seed: int = 0) -> dict:
    seeds = jax.random.split(jax.random.key(seed), 7)
    perturbation_in = centred(seeds[0], (NA, NR, V * C), 1.0, 6.0, ((0, 32), (1, 4)), jnp.float32)
    coefficients = centred(seeds[1], (V, 25 + V, NA, NR), 0.08, 0.4, ((2, 32), (3, 4)), jnp.float32)
    wall_cells = place_ends(jax.random.randint(seeds[2], (TILES * SLOTS,), 0, CA * CR), jax.random.fold_in(seeds[2], 1), 0, (CA * CR) - 1).astype(jnp.int32)
    wall_count = draw_wall_count(jax.random.fold_in(seeds[6], 71), 0)
    mode_row = place_ends(jax.random.randint(seeds[4], (TILES * SLOTS,), 0, PANELS), jax.random.fold_in(seeds[4], 1), 0, PANELS - 1).astype(jnp.int32)
    mode_table = centred(seeds[5], (PANELS, MODES), (SLOTS * N_AZIM * N_RAD // 4) ** -0.5, 0.03125)
    return {"perturbation_in": perturbation_in, "coefficients": coefficients, "wall_cells": wall_cells, "wall_count": wall_count, "mode_row": mode_row, "mode_table": mode_table}


def flux(extended, coef, center):
    height = center.shape[0]
    width = center.shape[1]
    nvar = coef.shape[0]
    total = jnp.zeros((height, width, nvar, center.shape[2] // nvar), jnp.float32)
    for i in range(5):
        for j in range(5):
            piece = extended[i:i + height, j:j + width].reshape(height, width, nvar, -1)
            weight = jnp.transpose(coef[:, 5 * i + j], (1, 2, 0))[..., None]
            total = total + weight * piece
    couple = jnp.einsum('vwhx,hxwc->hxvc', coef[:, 25:], center.reshape(height, width, nvar, -1),
                        precision=lax.Precision.HIGHEST)
    return (total + couple).reshape(height, width, -1)


def rimmed(field):
    cycle = jnp.concatenate([field[-2:], field, field[:2]], axis=0)
    return jnp.pad(cycle, ((0, 0), (2, 2), (0, 0)))


def reference(perturbation_in, coefficients, wall_cells, wall_count, mode_row, mode_table):
    state = perturbation_in
    for step in range(STEPS):
        first = state + flux(rimmed(state), coefficients, state)
        state = 0.5 * (state + first + flux(rimmed(first), coefficients, first))
    tiles = N_AZIM * N_RAD
    slot_ids = jnp.arange(tiles * SLOTS, dtype=jnp.int32)
    tile_ids = slot_ids // SLOTS
    live = ((slot_ids % SLOTS) < wall_count[tile_ids]).astype(jnp.float32)
    azim_cell = (tile_ids // N_RAD) * CA + wall_cells // CR
    radial_cell = (tile_ids % N_RAD) * CR + wall_cells % CR
    rows = state[azim_cell, radial_cell]
    weights = mode_table[mode_row].astype(jnp.float32) * live[:, None]
    markov = lax.dot_general(weights, rows, (((0,), (0,)), ((), ())), precision=lax.Precision.HIGHEST)
    return state, markov
```

```python
import jax
import jax.numpy as jnp
from jax import lax
from jax.experimental import pallas as pl
from jax.experimental.pallas import tpu as pltpu
from jax.sharding import PartitionSpec as P

STEPS = 2
VMEM_LIMIT = 32 * 1024 * 1024
F32 = jnp.float32
BF16 = jnp.bfloat16


def spec(block, index):
    return pl.BlockSpec(block, index)


def params(n):
    return pltpu.CompilerParams(
        vmem_limit_bytes=VMEM_LIMIT, dimension_semantics=("arbitrary",) * n
    )


def lanes(shape):
    return lax.broadcasted_iota(jnp.int32, shape, len(shape) - 1)


def pack_into(edge_ref, row, var, value):
    base = (row % 8) * 16 + var * 4
    lane = lanes(value.shape)
    here = (lane >= base) & (lane < base + 4)
    old = edge_ref[row // 8]
    edge_ref[row // 8] = jnp.where(here, pltpu.roll(value, base + 2, axis=1), old)


def enter(x_ref, u_ref, edge_ref):
    step = pl.program_id(0)

    @pl.when(step % 2 == 0)
    def _():
        edge_ref[...] = jnp.zeros_like(edge_ref)

    lane = lanes((64, 128))
    for k in range(4):
        turned = x_ref[k].T
        for v in range(4):
            piece = turned[64 * v : 64 * v + 64]
            u_ref[k, v] = piece
            base = ((step % 2) * 4 + k) * 16 + v * 4
            here = (lane >= base) & (lane < base + 4)
            edge_ref[0] = jnp.where(here, pltpu.roll(piece, base + 2, axis=1), edge_ref[0])


def call_enter(x):
    return pl.pallas_call(
        enter,
        grid=(4,),
        in_specs=[spec((4, 128, 256), lambda s: (s, 0, 0))],
        out_specs=[
            spec((4, 4, 64, 128), lambda s: (s, 0, 0, 0)),
            spec((1, 64, 128), lambda s: (s // 2, 0, 0)),
        ],
        out_shape=[
            jax.ShapeDtypeStruct((16, 4, 64, 128), F32),
            jax.ShapeDtypeStruct((2, 64, 128), F32),
        ],
        compiler_params=params(1),
        name="enter",
    )(x)


def stencil(count, source, rim, weight, finish):
    lane = lanes((32, 128))
    open_rows = {}
    for s in range(count + 4):
        u = source(s)
        edge = rim(s)
        shifted = [
            pltpu.roll(jnp.where(lane >= 126, edge, u), 2, axis=1),
            pltpu.roll(jnp.where(lane >= 127, edge, u), 1, axis=1),
            u,
            pltpu.roll(jnp.where(lane < 1, edge, u), 127, axis=1),
            pltpu.roll(jnp.where(lane < 2, edge, u), 126, axis=1),
        ]
        for i in range(5):
            row = s - i
            if 0 <= row < count:
                total = open_rows.get(row)
                for j in range(5):
                    term = weight(5 * i + j, row) * shifted[j]
                    total = term if total is None else total + term
                open_rows[row] = total
        if s >= 4:
            finish(s - 4, open_rows.pop(s - 4))


def first_stage(u_ref, top_ref, bot_ref, cl_ref, cr_ref, tl_ref, tr_ref, bl_ref, br_ref,
                coef_ref, ctop_ref, cbot_ref, y_ref, edge_ref):
    var = pl.program_id(1)

    @pl.when(var == 0)
    def _():
        edge_ref[...] = jnp.zeros_like(edge_ref)

    def at(s, v):
        if s < 4:
            return top_ref[s, v]
        if s < 20:
            return u_ref[s - 4, v]
        return bot_ref[s - 20, v]

    from_left = lanes((32, 128)) % 4 < 2

    def rim(s):
        row = (s - 4) % 16
        if s < 4:
            both = jnp.where(from_left, tl_ref[...], tr_ref[...])
        elif s < 20:
            both = jnp.where(from_left, cl_ref[row // 8], cr_ref[row // 8])
        else:
            both = jnp.where(from_left, bl_ref[...], br_ref[...])
        return pltpu.roll(both, lax.rem(254 - (row % 8) * 16 - var * 4, 128), axis=1)

    def weight(k, row):
        if row < 2:
            line = ctop_ref[0, k, row : row + 1]
        elif row < 18:
            line = coef_ref[0, k, row - 2 : row - 1]
        else:
            line = cbot_ref[0, k, row - 18 : row - 17]
        return jnp.broadcast_to(line, (32, 128))

    def finish(row, total):
        for w in range(4):
            total = total + weight(25 + w, row) * at(row + 2, w)
        value = at(row + 2, var) + 0.5 * total
        y_ref[row, 0] = value
        pack_into(edge_ref, row, var, value)

    stencil(20, lambda s: at(s, var), rim, weight, finish)


def second_stage(y_ref, left_ref, right_ref, base_ref, coef_ref, u_ref, edge_ref):
    var = pl.program_id(1)

    @pl.when(var == 0)
    def _():
        edge_ref[...] = jnp.zeros_like(edge_ref)

    from_left = lanes((32, 128)) % 4 < 2

    def rim(s):
        both = jnp.where(from_left, left_ref[s // 8], right_ref[s // 8])
        return pltpu.roll(both, lax.rem(254 - (s % 8) * 16 - var * 4, 128), axis=1)

    def weight(k, row):
        return jnp.broadcast_to(coef_ref[0, k, row : row + 1], (32, 128))

    def finish(row, total):
        for w in range(4):
            total = total + weight(25 + w, row) * y_ref[row + 2, w]
        value = base_ref[row, 0] + total
        u_ref[row, 0] = value
        pack_into(edge_ref, row, var, value)

    stencil(16, lambda s: y_ref[s, var], rim, weight, finish)


def column_half(*lead):
    return spec(lead + (32, 128), lambda h, v: (0,) * len(lead) + (h, 0))


def one_variable(rows):
    return spec((rows, 1, 32, 128), lambda h, v: (0, v, h, 0))


def weights_of(rows):
    return spec((1, 29, rows, 128), lambda h, v: (v, 0, 0, 0))


def stage_cost(rows):
    return pl.CostEstimate(flops=2 * 29 * rows * 128 * 256, bytes_accessed=8 << 20, transcendentals=0)


def call_first(u, top, bot, edges, coef, ctop, cbot):
    return pl.pallas_call(
        first_stage,
        grid=(2, 4),
        in_specs=[column_half(16, 4), column_half(4, 4), column_half(4, 4),
                  column_half(2), column_half(2)] + [column_half()] * 4
        + [weights_of(16), weights_of(2), weights_of(2)],
        out_specs=[one_variable(20), column_half(3)],
        out_shape=[
            jax.ShapeDtypeStruct((20, 4, 64, 128), F32),
            jax.ShapeDtypeStruct((3, 64, 128), F32),
        ],
        compiler_params=params(2),
        cost_estimate=stage_cost(20),
        name="first_stage",
    )(u, top, bot, *edges, coef, ctop, cbot)


def call_second(y, left, right, base, coef):
    return pl.pallas_call(
        second_stage,
        grid=(2, 4),
        in_specs=[column_half(20, 4), column_half(3), column_half(3), one_variable(16), weights_of(16)],
        out_specs=[one_variable(16), column_half(2)],
        out_shape=[
            jax.ShapeDtypeStruct((16, 4, 64, 128), F32),
            jax.ShapeDtypeStruct((2, 64, 128), F32),
        ],
        compiler_params=params(2),
        cost_estimate=stage_cost(16),
        name="second_stage",
    )(y, left, right, base, coef)


def spread(cells_ref, weights_ref, high_ref, low_ref):
    step = pl.program_id(0)
    cell = lax.broadcasted_iota(jnp.int32, (256, 1024), 0) + step * 256
    hit = jnp.where(cells_ref[...] == cell, 1.0, 0.0).astype(BF16)
    total = jnp.dot(hit, weights_ref[...], preferred_element_type=F32)
    high = total.astype(BF16)
    high_ref[...] = high
    low_ref[...] = (total - high.astype(F32)).astype(BF16)


def call_spread(cells, weights):
    return pl.pallas_call(
        spread,
        grid=(8,),
        in_specs=[spec((1, 1024), lambda s: (0, 0)), spec((1024, 512), lambda s: (0, 0))],
        out_specs=[spec((256, 512), lambda s: (s, 0))] * 2,
        out_shape=[jax.ShapeDtypeStruct((2048, 512), BF16)] * 2,
        compiler_params=params(1),
        cost_estimate=pl.CostEstimate(flops=2 << 30, bytes_accessed=6 << 20, transcendentals=0),
        name="spread",
    )(cells, weights)


def leave(u_ref, high_ref, low_ref, out_ref, markov_ref, total):
    step = pl.program_id(0)
    grid = pl.num_programs(0)

    @pl.when(step == 0)
    def _():
        total[...] = jnp.zeros_like(total)

    rows = [u_ref[k].reshape(256, 128) for k in range(4)]
    for k in range(4):
        out_ref[k] = rows[k].T
    sums = total[...]
    for k in range(2):
        u = jnp.concatenate([rows[2 * k], rows[2 * k + 1]], axis=1)
        u_high = u.astype(BF16)
        u_low = (u - u_high.astype(F32)).astype(BF16)
        w_high = high_ref[256 * k : 256 * k + 256]
        w_low = low_ref[256 * k : 256 * k + 256]
        sums = sums + jnp.dot(u_high, w_high, preferred_element_type=F32)
        sums = sums + jnp.dot(u_low, w_high, preferred_element_type=F32)
        sums = sums + jnp.dot(u_high, w_low, preferred_element_type=F32)
    total[...] = sums

    @pl.when(step == grid - 1)
    def _():
        markov_ref[...] = total[...].T


def call_leave(u, high, low):
    return pl.pallas_call(
        leave,
        grid=(4,),
        in_specs=[spec((4, 4, 64, 128), lambda s: (s, 0, 0, 0))]
        + [spec((512, 512), lambda s: (s, 0))] * 2,
        out_specs=[spec((4, 128, 256), lambda s: (s, 0, 0)), spec((512, 256), lambda s: (0, 0))],
        out_shape=[
            jax.ShapeDtypeStruct((16, 128, 256), F32),
            jax.ShapeDtypeStruct((512, 256), F32),
        ],
        scratch_shapes=[pltpu.VMEM((256, 512), F32)],
        compiler_params=params(1),
        cost_estimate=pl.CostEstimate(flops=2 << 30, bytes_accessed=8 << 20, transcendentals=0),
        name="leave",
    )(u, high, low)


def shifts(n_azim, n_rad, da, dr):
    pairs = []
    for a in range(n_azim):
        for r in range(n_rad):
            if 0 <= r + dr < n_rad:
                pairs.append((a * n_rad + r, ((a + da) % n_azim) * n_rad + r + dr))
    return pairs


def body(perturbation_in, coefficients, wall_cells, wall_count, mode_row, mode_table):
    n_azim, n_rad = lax.axis_size("azim"), lax.axis_size("rad")

    def send(block, da, dr):
        return lax.ppermute(block, ("azim", "rad"), shifts(n_azim, n_rad, da, dr))

    slots = wall_cells.shape[0]
    live = jnp.arange(slots, dtype=jnp.int32) < wall_count[0]
    weights = jnp.where(live[:, None], jnp.take(mode_table, mode_row, axis=0), jnp.zeros((), BF16))
    high, low = call_spread(wall_cells.reshape(1, slots), weights)

    ctop = send(coefficients[:, :, 14:], 1, 0)
    cbot = send(coefficients[:, :, :2], -1, 0)
    u, edge = call_enter(perturbation_in)
    for step in range(STEPS):
        top = send(u[12:], 1, 0)
        bot = send(u[:4], -1, 0)
        edges = [
            send(edge, 0, 1), send(edge, 0, -1),
            send(edge[1], 1, 1), send(edge[1], 1, -1),
            send(edge[0], -1, 1), send(edge[0], -1, -1),
        ]
        y, rims = call_first(u, top, bot, edges, coefficients, ctop, cbot)
        u, edge = call_second(y, send(rims, 0, 1), send(rims, 0, -1), u, coefficients)
    out, term = call_leave(u, high, low)
    count = n_azim * n_rad
    parts = lax.all_to_all(term.reshape(count, -1, term.shape[1]), ("azim", "rad"), 0, 0)
    return out, jnp.sum(parts, axis=0)


def solution(mesh):
    return jax.shard_map(
        body,
        mesh=mesh,
        in_specs=(
            P("azim", "rad", None),
            P(None, None, "azim", "rad"),
            P(("azim", "rad")),
            P(("azim", "rad")),
            P(("azim", "rad")),
            P(),
        ),
        out_specs=(P("azim", "rad", None), P(("azim", "rad"), None)),
        check_vma=False,
    )
```

```python
import jax
import jax.numpy as jnp
from jax import lax
from jax.experimental import pallas as pl
from jax.experimental.pallas import tpu as pltpu
from jax.sharding import PartitionSpec as P

STEPS = 2
VMEM_LIMIT = 32 * 1024 * 1024
F32 = jnp.float32
BF16 = jnp.bfloat16


def spec(block, index):
    return pl.BlockSpec(block, index)


def whole(n):
    return [pl.BlockSpec(memory_space=pltpu.VMEM)] * n


def params(n=0):
    order = ("arbitrary",) * n if n else None
    return pltpu.CompilerParams(vmem_limit_bytes=VMEM_LIMIT, dimension_semantics=order)


def cost(rows):
    return pl.CostEstimate(flops=2 * 29 * rows * 128 * 256, bytes_accessed=rows << 18, transcendentals=0)


def arrays(*shapes):
    return [jax.ShapeDtypeStruct(shape, F32) for shape in shapes]


def lanes(shape):
    return lax.broadcasted_iota(jnp.int32, shape, len(shape) - 1)


ROWS = 256
TAIL = 4 * ROWS


def window(ref, row, var, half):
    start = pl.multiple_of(row * ROWS + var * 64 + half * 32, 32)
    return ref[pl.ds(start, 32), :]


def put(ref, row, var, half, value):
    start = pl.multiple_of(row * ROWS + var * 64 + half * 32, 32)
    ref[pl.ds(start, 32), :] = value


def pick(parts, row, var, half):
    for first, stop, ref in parts:
        if first <= row < stop:
            return window(ref, row - first, var, half)
    raise IndexError(row)


def place(pack, row, value):
    lane = lanes(value.shape)
    base = 4 * (row + 4)
    here = (lane >= base) & (lane < base + 4)
    return jnp.where(here, pltpu.roll(value, (base + 2) % 128, axis=1), pack)


def unplace(pack, row):
    lane = lanes(pack.shape)
    base = 4 * (row + 4)
    turned = pltpu.roll(pack, (126 - base) % 128, axis=1)
    return jnp.where((lane < 2) | (lane >= 126), turned, 0.0)


def each_part(body):
    @pl.loop(0, 8)
    def _(step):
        body(step // 2, step % 2)


def sweep(first, stop, source, weight, finish, shift_ref, block=4):
    lane = lanes((32, 128))
    for s in range(first - 2, stop + 2):
        u = source(s)
        k = s - first + 2
        shift_ref[0, k] = jnp.where(lane >= 2, pltpu.roll(u, 2, axis=1), 0.0)
        shift_ref[1, k] = jnp.where(lane >= 1, pltpu.roll(u, 1, axis=1), 0.0)
        shift_ref[2, k] = jnp.where(lane < 127, pltpu.roll(u, 127, axis=1), 0.0)
        shift_ref[3, k] = jnp.where(lane < 126, pltpu.roll(u, 126, axis=1), 0.0)
    for begin in range(first, stop, block):
        totals = [None] * block
        for s in range(begin - 2, begin + block + 2):
            k = s - first + 2
            for j in range(5):
                x = source(s) if j == 2 else shift_ref[j - (j > 2), k]
                for b in range(block):
                    i = s + 2 - begin - b
                    if 0 <= i < 5:
                        term = weight(5 * i + j, begin + b) * x
                        totals[b] = term if totals[b] is None else totals[b] + term
        for b in range(block):
            finish(begin + b, totals[b])


def line_of(coef_ref, var, k, row):
    return jnp.broadcast_to(coef_ref[var, k, row : row + 1], (32, 128))


def tail_line(ref, var, k, row):
    lines = ref.at[pl.ds(pl.multiple_of(TAIL + var * 64, 64), 64)]
    return jnp.broadcast_to(lines[2 * k + row : 2 * k + row + 1], (32, 128))


def enter(x_ref, coef_ref, low_ref, mid_ref, high_ref):
    low_ref[TAIL:] = jnp.zeros((256, 128), F32)
    high_ref[TAIL:] = jnp.zeros((256, 128), F32)

    @pl.loop(0, 4)
    def _(k):
        at = pl.ds(pl.multiple_of(k * ROWS, ROWS), ROWS)
        low_ref[at] = x_ref[k].T
        mid_ref[at] = x_ref[k + 4].T
        mid_ref[pl.ds(pl.multiple_of((k + 4) * ROWS, ROWS), ROWS)] = x_ref[k + 8].T
        high_ref[at] = x_ref[k + 12].T
        lines = pl.ds(pl.multiple_of(TAIL + k * 64, 64), 58)
        low_ref[lines] = coef_ref[k, :, 0:2].reshape(58, 128)
        high_ref[lines] = coef_ref[k, :, 14:16].reshape(58, 128)


def call_enter(x, coef):
    return pl.pallas_call(
        enter,
        in_specs=whole(2),
        out_specs=whole(3),
        out_shape=arrays((TAIL + 256, 128), (8 * ROWS, 128), (TAIL + 256, 128)),
        compiler_params=params(),
        name="enter",
    )(x, coef)


def inner_first(low_ref, mid_ref, high_ref, coef_ref, y_ref, edge_y_ref, edge_u_ref, shift_ref):
    parts = ((0, 4, low_ref), (4, 12, mid_ref), (12, 16, high_ref))

    def one(var, half):
        at = pl.ds(pl.multiple_of(half * 32, 32), 32)

        def finish(row, total):
            for w in range(4):
                total = total + line_of(coef_ref, var, 25 + w, row) * pick(parts, row, w, half)
            put(y_ref, row - 2, var, half, pick(parts, row, var, half) + 0.5 * total)

        sweep(
            2, 14, lambda s: pick(parts, s, var, half),
            lambda k, row: line_of(coef_ref, var, k, row), finish, shift_ref,
        )
        pack = jnp.zeros((32, 128), F32)
        for row in range(16):
            pack = place(pack, row, pick(parts, row, var, half))
        edge_u_ref[var, at] = pack
        pack = jnp.zeros((32, 128), F32)
        for row in range(2, 14):
            pack = place(pack, row, window(y_ref, row - 2, var, half))
        edge_y_ref[var, at] = pack

    each_part(one)


def call_inner_first(low, mid, high, coef):
    return pl.pallas_call(
        inner_first,
        in_specs=whole(4),
        out_specs=whole(3),
        out_shape=arrays((12 * ROWS, 128), (4, 64, 128), (4, 64, 128)),
        scratch_shapes=[pltpu.VMEM((4, 16, 32, 128), F32)],
        compiler_params=params(),
        cost_estimate=cost(12),
        name="inner_first",
    )(low, mid, high, coef)


def halo_edges(top_ref, bot_ref, edge_ref, out_ref):
    def one(var, half):
        at = pl.ds(pl.multiple_of(half * 32, 32), 32)
        pack = edge_ref[var, at]
        for k in range(4):
            pack = place(pack, k - 4, window(top_ref, k, var, half))
            pack = place(pack, k + 16, window(bot_ref, k, var, half))
        out_ref[var, at] = pack

    each_part(one)


def call_halo_edges(top, bot, edge):
    return pl.pallas_call(
        halo_edges,
        in_specs=whole(3),
        out_specs=whole(1)[0],
        out_shape=arrays((4, 64, 128))[0],
        compiler_params=params(),
        name="halo_edges",
    )(top, bot, edge)


def outer_first(top_ref, low_ref, high_ref, bot_ref, coef_ref, ctop_ref, cbot_ref, edge_ref,
                y_low_ref, y_high_ref, edge_y_ref, shift_ref):
    parts = ((-4, 0, top_ref), (0, 4, low_ref), (12, 16, high_ref), (16, 20, bot_ref))

    def one(var, half):
        at = pl.ds(pl.multiple_of(half * 32, 32), 32)

        def weight(k, row):
            if row < 0:
                return tail_line(ctop_ref, var, k, row + 2)
            if row < 16:
                return line_of(coef_ref, var, k, row)
            return tail_line(cbot_ref, var, k, row - 16)

        def finish(row, total):
            for w in range(4):
                total = total + weight(25 + w, row) * pick(parts, row, w, half)
            value = pick(parts, row, var, half) + 0.5 * total
            if row < 2:
                put(y_low_ref, row + 2, var, half, value)
            else:
                put(y_high_ref, row - 14, var, half, value)

        for first in (-2, 14):
            sweep(first, first + 4, lambda s: pick(parts, s, var, half), weight, finish, shift_ref)
        pack = edge_ref[var, at]
        for k in range(4):
            pack = place(pack, k - 2, window(y_low_ref, k, var, half))
            pack = place(pack, k + 14, window(y_high_ref, k, var, half))
        edge_y_ref[var, at] = pack

    each_part(one)


def call_outer_first(top, low, high, bot, coef, ctop, cbot, edge):
    return pl.pallas_call(
        outer_first,
        in_specs=whole(8),
        out_specs=whole(3),
        out_shape=arrays((4 * ROWS, 128), (4 * ROWS, 128), (4, 64, 128)),
        scratch_shapes=[pltpu.VMEM((4, 8, 32, 128), F32)],
        compiler_params=params(),
        cost_estimate=cost(8),
        name="outer_first",
    )(top, low, high, bot, coef, ctop, cbot, edge)


def edge_weights(coef_ref, ctop_ref, cbot_ref, out_ref):
    lane = lanes((1, 128))
    inner = (lane % 4 == 1) | (lane % 4 == 2)

    @pl.loop(0, 4)
    def _(var):
        top = ctop_ref.at[pl.ds(pl.multiple_of(TAIL + var * 64, 64), 64)]
        bot = cbot_ref.at[pl.ds(pl.multiple_of(TAIL + var * 64, 64), 64)]

        def line(k, row):
            if row < 0:
                return top[2 * k + row + 2 : 2 * k + row + 3]
            if row < 16:
                return coef_ref[var, k, row : row + 1]
            return bot[2 * k + row - 16 : 2 * k + row - 15]

        for i in range(5):
            far = jnp.zeros((1, 128), F32)
            near = jnp.zeros((1, 128), F32)
            for row in range(-2, 18):
                far = place(far, row, jnp.where(lane < 64, line(5 * i, row), line(5 * i + 4, row)))
                near = place(near, row, jnp.where(lane < 64, line(5 * i + 1, row), line(5 * i + 3, row)))
            out_ref[var, i : i + 1] = far
            out_ref[var, 5 + i : 6 + i] = jnp.where(inner, near, 0.0)


def call_edge_weights(coef, ctop, cbot):
    return pl.pallas_call(
        edge_weights,
        in_specs=whole(3),
        out_specs=whole(1)[0],
        out_shape=arrays((4, 10, 128))[0],
        compiler_params=params(),
        name="edge_weights",
    )(coef, ctop, cbot)


def beyond(left_ref, right_ref, weight_ref, var):
    lane = lanes((64, 128)) % 4
    rim = jnp.where(
        lane < 2, pltpu.roll(right_ref[var], 126, axis=1), pltpu.roll(left_ref[var], 2, axis=1)
    )
    other = jnp.where(lane == 1, pltpu.roll(rim, 1, axis=1), pltpu.roll(rim, 127, axis=1))
    total = jnp.zeros((64, 128), F32)
    for i in range(5):
        turn = (4 * (2 - i)) % 128
        far, near = rim, other
        if turn:
            far, near = pltpu.roll(rim, turn, axis=1), pltpu.roll(other, turn, axis=1)
        total = total + weight_ref[var, i : i + 1] * far
        total = total + weight_ref[var, 5 + i : 6 + i] * near
    return total


def mend_edges(left_ref, right_ref, weight_ref, edge_ref, out_ref, mend_ref):
    @pl.loop(0, 4)
    def _(var):
        mend = 0.5 * beyond(left_ref, right_ref, weight_ref, var)
        mend_ref[var] = mend
        out_ref[var] = edge_ref[var] + mend


def call_mend_edges(left, right, weights, edge):
    return pl.pallas_call(
        mend_edges,
        in_specs=whole(4),
        out_specs=whole(2),
        out_shape=arrays((4, 64, 128), (4, 64, 128)),
        compiler_params=params(),
        name="mend_edges",
    )(left, right, weights, edge)


def second(y_low_ref, y_mid_ref, y_high_ref, mend_ref, low_ref, mid_ref, high_ref, coef_ref,
           out_ref, y_ref, shift_ref):
    y_parts = ((-2, 2, y_low_ref), (2, 14, y_mid_ref), (14, 18, y_high_ref))
    u_parts = ((0, 4, low_ref), (4, 12, mid_ref), (12, 16, high_ref))
    whole_y = ((-2, 18, y_ref),)

    def mend(var, half):
        pack = mend_ref[var, pl.ds(pl.multiple_of(half * 32, 32), 32)]
        for row in range(-2, 18):
            put(y_ref, row + 2, var, half, pick(y_parts, row, var, half) + unplace(pack, row))

    each_part(mend)

    def one(var, half):
        def finish(row, total):
            for w in range(4):
                total = total + line_of(coef_ref, var, 25 + w, row) * pick(whole_y, row, w, half)
            put(out_ref, row, var, half, pick(u_parts, row, var, half) + total)

        sweep(
            0, 16, lambda s: pick(whole_y, s, var, half),
            lambda k, row: line_of(coef_ref, var, k, row), finish, shift_ref,
        )

    each_part(one)


def call_second(y_low, y_mid, y_high, mend, low, mid, high, coef):
    return pl.pallas_call(
        second,
        in_specs=whole(8),
        out_specs=whole(1)[0],
        out_shape=arrays((16 * ROWS, 128))[0],
        scratch_shapes=[pltpu.VMEM((20 * ROWS, 128), F32), pltpu.VMEM((4, 20, 32, 128), F32)],
        compiler_params=params(),
        cost_estimate=cost(16),
        name="second",
    )(y_low, y_mid, y_high, mend, low, mid, high, coef)


def mend_state(left_ref, right_ref, weight_ref, u_ref, low_ref, mid_ref, high_ref, mend_ref):
    @pl.loop(0, 4)
    def _(var):
        mend_ref[var] = beyond(left_ref, right_ref, weight_ref, var)

    def one(var, half):
        pack = mend_ref[var, pl.ds(pl.multiple_of(half * 32, 32), 32)]
        for row in range(16):
            value = window(u_ref, row, var, half) + unplace(pack, row)
            for first, stop, ref in ((0, 4, low_ref), (4, 12, mid_ref), (12, 16, high_ref)):
                if first <= row < stop:
                    put(ref, row - first, var, half, value)

    each_part(one)


def call_mend_state(left, right, weights, u):
    return pl.pallas_call(
        mend_state,
        in_specs=whole(4),
        out_specs=whole(3),
        out_shape=arrays((4 * ROWS, 128), (8 * ROWS, 128), (4 * ROWS, 128)),
        scratch_shapes=[pltpu.VMEM((4, 64, 128), F32)],
        compiler_params=params(),
        name="mend_state",
    )(left, right, weights, u)


def spread(cells_ref, weights_ref, high_ref, low_ref):
    step = pl.program_id(0)
    cell = lax.broadcasted_iota(jnp.int32, (256, 1024), 0) + step * 256
    hit = jnp.where(cells_ref[...] == cell, 1.0, 0.0).astype(BF16)
    total = jnp.dot(hit, weights_ref[...], preferred_element_type=F32)
    high = total.astype(BF16)
    high_ref[...] = high
    low_ref[...] = (total - high.astype(F32)).astype(BF16)


def call_spread(cells, weights):
    return pl.pallas_call(
        spread,
        grid=(8,),
        in_specs=[spec((1, 1024), lambda s: (0, 0)), spec((1024, 512), lambda s: (0, 0))],
        out_specs=[spec((256, 512), lambda s: (s, 0))] * 2,
        out_shape=[jax.ShapeDtypeStruct((2048, 512), BF16)] * 2,
        compiler_params=params(1),
        cost_estimate=pl.CostEstimate(flops=2 << 30, bytes_accessed=6 << 20, transcendentals=0),
        name="spread",
    )(cells, weights)


def leave(low_ref, mid_ref, high_ref, w_high_ref, w_low_ref, out_ref, markov_ref):
    parts = ((0, 4, low_ref), (4, 12, mid_ref), (12, 16, high_ref))
    sums = jnp.zeros((256, 512), F32)
    for k in range(8):
        rows = []
        for row in (2 * k, 2 * k + 1):
            for first, stop, ref in parts:
                if first <= row < stop:
                    rows.append(ref[(row - first) * ROWS : (row - first + 1) * ROWS])
            out_ref[row] = rows[-1].T
        u = jnp.concatenate(rows, axis=1)
        u_high = u.astype(BF16)
        u_low = (u - u_high.astype(F32)).astype(BF16)
        w_high = w_high_ref[256 * k : 256 * k + 256]
        w_low = w_low_ref[256 * k : 256 * k + 256]
        sums = sums + jnp.dot(u_high, w_high, preferred_element_type=F32)
        sums = sums + jnp.dot(u_low, w_high, preferred_element_type=F32)
        sums = sums + jnp.dot(u_high, w_low, preferred_element_type=F32)
    markov_ref[...] = sums.T


def call_leave(low, mid, high, w_high, w_low):
    return pl.pallas_call(
        leave,
        in_specs=whole(5),
        out_specs=whole(2),
        out_shape=arrays((16, 128, 256), (512, 256)),
        compiler_params=params(),
        cost_estimate=pl.CostEstimate(flops=2 << 30, bytes_accessed=8 << 20, transcendentals=0),
        name="leave",
    )(low, mid, high, w_high, w_low)


def shifts(n_azim, n_rad, da, dr):
    pairs = []
    for a in range(n_azim):
        for r in range(n_rad):
            if 0 <= r + dr < n_rad:
                pairs.append((a * n_rad + r, ((a + da) % n_azim) * n_rad + r + dr))
    return pairs


def body(perturbation_in, coefficients, wall_cells, wall_count, mode_row, mode_table):
    n_azim, n_rad = lax.axis_size("azim"), lax.axis_size("rad")

    def send(block, da, dr):
        return lax.ppermute(block, ("azim", "rad"), shifts(n_azim, n_rad, da, dr))

    slots = wall_cells.shape[0]
    live = jnp.arange(slots, dtype=jnp.int32) < wall_count[0]
    weights = jnp.where(live[:, None], jnp.take(mode_table, mode_row, axis=0), jnp.zeros((), BF16))
    w_high, w_low = call_spread(wall_cells.reshape(1, slots), weights)

    low, mid, high = call_enter(perturbation_in, coefficients)
    tails = None
    for step in range(STEPS):
        top, bot = send(high, 1, 0), send(low, -1, 0)
        if tails is None:
            tails = top, bot
            edge_w = call_edge_weights(coefficients, *tails)
        y_mid, edge_y, edge_u = call_inner_first(low, mid, high, coefficients)
        edge_u = call_halo_edges(top, bot, edge_u)
        left, right = send(edge_u, 0, 1), send(edge_u, 0, -1)
        y_low, y_high, edge_y = call_outer_first(top, low, high, bot, coefficients, *tails, edge_y)
        edge_y, mend = call_mend_edges(left, right, edge_w, edge_y)
        left, right = send(edge_y, 0, 1), send(edge_y, 0, -1)
        u = call_second(y_low, y_mid, y_high, mend, low, mid, high, coefficients)
        low, mid, high = call_mend_state(left, right, edge_w, u)
    out, term = call_leave(low, mid, high, w_high, w_low)
    count = n_azim * n_rad
    parts = lax.all_to_all(term.reshape(count, -1, term.shape[1]), ("azim", "rad"), 0, 0)
    return out, jnp.sum(parts, axis=0)


def solution(mesh):
    return jax.shard_map(
        body,
        mesh=mesh,
        in_specs=(
            P("azim", "rad", None),
            P(None, None, "azim", "rad"),
            P(("azim", "rad")),
            P(("azim", "rad")),
            P(("azim", "rad")),
            P(),
        ),
        out_specs=(P("azim", "rad", None), P(("azim", "rad"), None)),
        check_vma=False,
    )
```

```python
import functools

import jax
import jax.numpy as jnp
from jax import lax
from jax.experimental import pallas as pl
from jax.experimental.pallas import tpu as pltpu
from jax.sharding import PartitionSpec as P

STEPS = 2
VMEM_LIMIT = 32 * 1024 * 1024
F32 = jnp.float32
BF16 = jnp.bfloat16


def spec(block, index):
    return pl.BlockSpec(block, index)


def whole(n):
    return [pl.BlockSpec(memory_space=pltpu.VMEM)] * n


def params(n=0):
    order = ("arbitrary",) * n if n else None
    return pltpu.CompilerParams(vmem_limit_bytes=VMEM_LIMIT, dimension_semantics=order)


def cost(rows):
    return pl.CostEstimate(flops=2 * 29 * rows * 128 * 256, bytes_accessed=rows << 18, transcendentals=0)


def arrays(*shapes):
    return [jax.ShapeDtypeStruct(shape, F32) for shape in shapes]


def lanes(shape):
    return lax.broadcasted_iota(jnp.int32, shape, len(shape) - 1)


ROWS = 256
TAIL = 4 * ROWS
COEF = 2 * ROWS


def window(ref, row, var, half):
    start = pl.multiple_of(row * ROWS + var * 64 + half * 32, 32)
    return ref[pl.ds(start, 32), :]


def put(ref, row, var, half, value):
    start = pl.multiple_of(row * ROWS + var * 64 + half * 32, 32)
    ref[pl.ds(start, 32), :] = value


def pick(parts, row, var, half):
    for first, stop, ref in parts:
        if first <= row < stop:
            return window(ref, row - first, var, half)
    raise IndexError(row)


def place(pack, row, value):
    lane = lanes(value.shape)
    base = 4 * (row + 4)
    here = (lane >= base) & (lane < base + 4)
    return jnp.where(here, pltpu.roll(value, (base + 2) % 128, axis=1), pack)


def place_far(pack, row, value):
    lane = lanes(value.shape)
    base = 4 * (row + 4)
    pack = jnp.where((lane >= base) & (lane < base + 2), pltpu.roll(value, (base + 4) % 128, axis=1), pack)
    return jnp.where((lane >= base + 2) & (lane < base + 4), pltpu.roll(value, base, axis=1), pack)


def unplace(pack, row):
    lane = lanes(pack.shape)
    base = 4 * (row + 4)
    turned = pltpu.roll(pack, (126 - base) % 128, axis=1)
    return jnp.where((lane < 2) | (lane >= 126), turned, 0.0)


def each_part(body):
    @pl.loop(0, 8)
    def _(step):
        body(step // 2, step % 2)


def sweep(first, stop, source, weight, finish, shift_ref, block=4):
    lane = lanes((32, 128))
    for s in range(first - 2, stop + 2):
        u = source(s)
        k = s - first + 2
        shift_ref[0, k] = jnp.where(lane >= 2, pltpu.roll(u, 2, axis=1), 0.0)
        shift_ref[1, k] = jnp.where(lane >= 1, pltpu.roll(u, 1, axis=1), 0.0)
        shift_ref[2, k] = jnp.where(lane < 127, pltpu.roll(u, 127, axis=1), 0.0)
        shift_ref[3, k] = jnp.where(lane < 126, pltpu.roll(u, 126, axis=1), 0.0)
    for begin in range(first, stop, block):
        totals = [None] * block
        for s in range(begin - 2, begin + block + 2):
            k = s - first + 2
            for j in range(5):
                x = source(s) if j == 2 else shift_ref[j - (j > 2), k]
                for b in range(block):
                    i = s + 2 - begin - b
                    if 0 <= i < 5:
                        term = weight(5 * i + j, begin + b) * x
                        totals[b] = term if totals[b] is None else totals[b] + term
        for b in range(block):
            finish(begin + b, totals[b])


def line_of(coef_ref, var, k, row):
    return jnp.broadcast_to(coef_ref[var, k, row : row + 1], (32, 128))


def tail_line(ref, var, k, row):
    lines = ref.at[pl.ds(pl.multiple_of(TAIL + var * 64, 64), 64)]
    return jnp.broadcast_to(lines[2 * k + row : 2 * k + row + 1], (32, 128))


def enter(x_ref, coef_ref, low_ref, mid_ref, high_ref):
    low_ref[TAIL:] = jnp.zeros((256, 128), F32)
    high_ref[TAIL:] = jnp.zeros((256, 128), F32)

    @pl.loop(0, 4)
    def _(k):
        at = pl.ds(pl.multiple_of(k * ROWS, ROWS), ROWS)
        low_ref[at] = x_ref[k].T
        mid_ref[at] = x_ref[k + 4].T
        mid_ref[pl.ds(pl.multiple_of((k + 4) * ROWS, ROWS), ROWS)] = x_ref[k + 8].T
        high_ref[at] = x_ref[k + 12].T
        lines = pl.ds(pl.multiple_of(TAIL + k * 64, 64), 58)
        low_ref[lines] = coef_ref[k, :, 0:2].reshape(58, 128)
        high_ref[lines] = coef_ref[k, :, 14:16].reshape(58, 128)


def call_enter(x, coef):
    return pl.pallas_call(
        enter,
        in_specs=whole(2),
        out_specs=whole(3),
        out_shape=arrays((TAIL + 256, 128), (8 * ROWS, 128), (TAIL + 256, 128)),
        compiler_params=params(),
        name="enter",
    )(x, coef)


def inner_first(low_ref, mid_ref, high_ref, coef_ref, y_ref, edge_ref, shift_ref):
    parts = ((0, 4, low_ref), (4, 12, mid_ref), (12, 16, high_ref))

    def one(var, half):
        def finish(row, total):
            for w in range(4):
                total = total + line_of(coef_ref, var, 25 + w, row) * pick(parts, row, w, half)
            put(y_ref, row - 2, var, half, pick(parts, row, var, half) + 0.5 * total)

        sweep(
            2, 14, lambda s: pick(parts, s, var, half),
            lambda k, row: line_of(coef_ref, var, k, row), finish, shift_ref,
        )
        near = jnp.zeros((32, 128), F32)
        far = jnp.zeros((32, 128), F32)
        for row in range(16):
            value = pick(parts, row, var, half)
            near, far = place(near, row, value), place_far(far, row, value)
        put(edge_ref, 0, var, half, near)
        put(edge_ref, 1, var, half, far)

    each_part(one)


def call_inner_first(low, mid, high, coef):
    return pl.pallas_call(
        inner_first,
        in_specs=whole(4),
        out_specs=whole(2),
        out_shape=arrays((12 * ROWS, 128), (2 * ROWS, 128)),
        scratch_shapes=[pltpu.VMEM((4, 16, 32, 128), F32)],
        compiler_params=params(),
        cost_estimate=cost(12),
        name="inner_first",
    )(low, mid, high, coef)


def coef_edges(coef_ref, out_ref):
    out_ref[...] = jnp.zeros_like(out_ref)
    for var in range(4):
        pack = jnp.zeros((29, 128), F32)
        for row in range(16):
            pack = place(pack, row, coef_ref[pl.ds(var * 464 + row, 29, stride=16), :])
        out_ref[32 * var : 32 * var + 29] = pack


def call_coef_edges(coef):
    return pl.pallas_call(
        coef_edges,
        in_specs=whole(1),
        out_specs=whole(1)[0],
        out_shape=arrays((128, 128))[0],
        compiler_params=params(),
        name="coef_edges",
    )(coef.reshape(-1, 128))


def halo_edges(top_ref, bot_ref, edge_ref, *refs):
    out_ref = refs[-1]

    def one(var, half):
        near = window(edge_ref, 0, var, half)
        far = window(edge_ref, 1, var, half)
        for k in range(4):
            for row, ref in ((k - 4, top_ref), (k + 16, bot_ref)):
                value = window(ref, k, var, half)
                near, far = place(near, row, value), place_far(far, row, value)
        put(out_ref, 0, var, half, near)
        put(out_ref, 1, var, half, far)

    each_part(one)
    if len(refs) == 2:
        for var in range(4):
            pack = refs[0][32 * var : 32 * var + 29]
            for k in range(2):
                lines = pl.ds(TAIL + 64 * var + k, 29, stride=2)
                pack = place(pack, k - 2, top_ref[lines, :])
                pack = place(pack, k + 16, bot_ref[lines, :])
            out_ref[COEF + 32 * var : COEF + 32 * var + 29] = pack
            out_ref[COEF + 32 * var + 29 : COEF + 32 * var + 32] = jnp.zeros((3, 128), F32)


def call_halo_edges(top, bot, edge, *coef_edge):
    return pl.pallas_call(
        halo_edges,
        in_specs=whole(3 + len(coef_edge)),
        out_specs=whole(1)[0],
        out_shape=arrays((COEF + 128 * len(coef_edge), 128))[0],
        compiler_params=params(),
        name="halo_edges",
    )(top, bot, edge, *coef_edge)


def outer_first(top_ref, low_ref, high_ref, bot_ref, coef_ref, ctop_ref, cbot_ref,
                y_low_ref, y_high_ref, shift_ref):
    parts = ((-4, 0, top_ref), (0, 4, low_ref), (12, 16, high_ref), (16, 20, bot_ref))

    def one(var, half):
        def weight(k, row):
            if row < 0:
                return tail_line(ctop_ref, var, k, row + 2)
            if row < 16:
                return line_of(coef_ref, var, k, row)
            return tail_line(cbot_ref, var, k, row - 16)

        def finish(row, total):
            for w in range(4):
                total = total + weight(25 + w, row) * pick(parts, row, w, half)
            value = pick(parts, row, var, half) + 0.5 * total
            if row < 2:
                put(y_low_ref, row + 2, var, half, value)
            else:
                put(y_high_ref, row - 14, var, half, value)

        for first in (-2, 14):
            sweep(first, first + 4, lambda s: pick(parts, s, var, half), weight, finish, shift_ref)

    each_part(one)


def call_outer_first(top, low, high, bot, coef, ctop, cbot):
    return pl.pallas_call(
        outer_first,
        in_specs=whole(7),
        out_specs=whole(2),
        out_shape=arrays((4 * ROWS, 128), (4 * ROWS, 128)),
        scratch_shapes=[pltpu.VMEM((4, 8, 32, 128), F32)],
        compiler_params=params(),
        cost_estimate=cost(8),
        name="outer_first",
    )(top, low, high, bot, coef, ctop, cbot)


def strips(left_ref, right_ref, own_ref, coef_left_ref, coef_right_ref, coef_own_ref,
           mend_y_ref, mend_u_ref, rim_ref):
    entry = lanes((64, 128)) % 4
    entry_line = lanes((32, 128)) % 4

    def merge(entry, left, right):
        return jnp.where(entry < 2, pltpu.roll(right, 126, axis=1), pltpu.roll(left, 2, axis=1))

    def rows_on(pack, i):
        turn = (4 * (2 - i)) % 128
        return pltpu.roll(pack, turn, axis=1) if turn else pack

    def pack_at(ref, kind, var):
        return ref[pl.ds(pl.multiple_of(kind * ROWS + var * 64, 64), 64), :]

    @pl.loop(0, 4)
    def _(var):
        rim_ref[var] = merge(entry, pack_at(left_ref, 0, var), pack_at(right_ref, 0, var))

    @pl.loop(0, 4)
    def _(var):
        near = pack_at(own_ref, 0, var)
        rim = rim_ref[var]
        outer = merge(entry, pack_at(left_ref, 1, var), pack_at(right_ref, 1, var))
        lines = pl.ds(pl.multiple_of(COEF + var * 32, 32), 32)
        own = coef_own_ref[lines, :]
        other = merge(entry_line, coef_left_ref[lines, :], coef_right_ref[lines, :])

        def beyond(rim):
            crossed = jnp.where(entry == 1, pltpu.roll(rim, 1, axis=1), pltpu.roll(rim, 127, axis=1))
            total = jnp.zeros((64, 128), F32)
            for i in range(5):
                two = jnp.where(entry_line[0:1] < 2, own[5 * i + 4 : 5 * i + 5], own[5 * i : 5 * i + 1])
                one = jnp.where(entry_line[0:1] == 1, own[5 * i + 3 : 5 * i + 4], 0.0)
                one = jnp.where(entry_line[0:1] == 2, own[5 * i + 1 : 5 * i + 2], one)
                total = total + two * rows_on(rim, i) + one * rows_on(crossed, i)
            return total

        before = jnp.where(
            entry == 0, pltpu.roll(near, 127, axis=1),
            jnp.where(entry == 2, pltpu.roll(outer, 127, axis=1), pltpu.roll(rim, 1, axis=1)),
        )
        after = jnp.where(
            entry == 1, pltpu.roll(outer, 1, axis=1),
            jnp.where(entry == 3, pltpu.roll(near, 1, axis=1), pltpu.roll(rim, 127, axis=1)),
        )
        shifted = (
            jnp.where(entry < 2, near, outer), before, rim, after, jnp.where(entry < 2, outer, near),
        )
        total = jnp.zeros((64, 128), F32)
        for i in range(5):
            for j in range(5):
                k = 5 * i + j
                total = total + other[k : k + 1] * rows_on(shifted[j], i)
        for w in range(4):
            total = total + other[25 + w : 26 + w] * rim_ref[w]
        mend_y_ref[var] = 0.5 * beyond(rim)
        mend_u_ref[var] = beyond(rim + 0.5 * total)


def call_strips(left, right, own, coef_left, coef_right, coef_own):
    return pl.pallas_call(
        strips,
        in_specs=whole(6),
        out_specs=whole(2),
        out_shape=arrays((4, 64, 128), (4, 64, 128)),
        scratch_shapes=[pltpu.VMEM((4, 64, 128), F32)],
        compiler_params=params(),
        name="strips",
    )(left, right, own, coef_left, coef_right, coef_own)


def second(ranges, n_y, *refs):
    y_refs, refs = refs[:n_y], refs[n_y:]
    mend_y_ref, mend_u_ref, coef_ref = refs[:3]
    u_refs, refs = refs[3 : 3 + len(ranges)], refs[3 + len(ranges) :]
    out_refs, refs = refs[: len(ranges)], refs[len(ranges) :]
    y_ref, shift_ref = refs
    bounds = {1: ((2, 14),), 3: ((-2, 2), (2, 14), (14, 18))}[n_y]
    y_parts = [(first, stop, ref) for (first, stop), ref in zip(bounds, y_refs)]
    sources = sorted({s for first, stop in ranges for s in range(first - 2, stop + 2)})
    whole_y = ((-2, 18, y_ref),)

    def mend(var, half):
        pack = mend_y_ref[var, pl.ds(pl.multiple_of(half * 32, 32), 32)]
        for row in sources:
            put(y_ref, row + 2, var, half, pick(y_parts, row, var, half) + unplace(pack, row))

    each_part(mend)

    def one(var, half):
        pack = mend_u_ref[var, pl.ds(pl.multiple_of(half * 32, 32), 32)]
        for (first, stop), u_ref, out_ref in zip(ranges, u_refs, out_refs):

            def finish(row, total):
                for w in range(4):
                    total = total + line_of(coef_ref, var, 25 + w, row) * pick(whole_y, row, w, half)
                total = total + unplace(pack, row)
                put(out_ref, row - first, var, half, window(u_ref, row - first, var, half) + total)

            sweep(
                first, stop, lambda s: pick(whole_y, s, var, half),
                lambda k, row: line_of(coef_ref, var, k, row), finish, shift_ref,
            )

    each_part(one)


def call_second(ranges, ys, mend_y, mend_u, coef, us):
    outs = [((stop - first) * ROWS, 128) for first, stop in ranges]
    return pl.pallas_call(
        functools.partial(second, ranges, len(ys)),
        in_specs=whole(len(ys) + 3 + len(us)),
        out_specs=whole(len(us)),
        out_shape=arrays(*outs),
        scratch_shapes=[pltpu.VMEM((20 * ROWS, 128), F32), pltpu.VMEM((4, 12, 32, 128), F32)],
        compiler_params=params(),
        cost_estimate=cost(8),
        name="second",
    )(*ys, mend_y, mend_u, coef, *us)


def spread(cells_ref, weights_ref, high_ref, low_ref):
    step = pl.program_id(0)
    cell = lax.broadcasted_iota(jnp.int32, (256, 1024), 0) + step * 256
    hit = jnp.where(cells_ref[...] == cell, 1.0, 0.0).astype(BF16)
    total = jnp.dot(hit, weights_ref[...], preferred_element_type=F32)
    high = total.astype(BF16)
    high_ref[...] = high
    low_ref[...] = (total - high.astype(F32)).astype(BF16)


def call_spread(cells, weights):
    return pl.pallas_call(
        spread,
        grid=(8,),
        in_specs=[spec((1, 1024), lambda s: (0, 0)), spec((1024, 512), lambda s: (0, 0))],
        out_specs=[spec((256, 512), lambda s: (s, 0))] * 2,
        out_shape=[jax.ShapeDtypeStruct((2048, 512), BF16)] * 2,
        compiler_params=params(1),
        cost_estimate=pl.CostEstimate(flops=2 << 30, bytes_accessed=6 << 20, transcendentals=0),
        name="spread",
    )(cells, weights)


def leave(low_ref, mid_ref, high_ref, w_high_ref, w_low_ref, out_ref, markov_ref):
    parts = ((0, 4, low_ref), (4, 12, mid_ref), (12, 16, high_ref))
    sums = jnp.zeros((256, 512), F32)
    for k in range(8):
        rows = []
        for row in (2 * k, 2 * k + 1):
            for first, stop, ref in parts:
                if first <= row < stop:
                    rows.append(ref[(row - first) * ROWS : (row - first + 1) * ROWS])
            out_ref[row] = rows[-1].T
        u = jnp.concatenate(rows, axis=1)
        u_high = u.astype(BF16)
        u_low = (u - u_high.astype(F32)).astype(BF16)
        w_high = w_high_ref[256 * k : 256 * k + 256]
        w_low = w_low_ref[256 * k : 256 * k + 256]
        sums = sums + jnp.dot(u_high, w_high, preferred_element_type=F32)
        sums = sums + jnp.dot(u_low, w_high, preferred_element_type=F32)
        sums = sums + jnp.dot(u_high, w_low, preferred_element_type=F32)
    markov_ref[...] = sums.T


def call_leave(low, mid, high, w_high, w_low):
    return pl.pallas_call(
        leave,
        in_specs=whole(5),
        out_specs=whole(2),
        out_shape=arrays((16, 128, 256), (512, 256)),
        compiler_params=params(),
        cost_estimate=pl.CostEstimate(flops=2 << 30, bytes_accessed=8 << 20, transcendentals=0),
        name="leave",
    )(low, mid, high, w_high, w_low)


def shifts(n_azim, n_rad, da, dr):
    pairs = []
    for a in range(n_azim):
        for r in range(n_rad):
            if 0 <= r + dr < n_rad:
                pairs.append((a * n_rad + r, ((a + da) % n_azim) * n_rad + r + dr))
    return pairs


def body(perturbation_in, coefficients, wall_cells, wall_count, mode_row, mode_table):
    n_azim, n_rad = lax.axis_size("azim"), lax.axis_size("rad")

    def send(block, da, dr):
        return lax.ppermute(block, ("azim", "rad"), shifts(n_azim, n_rad, da, dr))

    slots = wall_cells.shape[0]
    live = jnp.arange(slots, dtype=jnp.int32) < wall_count[0]
    weights = jnp.where(live[:, None], jnp.take(mode_table, mode_row, axis=0), jnp.zeros((), BF16))
    w_high, w_low = call_spread(wall_cells.reshape(1, slots), weights)

    low, mid, high = call_enter(perturbation_in, coefficients)
    tails = edge_coef = None
    for step in range(STEPS):
        top, bot = send(high, 1, 0), send(low, -1, 0)
        y_mid, edge = call_inner_first(low, mid, high, coefficients)
        if step == 0:
            tails = top, bot
            extra = (call_coef_edges(coefficients),)
            edge, w_high = lax.optimization_barrier((edge, w_high))
        else:
            extra = ()
        own = call_halo_edges(top, bot, edge, *extra)
        left, right = send(own, 0, 1), send(own, 0, -1)
        if step == 0:
            edge_coef = left, right, own
        y_low, y_high = call_outer_first(top, low, high, bot, coefficients, *tails)
        mends = call_strips(left, right, own, *edge_coef)
        new_low, new_high = call_second(
            ((0, 4), (12, 16)), (y_low, y_mid, y_high), *mends, coefficients, (low, high)
        )
        (mid,) = call_second(((4, 12),), (y_mid,), *mends, coefficients, (mid,))
        low, high = new_low, new_high
    out, term = call_leave(low, mid, high, w_high, w_low)
    count = n_azim * n_rad
    parts = lax.all_to_all(term.reshape(count, -1, term.shape[1]), ("azim", "rad"), 0, 0)
    return out, jnp.sum(parts, axis=0)


def solution(mesh):
    return jax.shard_map(
        body,
        mesh=mesh,
        in_specs=(
            P("azim", "rad", None),
            P(None, None, "azim", "rad"),
            P(("azim", "rad")),
            P(("azim", "rad")),
            P(("azim", "rad")),
            P(),
        ),
        out_specs=(P("azim", "rad", None), P(("azim", "rad"), None)),
        check_vma=False,
    )
```

```python
import functools

import jax
import jax.numpy as jnp
from jax import lax
from jax.experimental import pallas as pl
from jax.experimental.pallas import tpu as pltpu
from jax.sharding import PartitionSpec as P

STEPS = 2
VMEM_LIMIT = 32 * 1024 * 1024
ENTER_LIMIT = 58 * 1024 * 1024
F32 = jnp.float32
BF16 = jnp.bfloat16


def spec(block, index):
    return pl.BlockSpec(block, index)


def whole(n):
    return [pl.BlockSpec(memory_space=pltpu.VMEM)] * n


def params(n=0):
    order = ("arbitrary",) * n if n else None
    return pltpu.CompilerParams(vmem_limit_bytes=VMEM_LIMIT, dimension_semantics=order)


def cost(rows):
    return pl.CostEstimate(flops=2 * 29 * rows * 128 * 256, bytes_accessed=rows << 18, transcendentals=0)


def arrays(*shapes):
    return [jax.ShapeDtypeStruct(shape, F32) for shape in shapes]


def lanes(shape):
    return lax.broadcasted_iota(jnp.int32, shape, len(shape) - 1)


ROWS = 256
TAIL = 4 * ROWS
COEF = 2 * ROWS


def window(ref, row, var, half):
    start = pl.multiple_of(row * ROWS + var * 64 + half * 32, 32)
    return ref[pl.ds(start, 32), :]


def put(ref, row, var, half, value):
    start = pl.multiple_of(row * ROWS + var * 64 + half * 32, 32)
    ref[pl.ds(start, 32), :] = value


def pick(parts, row, var, half):
    for first, stop, ref in parts:
        if first <= row < stop:
            return window(ref, row - first, var, half)
    raise IndexError(row)


def place(pack, row, value):
    lane = lanes(value.shape)
    base = 4 * (row + 4)
    here = (lane >= base) & (lane < base + 4)
    return jnp.where(here, pltpu.roll(value, (base + 2) % 128, axis=1), pack)


def place_far(pack, row, value):
    lane = lanes(value.shape)
    base = 4 * (row + 4)
    pack = jnp.where((lane >= base) & (lane < base + 2), pltpu.roll(value, (base + 4) % 128, axis=1), pack)
    return jnp.where((lane >= base + 2) & (lane < base + 4), pltpu.roll(value, base, axis=1), pack)


def unplace(pack, row):
    lane = lanes(pack.shape)
    base = 4 * (row + 4)
    turned = pltpu.roll(pack, (126 - base) % 128, axis=1)
    return jnp.where((lane < 2) | (lane >= 126), turned, 0.0)


def each_part(body):
    @pl.loop(0, 8)
    def _(step):
        body(step // 2, step % 2)


def sweep(first, stop, source, weight, finish, shift_ref, block=4):
    for s in range(first - 2, stop + 2):
        u = source(s)
        k = s - first + 2
        shift_ref[0, k] = pltpu.roll(u, 2, axis=1)
        shift_ref[1, k] = pltpu.roll(u, 1, axis=1)
        shift_ref[2, k] = pltpu.roll(u, 127, axis=1)
        shift_ref[3, k] = pltpu.roll(u, 126, axis=1)
    for begin in range(first, stop, block):
        totals = [None] * block
        for s in range(begin - 2, begin + block + 2):
            k = s - first + 2
            for j in range(5):
                x = source(s) if j == 2 else shift_ref[j - (j > 2), k]
                for b in range(block):
                    i = s + 2 - begin - b
                    if 0 <= i < 5:
                        term = weight(5 * i + j, begin + b) * x
                        totals[b] = term if totals[b] is None else totals[b] + term
        for b in range(block):
            finish(begin + b, totals[b])


def inside(lane, k, line):
    if k >= 25 or k % 5 == 2:
        return line
    keep = (lane >= 2, lane >= 1, None, lane < 127, lane < 126)[k % 5]
    return jnp.where(keep, line, 0.0)


def line_of(coef_ref, var, k, row):
    return jnp.broadcast_to(coef_ref[var, k, row : row + 1], (32, 128))


def tail_line(ref, var, k, row):
    lines = ref.at[pl.ds(pl.multiple_of(TAIL + var * 64, 64), 64)]
    line = inside(lanes((1, 128)), k, lines[2 * k + row : 2 * k + row + 1])
    return jnp.broadcast_to(line, (32, 128))


def sort_sides(index, even_ref, odd_ref, below_ref, above_ref):
    even_is_above = index % 2 == 0

    @pl.when(even_is_above)
    def _():
        odd_ref[...], even_ref[...] = below_ref[...], above_ref[...]

    @pl.when(jnp.logical_not(even_is_above))
    def _():
        even_ref[...], odd_ref[...] = below_ref[...], above_ref[...]


def enter_outer(x_ref, coef_ref, low_ref, high_ref, even_ref, odd_ref, x_in, coef_in, sems):
    copies = [
        pltpu.make_async_copy(x_ref.at[pl.ds(0, 4)], x_in.at[0], sems.at[0]),
        pltpu.make_async_copy(x_ref.at[pl.ds(12, 4)], x_in.at[1], sems.at[1]),
        pltpu.make_async_copy(coef_ref, coef_in, sems.at[2]),
    ]
    for copy in copies:
        copy.start()
    low_ref[TAIL:] = jnp.zeros((256, 128), F32)
    high_ref[TAIL:] = jnp.zeros((256, 128), F32)
    for side, ref in ((0, low_ref), (1, high_ref)):
        copies[side].wait()

        @pl.loop(0, 4)
        def _(k):
            ref[pl.ds(pl.multiple_of(k * ROWS, ROWS), ROWS)] = x_in[side, k].T

    copies[2].wait()

    @pl.loop(0, 4)
    def _(k):
        lines = pl.ds(pl.multiple_of(TAIL + k * 64, 64), 58)
        low_ref[lines] = coef_in[k, :, 0:2].reshape(58, 128)
        high_ref[lines] = coef_in[k, :, 14:16].reshape(58, 128)

    sort_sides(lax.axis_index("azim"), even_ref, odd_ref, low_ref, high_ref)


def call_enter_outer(x, coef):
    return pl.pallas_call(
        enter_outer,
        in_specs=[pl.BlockSpec(memory_space=pltpu.HBM)] * 2,
        out_specs=whole(4),
        out_shape=arrays(*[(TAIL + 256, 128)] * 4),
        scratch_shapes=[
            pltpu.VMEM((2, 4, 128, 256), F32),
            pltpu.VMEM((4, 29, 16, 128), F32),
            pltpu.SemaphoreType.DMA((3,)),
        ],
        compiler_params=pltpu.CompilerParams(vmem_limit_bytes=ENTER_LIMIT),
        name="enter_outer",
    )(x, coef)


def enter_inner(x_ref, mid_ref, x_in, sem):
    copy = pltpu.make_async_copy(x_ref.at[pl.ds(4, 8)], x_in, sem)
    copy.start()
    copy.wait()

    @pl.loop(0, 8)
    def _(k):
        mid_ref[pl.ds(pl.multiple_of(k * ROWS, ROWS), ROWS)] = x_in[k].T


def call_enter_inner(x):
    return pl.pallas_call(
        enter_inner,
        in_specs=[pl.BlockSpec(memory_space=pltpu.HBM)],
        out_specs=whole(1)[0],
        out_shape=arrays((8 * ROWS, 128))[0],
        scratch_shapes=[pltpu.VMEM((8, 128, 256), F32), pltpu.SemaphoreType.DMA],
        compiler_params=params(),
        name="enter_inner",
    )(x)


def inner_first(low_ref, mid_ref, high_ref, coef_ref, y_ref, edge_ref, shift_ref):
    parts = ((0, 4, low_ref), (4, 12, mid_ref), (12, 16, high_ref))

    def one(var, half):
        def finish(row, total):
            for w in range(4):
                total = total + line_of(coef_ref, var, 25 + w, row) * pick(parts, row, w, half)
            put(y_ref, row - 2, var, half, pick(parts, row, var, half) + 0.5 * total)

        sweep(
            2, 14, lambda s: pick(parts, s, var, half),
            lambda k, row: line_of(coef_ref, var, k, row), finish, shift_ref,
        )
        near = jnp.zeros((32, 128), F32)
        far = jnp.zeros((32, 128), F32)
        for row in range(16):
            value = pick(parts, row, var, half)
            near, far = place(near, row, value), place_far(far, row, value)
        put(edge_ref, 0, var, half, near)
        put(edge_ref, 1, var, half, far)

    each_part(one)


def call_inner_first(low, mid, high, coef):
    return pl.pallas_call(
        inner_first,
        in_specs=whole(4),
        out_specs=whole(2),
        out_shape=arrays((12 * ROWS, 128), (2 * ROWS, 128)),
        scratch_shapes=[pltpu.VMEM((4, 16, 32, 128), F32)],
        compiler_params=params(),
        cost_estimate=cost(12),
        name="inner_first",
    )(low, mid, high, coef)


def coef_edges(coef_ref, out_ref, inside_ref):
    lane = lanes((16, 128))

    @pl.loop(0, 4)
    def _(var):
        for k in range(29):
            lines = pl.ds(pl.multiple_of(var * 464 + k * 16, 16), 16)
            inside_ref[var, k] = inside(lane, k, coef_ref[lines, :])

    out_ref[...] = jnp.zeros_like(out_ref)
    for var in range(4):
        pack = jnp.zeros((29, 128), F32)
        for row in range(16):
            pack = place(pack, row, coef_ref[pl.ds(var * 464 + row, 29, stride=16), :])
        out_ref[32 * var : 32 * var + 29] = pack


def call_coef_edges(coef):
    return pl.pallas_call(
        coef_edges,
        in_specs=whole(1),
        out_specs=whole(2),
        out_shape=arrays((128, 128), coef.shape),
        compiler_params=params(),
        name="coef_edges",
    )(coef.reshape(-1, 128))


def halo_edges(even_ref, odd_ref, edge_ref, *refs):
    top_ref, bot_ref, out_ref = refs[-3:]
    even_is_above = lax.axis_index("azim") % 2 == 0

    @pl.when(even_is_above)
    def _():
        top_ref[...], bot_ref[...] = odd_ref[...], even_ref[...]

    @pl.when(jnp.logical_not(even_is_above))
    def _():
        top_ref[...], bot_ref[...] = even_ref[...], odd_ref[...]

    def one(var, half):
        near = window(edge_ref, 0, var, half)
        far = window(edge_ref, 1, var, half)
        for k in range(4):
            for row, ref in ((k - 4, top_ref), (k + 16, bot_ref)):
                value = window(ref, k, var, half)
                near, far = place(near, row, value), place_far(far, row, value)
        put(out_ref, 0, var, half, near)
        put(out_ref, 1, var, half, far)

    each_part(one)
    if len(refs) == 4:
        for var in range(4):
            pack = refs[0][32 * var : 32 * var + 29]
            for k in range(2):
                lines = pl.ds(TAIL + 64 * var + k, 29, stride=2)
                pack = place(pack, k - 2, top_ref[lines, :])
                pack = place(pack, k + 16, bot_ref[lines, :])
            out_ref[COEF + 32 * var : COEF + 32 * var + 29] = pack
            out_ref[COEF + 32 * var + 29 : COEF + 32 * var + 32] = jnp.zeros((3, 128), F32)


def call_halo_edges(even, odd, edge, *coef_edge):
    return pl.pallas_call(
        halo_edges,
        in_specs=whole(3 + len(coef_edge)),
        out_specs=whole(3),
        out_shape=arrays(even.shape, odd.shape, (COEF + 128 * len(coef_edge), 128)),
        compiler_params=params(),
        name="halo_edges",
    )(even, odd, edge, *coef_edge)


def outer_first(top_ref, low_ref, high_ref, bot_ref, coef_ref, ctop_ref, cbot_ref,
                y_low_ref, y_high_ref, shift_ref):
    parts = ((-4, 0, top_ref), (0, 4, low_ref), (12, 16, high_ref), (16, 20, bot_ref))

    def one(var, half):
        def weight(k, row):
            if row < 0:
                return tail_line(ctop_ref, var, k, row + 2)
            if row < 16:
                return line_of(coef_ref, var, k, row)
            return tail_line(cbot_ref, var, k, row - 16)

        def finish(row, total):
            for w in range(4):
                total = total + weight(25 + w, row) * pick(parts, row, w, half)
            value = pick(parts, row, var, half) + 0.5 * total
            if row < 2:
                put(y_low_ref, row + 2, var, half, value)
            else:
                put(y_high_ref, row - 14, var, half, value)

        for first in (-2, 14):
            sweep(first, first + 4, lambda s: pick(parts, s, var, half), weight, finish, shift_ref)

    each_part(one)


def call_outer_first(top, low, high, bot, coef, ctop, cbot):
    return pl.pallas_call(
        outer_first,
        in_specs=whole(7),
        out_specs=whole(2),
        out_shape=arrays((4 * ROWS, 128), (4 * ROWS, 128)),
        scratch_shapes=[pltpu.VMEM((4, 8, 32, 128), F32)],
        compiler_params=params(),
        cost_estimate=cost(8),
        name="outer_first",
    )(top, low, high, bot, coef, ctop, cbot)


def strips(even_ref, odd_ref, own_ref, coef_even_ref, coef_odd_ref, coef_own_ref,
           mend_y_ref, mend_u_ref, rim_ref, line_ref):
    entry = lanes((32, 128)) % 4
    entry_line = lanes((1, 128)) % 4
    even_is_right = lanes((32, 128)) * 0 + lax.axis_index("rad") % 2 == 0

    def merge(even, odd):
        right = jnp.where(even_is_right, even, odd)
        left = jnp.where(even_is_right, odd, even)
        return jnp.where(entry < 2, pltpu.roll(right, 126, axis=1), pltpu.roll(left, 2, axis=1))

    def rows_on(pack, i):
        turn = (4 * (2 - i)) % 128
        return pltpu.roll(pack, turn, axis=1) if turn else pack

    def rim_of(var, half):
        at = pl.ds(pl.multiple_of(half * 32, 32), 32)
        rim_ref[var, at] = merge(window(even_ref, 0, var, half), window(odd_ref, 0, var, half))

    each_part(rim_of)

    @pl.loop(0, 4)
    def _(var):
        lines = pl.ds(pl.multiple_of(COEF + var * 32, 32), 32)
        own = coef_own_ref.at[lines]
        line_ref[var, 0:32] = merge(coef_even_ref[lines, :], coef_odd_ref[lines, :])
        for i in range(5):
            k = 5 * i
            two = jnp.where(entry_line < 2, own[k + 4 : k + 5], own[k : k + 1])
            one = jnp.where(entry_line == 1, own[k + 3 : k + 4], 0.0)
            one = jnp.where(entry_line == 2, own[k + 1 : k + 2], one)
            line_ref[var, 32 + i : 33 + i] = two
            line_ref[var, 37 + i : 38 + i] = one

    def one_part(var, half):
        at = pl.ds(pl.multiple_of(half * 32, 32), 32)

        def line(k):
            return jnp.broadcast_to(line_ref[var, k : k + 1], (32, 128))

        def beyond(rim):
            crossed = jnp.where(entry == 1, pltpu.roll(rim, 1, axis=1), pltpu.roll(rim, 127, axis=1))
            total = line(32) * rows_on(rim, 0) + line(37) * rows_on(crossed, 0)
            for i in range(1, 5):
                total = total + line(32 + i) * rows_on(rim, i) + line(37 + i) * rows_on(crossed, i)
            return total

        near = window(own_ref, 0, var, half)
        rim = rim_ref[var, at]
        outer = merge(window(even_ref, 1, var, half), window(odd_ref, 1, var, half))
        before = jnp.where(
            entry == 0, pltpu.roll(near, 127, axis=1),
            jnp.where(entry == 2, pltpu.roll(outer, 127, axis=1), pltpu.roll(rim, 1, axis=1)),
        )
        after = jnp.where(
            entry == 1, pltpu.roll(outer, 1, axis=1),
            jnp.where(entry == 3, pltpu.roll(near, 1, axis=1), pltpu.roll(rim, 127, axis=1)),
        )
        shifted = (
            jnp.where(entry < 2, near, outer), before, rim, after, jnp.where(entry < 2, outer, near),
        )
        total = line(25) * rim_ref[0, at]
        for w in range(1, 4):
            total = total + line(25 + w) * rim_ref[w, at]
        for j in range(5):
            for i in range(5):
                total = total + line(5 * i + j) * rows_on(shifted[j], i)
        mend_y_ref[var, at] = 0.5 * beyond(rim)
        mend_u_ref[var, at] = beyond(rim + 0.5 * total)

    each_part(one_part)


def call_strips(even, odd, own, coef_even, coef_odd, coef_own):
    return pl.pallas_call(
        strips,
        in_specs=whole(6),
        out_specs=whole(2),
        out_shape=arrays((4, 64, 128), (4, 64, 128)),
        scratch_shapes=[pltpu.VMEM((4, 64, 128), F32), pltpu.VMEM((4, 48, 128), F32)],
        compiler_params=params(),
        name="strips",
    )(even, odd, own, coef_even, coef_odd, coef_own)


PARTS = ((0, 4), (4, 12), (12, 16))


def second(ranges, parts, n_y, sides, *refs):
    y_refs, refs = refs[:n_y], refs[n_y:]
    mend_y_ref, mend_u_ref, coef_ref = refs[:3]
    u_refs, refs = refs[3 : 3 + len(parts)], refs[3 + len(parts) :]
    out_refs, refs = refs[: len(parts)], refs[len(parts) :]
    y_ref, shift_ref = refs[-2:]
    bounds = {1: ((2, 14),), 3: ((-2, 2), (2, 14), (14, 18))}[n_y]
    y_parts = [(first, stop, ref) for (first, stop), ref in zip(bounds, y_refs)]
    u_parts = [(first, stop, ref) for (first, stop), ref in zip(parts, u_refs)]
    sources = sorted({s for first, stop in ranges for s in range(first - 2, stop + 2)})
    whole_y = ((-2, 18, y_ref),)

    def mend(var, half):
        pack = mend_y_ref[var, pl.ds(pl.multiple_of(half * 32, 32), 32)]
        for row in sources:
            put(y_ref, row + 2, var, half, pick(y_parts, row, var, half) + unplace(pack, row))

    each_part(mend)

    def one(var, half):
        pack = mend_u_ref[var, pl.ds(pl.multiple_of(half * 32, 32), 32)]

        def finish(row, total):
            for w in range(4):
                total = total + line_of(coef_ref, var, 25 + w, row) * pick(whole_y, row, w, half)
            total = total + unplace(pack, row)
            for (first, stop), ref in zip(parts, out_refs):
                if first <= row < stop:
                    put(ref, row - first, var, half, pick(u_parts, row, var, half) + total)

        for first, stop in ranges:
            sweep(
                first, stop, lambda s: pick(whole_y, s, var, half),
                lambda k, row: line_of(coef_ref, var, k, row), finish, shift_ref,
            )

    each_part(one)
    if sides:
        sort_sides(lax.axis_index("azim"), refs[0], refs[1], out_refs[0], out_refs[-1])


def call_second(ranges, parts, ys, mend_y, mend_u, coef, us, sides=False):
    outs = [((stop - first) * ROWS, 128) for first, stop in parts]
    outs += [outs[0]] * (2 * sides)
    most = max(stop - first for first, stop in ranges)
    return pl.pallas_call(
        functools.partial(second, ranges, parts, len(ys), sides),
        in_specs=whole(len(ys) + 3 + len(us)),
        out_specs=whole(len(outs)),
        out_shape=arrays(*outs),
        scratch_shapes=[pltpu.VMEM((20 * ROWS, 128), F32), pltpu.VMEM((4, most + 4, 32, 128), F32)],
        compiler_params=params(),
        cost_estimate=cost(8),
        name="second",
    )(*ys, mend_y, mend_u, coef, *us)


def gather(rows_ref, table_ref, out_ref, wide_ref, picked_ref):
    @pl.loop(0, 16)
    def _(k):
        at = pl.ds(pl.multiple_of(k * 256, 256), 256)
        wide_ref[at] = table_ref[at].astype(F32)

    @pl.loop(0, 32)
    def _(k):
        for t in range(32):
            slot = k * 32 + t
            picked_ref[pl.ds(slot, 1)] = wide_ref[pl.ds(rows_ref[slot], 1)]

    @pl.loop(0, 4)
    def _(k):
        at = pl.ds(pl.multiple_of(k * 256, 256), 256)
        out_ref[at] = picked_ref[at].astype(BF16)


def call_gather(rows, table):
    return pl.pallas_call(
        gather,
        in_specs=[pl.BlockSpec(memory_space=pltpu.SMEM)] + whole(1),
        out_specs=whole(1)[0],
        out_shape=jax.ShapeDtypeStruct((rows.shape[0], table.shape[1]), BF16),
        scratch_shapes=[pltpu.VMEM((4096, 512), F32), pltpu.VMEM((1024, 512), F32)],
        compiler_params=params(),
        name="gather",
    )(rows, table)


def spread(count_ref, cells_ref, weights_ref, high_ref, low_ref):
    step = pl.program_id(0)
    cell = lax.broadcasted_iota(jnp.int32, (256, 1024), 0) + step * 256
    live = lax.broadcasted_iota(jnp.int32, (1, 1024), 1) < count_ref[0]
    cells = jnp.where(live, cells_ref[...], -1)
    hit = jnp.where(cells == cell, 1.0, 0.0).astype(BF16)
    total = jnp.dot(hit, weights_ref[...], preferred_element_type=F32)
    high = total.astype(BF16)
    high_ref[...] = high
    low_ref[...] = (total - high.astype(F32)).astype(BF16)


def call_spread(count, cells, weights):
    return pl.pallas_call(
        spread,
        grid=(8,),
        in_specs=[pl.BlockSpec(memory_space=pltpu.SMEM)]
        + [spec((1, 1024), lambda s: (0, 0)), spec((1024, 512), lambda s: (0, 0))],
        out_specs=[spec((256, 512), lambda s: (s, 0))] * 2,
        out_shape=[jax.ShapeDtypeStruct((2048, 512), BF16)] * 2,
        compiler_params=params(1),
        cost_estimate=pl.CostEstimate(flops=2 << 30, bytes_accessed=6 << 20, transcendentals=0),
        name="spread",
    )(count, cells, weights)


def leave(low_ref, mid_ref, high_ref, w_high_ref, w_low_ref, out_ref, markov_ref):
    parts = ((0, 4, low_ref), (4, 12, mid_ref), (12, 16, high_ref))
    sums = jnp.zeros((256, 512), F32)
    for k in range(8):
        rows = []
        for row in (2 * k, 2 * k + 1):
            for first, stop, ref in parts:
                if first <= row < stop:
                    rows.append(ref[(row - first) * ROWS : (row - first + 1) * ROWS])
            out_ref[row] = rows[-1].T
        u = jnp.concatenate(rows, axis=1)
        u_high = u.astype(BF16)
        u_low = (u - u_high.astype(F32)).astype(BF16)
        w_high = w_high_ref[256 * k : 256 * k + 256]
        w_low = w_low_ref[256 * k : 256 * k + 256]
        sums = sums + jnp.dot(u_high, w_high, preferred_element_type=F32)
        sums = sums + jnp.dot(u_low, w_high, preferred_element_type=F32)
        sums = sums + jnp.dot(u_high, w_low, preferred_element_type=F32)
    markov_ref[...] = sums.T


def call_leave(low, mid, high, w_high, w_low):
    return pl.pallas_call(
        leave,
        in_specs=whole(5),
        out_specs=whole(2),
        out_shape=arrays((16, 128, 256), (512, 256)),
        compiler_params=params(),
        cost_estimate=pl.CostEstimate(flops=2 << 30, bytes_accessed=8 << 20, transcendentals=0),
        name="leave",
    )(low, mid, high, w_high, w_low)


def swaps(count, first, periodic):
    pairs = [(k, (k + 1) % count) for k in range(first, count, 2) if periodic or k + 1 < count]
    return pairs + [(target, source) for source, target in pairs]


def body(perturbation_in, coefficients, wall_cells, wall_count, mode_row, mode_table):
    n_azim, n_rad = lax.axis_size("azim"), lax.axis_size("rad")

    def swap(block, axis, odd):
        count = lax.axis_size(axis)
        return lax.ppermute(block, axis, swaps(count, odd, axis == "azim"))

    slots = wall_cells.shape[0]
    weights = call_gather(mode_row, mode_table)
    w_high, w_low = call_spread(wall_count, wall_cells.reshape(1, slots), weights)

    low, high, even, odd = call_enter_outer(perturbation_in, coefficients)
    mid = call_enter_inner(perturbation_in)
    coef_edge, coef = call_coef_edges(coefficients)
    for step in range(STEPS):
        even = swap(even, "azim", 0)
        odd = swap(odd, "azim", 1)
        y_mid, edge = call_inner_first(low, mid, high, coef)
        if step == 0:
            edge, w_high = lax.optimization_barrier((edge, w_high))
            top, bot, own = call_halo_edges(even, odd, edge, coef_edge)
            tails = top, bot
        else:
            top, bot, own = call_halo_edges(even, odd, edge)
        sides = swap(own, "rad", 0), swap(own, "rad", 1), own
        if step == 0:
            coef_sides = sides
        ys = call_outer_first(top, low, high, bot, coef, *tails)
        ys = ys[0], y_mid, ys[1]
        mends = call_strips(*sides, *coef_sides)
        if step < STEPS - 1:
            (new_mid,) = call_second(((4, 12),), PARTS[1:2], ys[1:2], *mends, coef, (mid,))
            low, high, even, odd = call_second(
                (PARTS[0], PARTS[2]), (PARTS[0], PARTS[2]), ys, *mends, coef, (low, high), sides=True
            )
            mid = new_mid
        else:
            low, mid, high = call_second(((0, 16),), PARTS, ys, *mends, coef, (low, mid, high))
    out, term = call_leave(low, mid, high, w_high, w_low)
    count = n_azim * n_rad
    parts = lax.all_to_all(term.reshape(count, -1, term.shape[1]), ("azim", "rad"), 0, 0)
    return out, jnp.sum(parts, axis=0)


def solution(mesh):
    return jax.shard_map(
        body,
        mesh=mesh,
        in_specs=(
            P("azim", "rad", None),
            P(None, None, "azim", "rad"),
            P(("azim", "rad")),
            P(("azim", "rad")),
            P(("azim", "rad")),
            P(),
        ),
        out_specs=(P("azim", "rad", None), P(("azim", "rad"), None)),
        check_vma=False,
    )
```

```python
import functools

import jax
import jax.numpy as jnp
from jax import lax
from jax.experimental import pallas as pl
from jax.experimental.pallas import tpu as pltpu
from jax.sharding import PartitionSpec as P

STEPS = 2
VMEM_LIMIT = 32 * 1024 * 1024
ENTER_LIMIT = 58 * 1024 * 1024
F32 = jnp.float32
BF16 = jnp.bfloat16


def spec(block, index):
    return pl.BlockSpec(block, index)


def whole(n):
    return [pl.BlockSpec(memory_space=pltpu.VMEM)] * n


def params(n=0):
    order = ("arbitrary",) * n if n else None
    return pltpu.CompilerParams(vmem_limit_bytes=VMEM_LIMIT, dimension_semantics=order)


def cost(rows):
    return pl.CostEstimate(flops=2 * 29 * rows * 128 * 256, bytes_accessed=rows << 18, transcendentals=0)


def arrays(*shapes):
    return [jax.ShapeDtypeStruct(shape, F32) for shape in shapes]


def lanes(shape):
    return lax.broadcasted_iota(jnp.int32, shape, len(shape) - 1)


ROWS = 256
WIDTH = 32
UNROLL = 8
TAIL = 4 * ROWS
COEF = 2 * ROWS


def window(ref, row, var, half):
    start = pl.multiple_of(row * ROWS + var * 64 + half * WIDTH, 8)
    return ref[pl.ds(start, WIDTH), :]


def put(ref, row, var, half, value):
    start = pl.multiple_of(row * ROWS + var * 64 + half * WIDTH, 8)
    ref[pl.ds(start, WIDTH), :] = value


def pick(parts, row, var, half):
    for first, stop, ref in parts:
        if first <= row < stop:
            return window(ref, row - first, var, half)
    raise IndexError(row)


def place(pack, row, value, cell):
    lane = lanes(value.shape)
    base = 4 * (row + 4)
    here = (lane >= base) & (lane < base + 4)
    return jnp.where(here, pltpu.roll(value, (base - cell) % 128, axis=1), pack)


def unplace(pack, row):
    lane = lanes(pack.shape)
    base = 4 * (row + 4)
    turned = pltpu.roll(pack, (126 - base) % 128, axis=1)
    return jnp.where((lane < 2) | (lane >= 126), turned, 0.0)


def each_part(body):
    halves = 64 // WIDTH

    @pl.loop(0, 4 * halves, unroll=UNROLL)
    def _(step):
        body(step // halves, step % halves)


def sweep(first, stop, source, weight, finish):
    for row in range(first, stop):
        sums = [None] * 5
        for i in range(5):
            u = source(row + i - 2)
            for j in range(5):
                term = weight(5 * i + j, row) * u
                sums[j] = term if i == 0 else sums[j] + term
        total = sums[2]
        for j in (0, 1, 3, 4):
            total = total + pltpu.roll(sums[j], (2 - j) % 128, axis=1)
        finish(row, total)


def turned(k, line):
    if k >= 25 or k % 5 == 2:
        return line
    lane = lanes(line.shape)
    keep = (lane < 126, lane < 127, None, lane >= 1, lane >= 2)[k % 5]
    return jnp.where(keep, pltpu.roll(line, (k % 5 - 2) % 128, axis=1), 0.0)


def line_of(coef_ref, var, k, row):
    return jnp.broadcast_to(coef_ref[var, k, row : row + 1], (WIDTH, 128))


def tail_line(ref, var, k, row):
    lines = ref.at[pl.ds(pl.multiple_of(var * 64, 64), 64)]
    return jnp.broadcast_to(lines[2 * k + row : 2 * k + row + 1], (WIDTH, 128))


def sort_sides(index, even_ref, odd_ref, below_ref, above_ref):
    even_is_above = index % 2 == 0

    @pl.when(even_is_above)
    def _():
        odd_ref[...], even_ref[...] = below_ref[...], above_ref[...]

    @pl.when(jnp.logical_not(even_is_above))
    def _():
        even_ref[...], odd_ref[...] = below_ref[...], above_ref[...]


def enter_outer(x_ref, coef_ref, low_ref, high_ref, even_ref, odd_ref, x_in, coef_in, sems):
    copies = [
        pltpu.make_async_copy(x_ref.at[pl.ds(0, 4)], x_in.at[0], sems.at[0]),
        pltpu.make_async_copy(x_ref.at[pl.ds(12, 4)], x_in.at[1], sems.at[1]),
        pltpu.make_async_copy(coef_ref, coef_in, sems.at[2]),
    ]
    for copy in copies:
        copy.start()
    low_ref[TAIL:] = jnp.zeros((256, 128), F32)
    high_ref[TAIL:] = jnp.zeros((256, 128), F32)
    for side, ref in ((0, low_ref), (1, high_ref)):
        copies[side].wait()

        @pl.loop(0, 4)
        def _(k):
            ref[pl.ds(pl.multiple_of(k * ROWS, ROWS), ROWS)] = x_in[side, k].T

    copies[2].wait()

    @pl.loop(0, 4)
    def _(k):
        lines = pl.ds(pl.multiple_of(TAIL + k * 64, 64), 58)
        low_ref[lines] = coef_in[k, :, 0:2].reshape(58, 128)
        high_ref[lines] = coef_in[k, :, 14:16].reshape(58, 128)

    sort_sides(lax.axis_index("azim"), even_ref, odd_ref, low_ref, high_ref)


def call_enter_outer(x, coef):
    return pl.pallas_call(
        enter_outer,
        in_specs=[pl.BlockSpec(memory_space=pltpu.HBM)] * 2,
        out_specs=whole(4),
        out_shape=arrays(*[(TAIL + 256, 128)] * 4),
        scratch_shapes=[
            pltpu.VMEM((2, 4, 128, 256), F32),
            pltpu.VMEM((4, 29, 16, 128), F32),
            pltpu.SemaphoreType.DMA((3,)),
        ],
        compiler_params=pltpu.CompilerParams(vmem_limit_bytes=ENTER_LIMIT),
        name="enter_outer",
    )(x, coef)


def enter_inner(x_ref, mid_ref, x_in, sem):
    copy = pltpu.make_async_copy(x_ref.at[pl.ds(4, 8)], x_in, sem)
    copy.start()
    copy.wait()

    @pl.loop(0, 8)
    def _(k):
        mid_ref[pl.ds(pl.multiple_of(k * ROWS, ROWS), ROWS)] = x_in[k].T


def call_enter_inner(x):
    return pl.pallas_call(
        enter_inner,
        in_specs=[pl.BlockSpec(memory_space=pltpu.HBM)],
        out_specs=whole(1)[0],
        out_shape=arrays((8 * ROWS, 128))[0],
        scratch_shapes=[pltpu.VMEM((8, 128, 256), F32), pltpu.SemaphoreType.DMA],
        compiler_params=params(),
        name="enter_inner",
    )(x)


def inner_first(low_ref, mid_ref, high_ref, coef_ref, y_ref, edge_ref):
    parts = ((0, 4, low_ref), (4, 12, mid_ref), (12, 16, high_ref))

    def one(var, half):
        def finish(row, total):
            for w in range(4):
                total = total + line_of(coef_ref, var, 25 + w, row) * pick(parts, row, w, half)
            put(y_ref, row - 2, var, half, pick(parts, row, var, half) + 0.5 * total)

        sweep(
            2, 14, lambda s: pick(parts, s, var, half),
            lambda k, row: line_of(coef_ref, var, k, row), finish,
        )
        tail = jnp.zeros((WIDTH, 128), F32)
        head = jnp.zeros((WIDTH, 128), F32)
        for row in range(16):
            value = pick(parts, row, var, half)
            tail, head = place(tail, row, value, 124), place(head, row, value, 0)
        put(edge_ref, 0, var, half, tail)
        put(edge_ref, 1, var, half, head)

    each_part(one)


def call_inner_first(low, mid, high, coef):
    return pl.pallas_call(
        inner_first,
        in_specs=whole(4),
        out_specs=whole(2),
        out_shape=arrays((12 * ROWS, 128), (2 * ROWS, 128)),
        compiler_params=params(),
        cost_estimate=cost(12),
        name="inner_first",
    )(low, mid, high, coef)


def coef_edges(coef_ref, out_ref, turned_ref):
    @pl.loop(0, 4)
    def _(var):
        for k in range(29):
            lines = pl.ds(pl.multiple_of(var * 464 + k * 16, 16), 16)
            turned_ref[var, k] = turned(k, coef_ref[lines, :])

    out_ref[...] = jnp.zeros_like(out_ref)
    for var in range(4):
        pack = jnp.zeros((29, 128), F32)
        for row in range(16):
            pack = place(pack, row, coef_ref[pl.ds(var * 464 + row, 29, stride=16), :], 126)
        out_ref[32 * var : 32 * var + 29] = pack


def call_coef_edges(coef):
    return pl.pallas_call(
        coef_edges,
        in_specs=whole(1),
        out_specs=whole(2),
        out_shape=arrays((128, 128), coef.shape),
        compiler_params=params(),
        name="coef_edges",
    )(coef.reshape(-1, 128))


def halo_edges(even_ref, odd_ref, edge_ref, *refs):
    top_ref, bot_ref, out_ref = refs[len(refs) > 3 :][:3]
    even_is_above = lax.axis_index("azim") % 2 == 0

    @pl.when(even_is_above)
    def _():
        top_ref[...], bot_ref[...] = odd_ref[:TAIL], even_ref[:TAIL]

    @pl.when(jnp.logical_not(even_is_above))
    def _():
        top_ref[...], bot_ref[...] = even_ref[:TAIL], odd_ref[:TAIL]

    def one(var, half):
        tail = window(edge_ref, 0, var, half)
        head = window(edge_ref, 1, var, half)
        for k in range(4):
            for row, ref in ((k - 4, top_ref), (k + 16, bot_ref)):
                value = window(ref, k, var, half)
                tail, head = place(tail, row, value, 124), place(head, row, value, 0)
        put(out_ref, 0, var, half, tail)
        put(out_ref, 1, var, half, head)

    each_part(one)
    if len(refs) > 3:
        coef_edge_ref, (ctop_ref, cbot_ref) = refs[0], refs[4:]

        @pl.when(even_is_above)
        def _():
            ctop_ref[...], cbot_ref[...] = odd_ref[TAIL:], even_ref[TAIL:]

        @pl.when(jnp.logical_not(even_is_above))
        def _():
            ctop_ref[...], cbot_ref[...] = even_ref[TAIL:], odd_ref[TAIL:]

        number = lax.broadcasted_iota(jnp.int32, (64, 128), 0) // 2
        for var in range(4):
            pack = coef_edge_ref[32 * var : 32 * var + 29]
            for k in range(2):
                lines = pl.ds(64 * var + k, 29, stride=2)
                pack = place(pack, k - 2, ctop_ref[lines, :], 126)
                pack = place(pack, k + 16, cbot_ref[lines, :], 126)
            out_ref[COEF + 32 * var : COEF + 32 * var + 29] = pack
            out_ref[COEF + 32 * var + 29 : COEF + 32 * var + 32] = jnp.zeros((3, 128), F32)
        for var in range(4):
            at = slice(64 * var, 64 * var + 64)
            for ref in (ctop_ref, cbot_ref):
                lines = ref[at]
                result = lines
                for j in (0, 1, 3, 4):
                    here = (number % 5 == j) & (number < 25)
                    result = jnp.where(here, turned(j, lines), result)
                ref[at] = result


def call_halo_edges(even, odd, edge, *coef_edge):
    return pl.pallas_call(
        halo_edges,
        in_specs=whole(3 + len(coef_edge)),
        out_specs=whole(3 + 2 * len(coef_edge)),
        out_shape=arrays(
            (TAIL, 128), (TAIL, 128), (COEF + 128 * len(coef_edge), 128),
            *[(256, 128)] * (2 * len(coef_edge)),
        ),
        compiler_params=params(),
        name="halo_edges",
    )(even, odd, edge, *coef_edge)


def outer_first(top_ref, low_ref, high_ref, bot_ref, coef_ref, ctop_ref, cbot_ref,
                y_low_ref, y_high_ref):
    parts = ((-4, 0, top_ref), (0, 4, low_ref), (12, 16, high_ref), (16, 20, bot_ref))

    def one(var, half):
        def weight(k, row):
            if row < 0:
                return tail_line(ctop_ref, var, k, row + 2)
            if row < 16:
                return line_of(coef_ref, var, k, row)
            return tail_line(cbot_ref, var, k, row - 16)

        def finish(row, total):
            for w in range(4):
                total = total + weight(25 + w, row) * pick(parts, row, w, half)
            value = pick(parts, row, var, half) + 0.5 * total
            if row < 2:
                put(y_low_ref, row + 2, var, half, value)
            else:
                put(y_high_ref, row - 14, var, half, value)

        for first in (-2, 14):
            sweep(first, first + 4, lambda s: pick(parts, s, var, half), weight, finish)

    each_part(one)


def call_outer_first(top, low, high, bot, coef, ctop, cbot):
    return pl.pallas_call(
        outer_first,
        in_specs=whole(7),
        out_specs=whole(2),
        out_shape=arrays((4 * ROWS, 128), (4 * ROWS, 128)),
        compiler_params=params(),
        cost_estimate=cost(8),
        name="outer_first",
    )(top, low, high, bot, coef, ctop, cbot)


def strip_lines(even_ref, odd_ref, own_ref, out_ref):
    entry = lanes((32, 128)) % 4
    even_is_right = lanes((32, 128)) * 0 + lax.axis_index("rad") % 2 == 0
    number = lax.broadcasted_iota(jnp.int32, (32, 128), 0)
    for var in range(4):
        at = slice(COEF + 32 * var, COEF + 32 * var + 32)
        even, odd = even_ref[at], odd_ref[at]
        right = jnp.where(even_is_right, even, odd)
        left = jnp.where(even_is_right, odd, even)
        lines = jnp.where(entry < 2, pltpu.roll(right, 126, axis=1), pltpu.roll(left, 2, axis=1))
        result = lines
        for i in (0, 1, 3, 4):
            here = (number >= 5 * i) & (number < 5 * i + 5)
            result = jnp.where(here, pltpu.roll(lines, (4 * (i - 2)) % 128, axis=1), result)
        out_ref[var, 0:32] = result
        own = own_ref.at[at]
        one_entry = entry[0:1]
        for i in range(5):
            k = 5 * i
            two = jnp.where(one_entry < 2, own[k + 4 : k + 5], own[k : k + 1])
            one = jnp.where(one_entry == 1, own[k + 3 : k + 4], 0.0)
            one = jnp.where(one_entry == 2, own[k + 1 : k + 2], one)
            turn = (4 * (i - 2)) % 128
            out_ref[var, 32 + i : 33 + i] = pltpu.roll(two, turn, axis=1) if turn else two
            out_ref[var, 37 + i : 38 + i] = pltpu.roll(one, turn, axis=1) if turn else one
        out_ref[var, 42:48] = jnp.zeros((6, 128), F32)


def call_strip_lines(even, odd, own):
    return pl.pallas_call(
        strip_lines,
        in_specs=whole(3),
        out_specs=whole(1)[0],
        out_shape=arrays((4, 48, 128))[0],
        compiler_params=params(),
        name="strip_lines",
    )(even, odd, own)


def strips(even_ref, odd_ref, own_ref, line_ref, mend_y_ref, mend_u_ref, shift_ref):
    entry = lanes((32, 128)) % 4
    even_is_right = lanes((32, 128)) * 0 + lax.axis_index("rad") % 2 == 0
    every = [(var, half) for var in range(4) for half in range(2)]

    def part(ref, kind, var, half):
        start = kind * ROWS + var * 64 + half * 32
        return ref[start : start + 32]

    def line(var, k):
        return jnp.broadcast_to(line_ref[var, k : k + 1], (32, 128))

    def turn(pack, by):
        return pltpu.roll(pack, by % 128, axis=1)

    def over_rows(sums):
        total = sums[2]
        for i in (0, 1, 3, 4):
            total = total + turn(sums[i], 4 * (2 - i))
        return total

    def beyond(var, rim, crossed):
        return over_rows([line(var, 32 + i) * rim + line(var, 37 + i) * crossed for i in range(5)])

    for var, half in every:
        at = slice(32 * half, 32 * half + 32)
        tail = jnp.where(even_is_right, part(odd_ref, 0, var, half), part(even_ref, 0, var, half))
        head = jnp.where(even_is_right, part(even_ref, 1, var, half), part(odd_ref, 1, var, half))
        rim = jnp.where(entry < 2, head, tail)
        outer = jnp.where(entry < 2, tail, head)
        own = jnp.where(entry < 2, part(own_ref, 1, var, half), part(own_ref, 0, var, half))
        up, down = turn(rim, 1), turn(rim, -1)
        shift_ref[0, var, at] = jnp.where(entry < 2, turn(own, -2), turn(outer, 2))
        shift_ref[1, var, at] = jnp.where(
            entry == 0, turn(own, -3), jnp.where(entry == 2, turn(outer, 1), up)
        )
        shift_ref[2, var, at] = rim
        shift_ref[3, var, at] = jnp.where(
            entry == 3, turn(own, 3), jnp.where(entry == 1, turn(outer, -1), down)
        )
        shift_ref[4, var, at] = jnp.where(entry < 2, turn(outer, -2), turn(own, 2))
        shift_ref[5, var, at] = jnp.where(entry == 1, up, down)
    for var, half in every:
        at = slice(32 * half, 32 * half + 32)
        mend_y_ref[var, at] = 0.5 * beyond(var, shift_ref[2, var, at], shift_ref[5, var, at])
    for var, half in every:
        at = slice(32 * half, 32 * half + 32)
        sums = []
        for i in range(5):
            total = line(var, 5 * i) * shift_ref[0, var, at]
            for j in range(1, 5):
                total = total + line(var, 5 * i + j) * shift_ref[j, var, at]
            sums.append(total)
        total = over_rows(sums)
        for w in range(4):
            total = total + line(var, 25 + w) * shift_ref[2, w, at]
        shift_ref[6, var, at] = shift_ref[2, var, at] + 0.5 * total
    for var, half in every:
        at = slice(32 * half, 32 * half + 32)
        rim = shift_ref[6, var, at]
        crossed = jnp.where(entry == 1, turn(rim, 1), turn(rim, -1))
        mend_u_ref[var, at] = beyond(var, rim, crossed)


def call_strips(even, odd, own, lines):
    return pl.pallas_call(
        strips,
        in_specs=whole(4),
        out_specs=whole(2),
        out_shape=arrays((4, 64, 128), (4, 64, 128)),
        scratch_shapes=[pltpu.VMEM((7, 4, 64, 128), F32)],
        compiler_params=params(),
        name="strips",
    )(even, odd, own, lines)


PARTS = ((0, 4), (4, 12), (12, 16))


def second(ranges, parts, n_y, sides, *refs):
    y_refs, refs = refs[:n_y], refs[n_y:]
    mend_y_ref, mend_u_ref, coef_ref = refs[:3]
    u_refs, refs = refs[3 : 3 + len(parts)], refs[3 + len(parts) :]
    out_refs, refs = refs[: len(parts)], refs[len(parts) :]
    y_ref = refs[-1]
    bounds = {1: ((2, 14),), 3: ((-2, 2), (2, 14), (14, 18))}[n_y]
    y_parts = [(first, stop, ref) for (first, stop), ref in zip(bounds, y_refs)]
    u_parts = [(first, stop, ref) for (first, stop), ref in zip(parts, u_refs)]
    sources = sorted({s for first, stop in ranges for s in range(first - 2, stop + 2)})
    whole_y = ((-2, 18, y_ref),)

    def mend(var, half):
        pack = mend_y_ref[var, pl.ds(pl.multiple_of(half * WIDTH, WIDTH), WIDTH)]
        for row in sources:
            put(y_ref, row + 2, var, half, pick(y_parts, row, var, half) + unplace(pack, row))

    each_part(mend)

    def one(var, half):
        pack = mend_u_ref[var, pl.ds(pl.multiple_of(half * WIDTH, WIDTH), WIDTH)]

        def finish(row, total):
            for w in range(4):
                total = total + line_of(coef_ref, var, 25 + w, row) * pick(whole_y, row, w, half)
            total = total + unplace(pack, row)
            for (first, stop), ref in zip(parts, out_refs):
                if first <= row < stop:
                    put(ref, row - first, var, half, pick(u_parts, row, var, half) + total)

        for first, stop in ranges:
            sweep(
                first, stop, lambda s: pick(whole_y, s, var, half),
                lambda k, row: line_of(coef_ref, var, k, row), finish,
            )

    each_part(one)
    if sides:
        sort_sides(lax.axis_index("azim"), refs[0], refs[1], out_refs[0], out_refs[-1])


def call_second(ranges, parts, ys, mend_y, mend_u, coef, us, sides=False):
    outs = [((stop - first) * ROWS, 128) for first, stop in parts]
    outs += [outs[0]] * (2 * sides)
    return pl.pallas_call(
        functools.partial(second, ranges, parts, len(ys), sides),
        in_specs=whole(len(ys) + 3 + len(us)),
        out_specs=whole(len(outs)),
        out_shape=arrays(*outs),
        scratch_shapes=[pltpu.VMEM((20 * ROWS, 128), F32)],
        compiler_params=params(),
        cost_estimate=cost(8),
        name="second",
    )(*ys, mend_y, mend_u, coef, *us)


def gather(rows_ref, table_ref, out_ref, wide_ref, picked_ref):
    @pl.loop(0, 16)
    def _(k):
        at = pl.ds(pl.multiple_of(k * 256, 256), 256)
        wide_ref[at] = table_ref[at].astype(F32)

    @pl.loop(0, 32)
    def _(k):
        for t in range(32):
            slot = k * 32 + t
            picked_ref[pl.ds(slot, 1)] = wide_ref[pl.ds(rows_ref[slot], 1)]

    @pl.loop(0, 4)
    def _(k):
        at = pl.ds(pl.multiple_of(k * 256, 256), 256)
        out_ref[at] = picked_ref[at].astype(BF16)


def call_gather(rows, table):
    return pl.pallas_call(
        gather,
        in_specs=[pl.BlockSpec(memory_space=pltpu.SMEM)] + whole(1),
        out_specs=whole(1)[0],
        out_shape=jax.ShapeDtypeStruct((rows.shape[0], table.shape[1]), BF16),
        scratch_shapes=[pltpu.VMEM((4096, 512), F32), pltpu.VMEM((1024, 512), F32)],
        compiler_params=params(),
        name="gather",
    )(rows, table)


def spread(count_ref, cells_ref, weights_ref, high_ref, low_ref):
    step = pl.program_id(0)
    cell = lax.broadcasted_iota(jnp.int32, (256, 1024), 0) + step * 256
    live = lax.broadcasted_iota(jnp.int32, (1, 1024), 1) < count_ref[0]
    cells = jnp.where(live, cells_ref[...], -1)
    hit = jnp.where(cells == cell, 1.0, 0.0).astype(BF16)
    total = jnp.dot(hit, weights_ref[...], preferred_element_type=F32)
    high = total.astype(BF16)
    high_ref[...] = high
    low_ref[...] = (total - high.astype(F32)).astype(BF16)


def call_spread(count, cells, weights):
    return pl.pallas_call(
        spread,
        grid=(8,),
        in_specs=[pl.BlockSpec(memory_space=pltpu.SMEM)]
        + [spec((1, 1024), lambda s: (0, 0)), spec((1024, 512), lambda s: (0, 0))],
        out_specs=[spec((256, 512), lambda s: (s, 0))] * 2,
        out_shape=[jax.ShapeDtypeStruct((2048, 512), BF16)] * 2,
        compiler_params=params(1),
        cost_estimate=pl.CostEstimate(flops=2 << 30, bytes_accessed=6 << 20, transcendentals=0),
        name="spread",
    )(count, cells, weights)


def leave(low_ref, mid_ref, high_ref, w_high_ref, w_low_ref, out_ref, markov_ref, turned_ref, sems):
    copies = []
    rows = []
    for k, ((first, stop), ref) in enumerate(zip(PARTS, (low_ref, mid_ref, high_ref))):
        for row in range(first, stop):
            rows.append(ref.at[(row - first) * ROWS : (row - first + 1) * ROWS])
            turned_ref[row] = rows[-1][...].T
        at = pl.ds(first, stop - first)
        copies.append(pltpu.make_async_copy(turned_ref.at[at], out_ref.at[at], sems.at[k]))
        copies[-1].start()
    sums = jnp.zeros((256, 512), F32)
    for k in range(8):
        u = jnp.concatenate([rows[2 * k][...], rows[2 * k + 1][...]], axis=1)
        u_high = u.astype(BF16)
        u_low = (u - u_high.astype(F32)).astype(BF16)
        w_high = w_high_ref[256 * k : 256 * k + 256]
        w_low = w_low_ref[256 * k : 256 * k + 256]
        sums = sums + jnp.dot(u_high, w_high, preferred_element_type=F32)
        sums = sums + jnp.dot(u_low, w_high, preferred_element_type=F32)
        sums = sums + jnp.dot(u_high, w_low, preferred_element_type=F32)
    markov_ref[...] = sums.T
    for copy in copies:
        copy.wait()


def call_leave(low, mid, high, w_high, w_low):
    return pl.pallas_call(
        leave,
        in_specs=whole(5),
        out_specs=[pl.BlockSpec(memory_space=pltpu.HBM)] + whole(1),
        out_shape=arrays((16, 128, 256), (512, 256)),
        scratch_shapes=[pltpu.VMEM((16, 128, 256), F32), pltpu.SemaphoreType.DMA((3,))],
        compiler_params=params(),
        cost_estimate=pl.CostEstimate(flops=2 << 30, bytes_accessed=8 << 20, transcendentals=0),
        name="leave",
    )(low, mid, high, w_high, w_low)


def swaps(count, first, periodic):
    pairs = [(k, (k + 1) % count) for k in range(first, count, 2) if periodic or k + 1 < count]
    return pairs + [(target, source) for source, target in pairs]


def body(perturbation_in, coefficients, wall_cells, wall_count, mode_row, mode_table):
    n_azim, n_rad = lax.axis_size("azim"), lax.axis_size("rad")

    def swap(block, axis, odd):
        count = lax.axis_size(axis)
        return lax.ppermute(block, axis, swaps(count, odd, axis == "azim"))

    slots = wall_cells.shape[0]
    weights = call_gather(mode_row, mode_table)
    w_high, w_low = call_spread(wall_count, wall_cells.reshape(1, slots), weights)

    low, high, even, odd = call_enter_outer(perturbation_in, coefficients)
    mid = call_enter_inner(perturbation_in)
    coef_edge, coef = call_coef_edges(coefficients)
    for step in range(STEPS):
        even = swap(even, "azim", 0)
        odd = swap(odd, "azim", 1)
        y_mid, edge = call_inner_first(low, mid, high, coef)
        if step == 0:
            edge, w_high = lax.optimization_barrier((edge, w_high))
            top, bot, own, *tails = call_halo_edges(even, odd, edge, coef_edge)
        else:
            top, bot, own = call_halo_edges(even, odd, edge)
        sides = swap(own, "rad", 0), swap(own, "rad", 1), own
        ys = call_outer_first(top, low, high, bot, coef, *tails)
        ys = ys[0], y_mid, ys[1]
        if step == 0:
            lines = call_strip_lines(*sides)
        mends = call_strips(*sides, lines)
        if step < STEPS - 1:
            (new_mid,) = call_second(((4, 12),), PARTS[1:2], ys[1:2], *mends, coef, (mid,))
            low, high, even, odd = call_second(
                (PARTS[0], PARTS[2]), (PARTS[0], PARTS[2]), ys, *mends, coef, (low, high), sides=True
            )
            mid = new_mid
        else:
            low, mid, high = call_second(((0, 16),), PARTS, ys, *mends, coef, (low, mid, high))
    out, term = call_leave(low, mid, high, w_high, w_low)
    count = n_azim * n_rad
    parts = lax.all_to_all(term.reshape(count, -1, term.shape[1]), ("azim", "rad"), 0, 0)
    return out, jnp.sum(parts, axis=0)


def solution(mesh):
    return jax.shard_map(
        body,
        mesh=mesh,
        in_specs=(
            P("azim", "rad", None),
            P(None, None, "azim", "rad"),
            P(("azim", "rad")),
            P(("azim", "rad")),
            P(("azim", "rad")),
            P(),
        ),
        out_specs=(P("azim", "rad", None), P(("azim", "rad"), None)),
        check_vma=False,
    )
```

```python
import functools

import jax
import jax.numpy as jnp
from jax import lax
from jax.experimental import pallas as pl
from jax.experimental.pallas import tpu as pltpu
from jax.sharding import PartitionSpec as P

STEPS = 2
VMEM_LIMIT = 32 * 1024 * 1024
ENTER_LIMIT = 58 * 1024 * 1024
F32 = jnp.float32
BF16 = jnp.bfloat16


def spec(block, index):
    return pl.BlockSpec(block, index)


def whole(n):
    return [pl.BlockSpec(memory_space=pltpu.VMEM)] * n


def params(n=0):
    order = ("arbitrary",) * n if n else None
    return pltpu.CompilerParams(vmem_limit_bytes=VMEM_LIMIT, dimension_semantics=order)


def cost(rows):
    return pl.CostEstimate(flops=2 * 29 * rows * 128 * 256, bytes_accessed=rows << 18, transcendentals=0)


def arrays(*shapes):
    return [jax.ShapeDtypeStruct(shape, F32) for shape in shapes]


def lanes(shape):
    return lax.broadcasted_iota(jnp.int32, shape, len(shape) - 1)


ROWS = 256
WIDTH = 32
UNROLL = 8
TAIL = 4 * ROWS
COEF = 2 * ROWS
LINES = 3 * ROWS


def window(ref, row, var, half):
    start = pl.multiple_of(row * ROWS + var * 64 + half * WIDTH, 8)
    return ref[pl.ds(start, WIDTH), :]


def put(ref, row, var, half, value):
    start = pl.multiple_of(row * ROWS + var * 64 + half * WIDTH, 8)
    ref[pl.ds(start, WIDTH), :] = value


def pick(parts, row, var, half):
    for first, stop, ref in parts:
        if first <= row < stop:
            return window(ref, row - first, var, half)
    raise IndexError(row)


def place(pack, row, value, cell):
    lane = lanes(value.shape)
    base = 4 * (row + 4)
    here = (lane >= base) & (lane < base + 4)
    return jnp.where(here, pltpu.roll(value, (base - cell) % 128, axis=1), pack)


def unplace(pack, row):
    lane = lanes(pack.shape)
    base = 4 * (row + 4)
    turned = pltpu.roll(pack, (126 - base) % 128, axis=1)
    return jnp.where((lane < 2) | (lane >= 126), turned, 0.0)


def each_part(body):
    halves = 64 // WIDTH

    @pl.loop(0, 4 * halves, unroll=UNROLL)
    def _(step):
        body(step // halves, step % halves)


def sweep(first, stop, source, weight, finish):
    for row in range(first, stop):
        sums = [None] * 5
        for i in range(5):
            u = source(row + i - 2)
            for j in range(5):
                term = weight(5 * i + j, row) * u
                sums[j] = term if i == 0 else sums[j] + term
        total = sums[2]
        for j in (0, 1, 3, 4):
            total = total + pltpu.roll(sums[j], (2 - j) % 128, axis=1)
        finish(row, total)


def turned(k, line):
    if k >= 25 or k % 5 == 2:
        return line
    lane = lanes(line.shape)
    keep = (lane < 126, lane < 127, None, lane >= 1, lane >= 2)[k % 5]
    return jnp.where(keep, pltpu.roll(line, (k % 5 - 2) % 128, axis=1), 0.0)


def line_of(coef_ref, var, k, row):
    return jnp.broadcast_to(coef_ref[var, k, row : row + 1], (WIDTH, 128))


def tail_line(ref, var, k, row):
    lines = ref.at[pl.ds(pl.multiple_of(var * 64, 64), 64)]
    return jnp.broadcast_to(lines[2 * k + row : 2 * k + row + 1], (WIDTH, 128))


def sort_sides(index, even_ref, odd_ref, below_ref, above_ref):
    even_is_above = index % 2 == 0

    @pl.when(even_is_above)
    def _():
        odd_ref[...], even_ref[...] = below_ref[...], above_ref[...]

    @pl.when(jnp.logical_not(even_is_above))
    def _():
        even_ref[...], odd_ref[...] = below_ref[...], above_ref[...]


def enter_outer(x_ref, coef_ref, low_ref, high_ref, even_ref, odd_ref, x_in, coef_in, sems):
    copies = [
        pltpu.make_async_copy(x_ref.at[pl.ds(0, 4)], x_in.at[0], sems.at[0]),
        pltpu.make_async_copy(x_ref.at[pl.ds(12, 4)], x_in.at[1], sems.at[1]),
        pltpu.make_async_copy(coef_ref, coef_in, sems.at[2]),
    ]
    for copy in copies:
        copy.start()
    low_ref[TAIL:] = jnp.zeros((256, 128), F32)
    high_ref[TAIL:] = jnp.zeros((256, 128), F32)
    for side, ref in ((0, low_ref), (1, high_ref)):
        copies[side].wait()

        @pl.loop(0, 4)
        def _(k):
            ref[pl.ds(pl.multiple_of(k * ROWS, ROWS), ROWS)] = x_in[side, k].T

    copies[2].wait()

    @pl.loop(0, 4)
    def _(k):
        lines = pl.ds(pl.multiple_of(TAIL + k * 64, 64), 58)
        low_ref[lines] = coef_in[k, :, 0:2].reshape(58, 128)
        high_ref[lines] = coef_in[k, :, 14:16].reshape(58, 128)

    sort_sides(lax.axis_index("azim"), even_ref, odd_ref, low_ref, high_ref)


def call_enter_outer(x, coef):
    return pl.pallas_call(
        enter_outer,
        in_specs=[pl.BlockSpec(memory_space=pltpu.HBM)] * 2,
        out_specs=whole(4),
        out_shape=arrays(*[(TAIL + 256, 128)] * 4),
        scratch_shapes=[
            pltpu.VMEM((2, 4, 128, 256), F32),
            pltpu.VMEM((4, 29, 16, 128), F32),
            pltpu.SemaphoreType.DMA((3,)),
        ],
        compiler_params=pltpu.CompilerParams(vmem_limit_bytes=ENTER_LIMIT),
        name="enter_outer",
    )(x, coef)


def enter_inner(x_ref, mid_ref, x_in, sem):
    copy = pltpu.make_async_copy(x_ref.at[pl.ds(4, 8)], x_in, sem)
    copy.start()
    copy.wait()

    @pl.loop(0, 8)
    def _(k):
        mid_ref[pl.ds(pl.multiple_of(k * ROWS, ROWS), ROWS)] = x_in[k].T


def call_enter_inner(x):
    return pl.pallas_call(
        enter_inner,
        in_specs=[pl.BlockSpec(memory_space=pltpu.HBM)],
        out_specs=whole(1)[0],
        out_shape=arrays((8 * ROWS, 128))[0],
        scratch_shapes=[pltpu.VMEM((8, 128, 256), F32), pltpu.SemaphoreType.DMA],
        compiler_params=params(),
        name="enter_inner",
    )(x)


def inner_first(low_ref, mid_ref, high_ref, coef_ref, y_ref):
    parts = ((0, 4, low_ref), (4, 12, mid_ref), (12, 16, high_ref))

    def one(var, half):
        def finish(row, total):
            for w in range(4):
                total = total + line_of(coef_ref, var, 25 + w, row) * pick(parts, row, w, half)
            put(y_ref, row - 2, var, half, pick(parts, row, var, half) + 0.5 * total)

        sweep(
            2, 14, lambda s: pick(parts, s, var, half),
            lambda k, row: line_of(coef_ref, var, k, row), finish,
        )

    each_part(one)


def call_inner_first(low, mid, high, coef):
    return pl.pallas_call(
        inner_first,
        in_specs=whole(4),
        out_specs=whole(1)[0],
        out_shape=arrays((12 * ROWS, 128))[0],
        compiler_params=params(),
        cost_estimate=cost(12),
        name="inner_first",
    )(low, mid, high, coef)


def coef_edges(coef_ref, out_ref, turned_ref):
    @pl.loop(0, 4)
    def _(var):
        for k in range(29):
            lines = pl.ds(pl.multiple_of(var * 464 + k * 16, 16), 16)
            turned_ref[var, k] = turned(k, coef_ref[lines, :])

    out_ref[...] = jnp.zeros_like(out_ref)
    for var in range(4):
        pack = jnp.zeros((29, 128), F32)
        for row in range(16):
            pack = place(pack, row, coef_ref[pl.ds(var * 464 + row, 29, stride=16), :], 126)
        out_ref[32 * var : 32 * var + 29] = pack


def call_coef_edges(coef):
    return pl.pallas_call(
        coef_edges,
        in_specs=whole(1),
        out_specs=whole(2),
        out_shape=arrays((128, 128), coef.shape),
        compiler_params=params(),
        name="coef_edges",
    )(coef.reshape(-1, 128))


def edges(low_ref, mid_ref, high_ref, *refs):
    out_ref = refs[-1]
    parts = ((0, 4, low_ref), (4, 12, mid_ref), (12, 16, high_ref))

    def one(var, half):
        tail = jnp.zeros((WIDTH, 128), F32)
        head = jnp.zeros((WIDTH, 128), F32)
        for row in range(16):
            value = pick(parts, row, var, half)
            tail, head = place(tail, row, value, 124), place(head, row, value, 0)
        put(out_ref, 0, var, half, tail)
        put(out_ref, 1, var, half, head)

    each_part(one)
    if len(refs) > 1:
        out_ref[COEF:] = refs[0][...]


def call_edges(low, mid, high, *coef_edge):
    return pl.pallas_call(
        edges,
        in_specs=whole(3 + len(coef_edge)),
        out_specs=whole(1)[0],
        out_shape=arrays((COEF + 128 * len(coef_edge), 128))[0],
        compiler_params=params(),
        name="edges",
    )(low, mid, high, *coef_edge)


def corner(even_ref, odd_ref, own_ref, pack_ref, *refs):
    fold_even_ref, fold_odd_ref, low_ref, high_ref = refs
    entry = lanes((32, 128)) % 4
    even_is_right = lanes((32, 128)) * 0 + lax.axis_index("rad") % 2 == 0
    lane = lanes((32, 128))

    def turn(pack, by):
        return pltpu.roll(pack, by % 128, axis=1) if by % 128 else pack

    folds = {}
    for var in range(4):
        for half in range(2):
            at = slice(var * 64 + half * 32, var * 64 + half * 32 + 32)
            below = slice(ROWS + at.start, ROWS + at.stop)
            tail = jnp.where(even_is_right, odd_ref[at], even_ref[at])
            head = jnp.where(even_is_right, even_ref[below], odd_ref[below])
            rims = jnp.where(entry < 2, head, tail), jnp.where(entry < 2, tail, head)
            pack_ref[at] = rims[0]
            pack_ref[below] = rims[1]
            pack_ref[2 * ROWS + at.start : 2 * ROWS + at.stop] = jnp.where(
                entry < 2, turn(own_ref[at], -2), turn(own_ref[below], 2)
            )
            for side, first in (("low", 16), ("high", 64)):
                fold = folds.get((side, half), jnp.zeros((32, 128), F32))
                for k in range(2):
                    to = 32 * var + 16 * k
                    here = (lane >= to) & (lane < to + 16)
                    fold = jnp.where(here, turn(rims[k], to - first), fold)
                folds[side, half] = fold
    for half in range(2):
        at = slice(32 * half, 32 * half + 32)
        low_ref[at], high_ref[at] = folds["low", half], folds["high", half]
    if own_ref.shape[0] > COEF:
        fold = {"low": jnp.zeros((32, 128), F32), "high": jnp.zeros((32, 128), F32)}
        for var in range(4):
            at = slice(COEF + 32 * var, COEF + 32 * var + 32)
            right = jnp.where(even_is_right, even_ref[at], odd_ref[at])
            left = jnp.where(even_is_right, odd_ref[at], even_ref[at])
            lines = jnp.where(entry < 2, turn(right, 126), turn(left, 2))
            pack_ref[LINES + 32 * var : LINES + 32 * var + 32] = lines
            for side, first in (("low", 16), ("high", 72)):
                here = (lane >= 32 * var) & (lane < 32 * var + 8)
                fold[side] = jnp.where(here, turn(lines, 32 * var - first), fold[side])
        low_ref[64:96], high_ref[64:96] = fold["low"], fold["high"]
    sort_sides(lax.axis_index("azim"), fold_even_ref, fold_odd_ref, low_ref, high_ref)


def call_corner(even, odd, own):
    first = own.shape[0] > COEF
    fold = (64 + 32 * first, 128)
    return pl.pallas_call(
        corner,
        in_specs=whole(3),
        out_specs=whole(3),
        out_shape=arrays((LINES + 128 * first, 128), fold, fold),
        scratch_shapes=[pltpu.VMEM(fold, F32)] * 2,
        compiler_params=params(),
        name="corner",
    )(even, odd, own)


def halo(even_ref, odd_ref, fold_even_ref, fold_odd_ref, pack_ref, *refs):
    first_step = len(refs) > 5
    coef_edge_ref = refs[0] if first_step else None
    refs = refs[first_step:]
    top_ref, bot_ref, out_ref = refs[:3]
    fold_top_ref, fold_bot_ref = refs[-2:]
    even_is_above = lax.axis_index("azim") % 2 == 0
    lane = lanes((32, 128))

    def turn(pack, by):
        return pltpu.roll(pack, by % 128, axis=1) if by % 128 else pack

    def sorted_sides(above):
        below_from, above_from = (odd_ref, even_ref) if above else (even_ref, odd_ref)
        folds = (fold_odd_ref, fold_even_ref) if above else (fold_even_ref, fold_odd_ref)
        top_ref[...], bot_ref[...] = below_from[:TAIL], above_from[:TAIL]
        fold_top_ref[...], fold_bot_ref[...] = folds[0][...], folds[1][...]
        if first_step:
            refs[3][...], refs[4][...] = below_from[TAIL:], above_from[TAIL:]

    pl.when(even_is_above)(lambda: sorted_sides(True))
    pl.when(jnp.logical_not(even_is_above))(lambda: sorted_sides(False))
    for var in range(4):
        for half in range(2):
            at = slice(var * 64 + half * 32, var * 64 + half * 32 + 32)
            c = slice(half * 32, half * 32 + 32)
            for k in range(2):
                here = slice(ROWS * k + at.start, ROWS * k + at.stop)
                source = 32 * var + 16 * k
                pack = jnp.where(lane < 16, turn(fold_top_ref[c], -source), pack_ref[here])
                out_ref[here] = jnp.where(
                    (lane >= 80) & (lane < 96), turn(fold_bot_ref[c], 80 - source), pack
                )
            here = slice(2 * ROWS + at.start, 2 * ROWS + at.stop)
            seam = pack_ref[here]
            for k in range(4):
                rows = slice(ROWS * k + at.start, ROWS * k + at.stop)
                seam = place(seam, k - 4, top_ref[rows], 126)
                seam = place(seam, k + 16, bot_ref[rows], 126)
            out_ref[here] = seam
    if first_step:
        ctop_ref, cbot_ref = refs[3:5]
        number = lax.broadcasted_iota(jnp.int32, (64, 128), 0) // 2
        for var in range(4):
            here = slice(LINES + 32 * var, LINES + 32 * var + 32)
            pack = pack_ref[here]
            pack = jnp.where((lane >= 8) & (lane < 16), turn(fold_top_ref[64:96], 8 - 32 * var), pack)
            out_ref[here] = jnp.where(
                (lane >= 80) & (lane < 88), turn(fold_bot_ref[64:96], 80 - 32 * var), pack
            )
            pack = coef_edge_ref[32 * var : 32 * var + 29]
            for k in range(2):
                lines = pl.ds(64 * var + k, 29, stride=2)
                pack = place(pack, k - 2, ctop_ref[lines, :], 126)
                pack = place(pack, k + 16, cbot_ref[lines, :], 126)
            start = LINES + 128 + 32 * var
            out_ref[start : start + 29] = pack
            out_ref[start + 29 : start + 32] = jnp.zeros((3, 128), F32)
        for var in range(4):
            at = slice(64 * var, 64 * var + 64)
            for ref in (ctop_ref, cbot_ref):
                lines = ref[at]
                result = lines
                for j in (0, 1, 3, 4):
                    here = (number % 5 == j) & (number < 25)
                    result = jnp.where(here, turned(j, lines), result)
                ref[at] = result


def call_halo(even, odd, fold_even, fold_odd, pack, *coef_edge):
    return pl.pallas_call(
        halo,
        in_specs=whole(5 + len(coef_edge)),
        out_specs=whole(3 + 2 * len(coef_edge)),
        out_shape=arrays(
            (TAIL, 128), (TAIL, 128), (LINES + 256 * len(coef_edge), 128),
            *[(256, 128)] * (2 * len(coef_edge)),
        ),
        scratch_shapes=[pltpu.VMEM(fold_even.shape, F32)] * 2,
        compiler_params=params(),
        name="halo",
    )(even, odd, fold_even, fold_odd, pack, *coef_edge)


def outer_first(top_ref, low_ref, high_ref, bot_ref, coef_ref, ctop_ref, cbot_ref,
                y_low_ref, y_high_ref):
    parts = ((-4, 0, top_ref), (0, 4, low_ref), (12, 16, high_ref), (16, 20, bot_ref))

    def one(var, half):
        def weight(k, row):
            if row < 0:
                return tail_line(ctop_ref, var, k, row + 2)
            if row < 16:
                return line_of(coef_ref, var, k, row)
            return tail_line(cbot_ref, var, k, row - 16)

        def finish(row, total):
            for w in range(4):
                total = total + weight(25 + w, row) * pick(parts, row, w, half)
            value = pick(parts, row, var, half) + 0.5 * total
            if row < 2:
                put(y_low_ref, row + 2, var, half, value)
            else:
                put(y_high_ref, row - 14, var, half, value)

        for first in (-2, 14):
            sweep(first, first + 4, lambda s: pick(parts, s, var, half), weight, finish)

    each_part(one)


def call_outer_first(top, low, high, bot, coef, ctop, cbot):
    return pl.pallas_call(
        outer_first,
        in_specs=whole(7),
        out_specs=whole(2),
        out_shape=arrays((4 * ROWS, 128), (4 * ROWS, 128)),
        compiler_params=params(),
        cost_estimate=cost(8),
        name="outer_first",
    )(top, low, high, bot, coef, ctop, cbot)


def strip_lines(pack_ref, out_ref):
    entry = lanes((1, 128)) % 4
    number = lax.broadcasted_iota(jnp.int32, (32, 128), 0)
    for var in range(4):
        lines = pack_ref[LINES + 32 * var : LINES + 32 * var + 32]
        result = lines
        for i in (0, 1, 3, 4):
            here = (number >= 5 * i) & (number < 5 * i + 5)
            result = jnp.where(here, pltpu.roll(lines, (4 * (i - 2)) % 128, axis=1), result)
        out_ref[var, 0:32] = result
        start = LINES + 128 + 32 * var
        own = pack_ref.at[start : start + 32]
        for i in range(5):
            k = 5 * i
            two = jnp.where(entry < 2, own[k + 4 : k + 5], own[k : k + 1])
            one = jnp.where(entry == 1, own[k + 3 : k + 4], 0.0)
            one = jnp.where(entry == 2, own[k + 1 : k + 2], one)
            turn = (4 * (i - 2)) % 128
            out_ref[var, 32 + i : 33 + i] = pltpu.roll(two, turn, axis=1) if turn else two
            out_ref[var, 37 + i : 38 + i] = pltpu.roll(one, turn, axis=1) if turn else one
        out_ref[var, 42:48] = jnp.zeros((6, 128), F32)


def call_strip_lines(pack):
    return pl.pallas_call(
        strip_lines,
        in_specs=whole(1),
        out_specs=whole(1)[0],
        out_shape=arrays((4, 48, 128))[0],
        compiler_params=params(),
        name="strip_lines",
    )(pack)


def strips(pack_ref, line_ref, mend_y_ref, mend_u_ref, shift_ref):
    entry = lanes((32, 128)) % 4
    every = [(var, half) for var in range(4) for half in range(2)]

    def part(kind, var, half):
        start = kind * ROWS + var * 64 + half * 32
        return pack_ref[start : start + 32]

    def line(var, k):
        return jnp.broadcast_to(line_ref[var, k : k + 1], (32, 128))

    def turn(pack, by):
        return pltpu.roll(pack, by % 128, axis=1)

    def over_rows(sums):
        total = sums[2]
        for i in (0, 1, 3, 4):
            total = total + turn(sums[i], 4 * (2 - i))
        return total

    def beyond(var, rim, crossed):
        return over_rows([line(var, 32 + i) * rim + line(var, 37 + i) * crossed for i in range(5)])

    for var, half in every:
        at = slice(32 * half, 32 * half + 32)
        rim, outer, seam = (part(kind, var, half) for kind in range(3))
        up, down = turn(rim, 1), turn(rim, -1)
        shift_ref[0, var, at] = jnp.where(entry < 2, seam, turn(outer, 2))
        shift_ref[1, var, at] = jnp.where(
            entry == 0, turn(seam, -1), jnp.where(entry == 2, turn(outer, 1), up)
        )
        shift_ref[2, var, at] = rim
        shift_ref[3, var, at] = jnp.where(
            entry == 3, turn(seam, 1), jnp.where(entry == 1, turn(outer, -1), down)
        )
        shift_ref[4, var, at] = jnp.where(entry < 2, turn(outer, -2), seam)
        shift_ref[5, var, at] = jnp.where(entry == 1, up, down)
    for var, half in every:
        at = slice(32 * half, 32 * half + 32)
        mend_y_ref[var, at] = 0.5 * beyond(var, shift_ref[2, var, at], shift_ref[5, var, at])
    for var, half in every:
        at = slice(32 * half, 32 * half + 32)
        sums = []
        for i in range(5):
            total = line(var, 5 * i) * shift_ref[0, var, at]
            for j in range(1, 5):
                total = total + line(var, 5 * i + j) * shift_ref[j, var, at]
            sums.append(total)
        total = over_rows(sums)
        for w in range(4):
            total = total + line(var, 25 + w) * shift_ref[2, w, at]
        shift_ref[6, var, at] = shift_ref[2, var, at] + 0.5 * total
    for var, half in every:
        at = slice(32 * half, 32 * half + 32)
        rim = shift_ref[6, var, at]
        crossed = jnp.where(entry == 1, turn(rim, 1), turn(rim, -1))
        mend_u_ref[var, at] = beyond(var, rim, crossed)


def call_strips(pack, lines):
    return pl.pallas_call(
        strips,
        in_specs=whole(2),
        out_specs=whole(2),
        out_shape=arrays((4, 64, 128), (4, 64, 128)),
        scratch_shapes=[pltpu.VMEM((7, 4, 64, 128), F32)],
        compiler_params=params(),
        name="strips",
    )(pack, lines)


PARTS = ((0, 4), (4, 12), (12, 16))


def second(ranges, parts, n_y, sides, *refs):
    y_refs, refs = refs[:n_y], refs[n_y:]
    mend_y_ref, mend_u_ref, coef_ref = refs[:3]
    u_refs, refs = refs[3 : 3 + len(parts)], refs[3 + len(parts) :]
    out_refs, refs = refs[: len(parts)], refs[len(parts) :]
    y_ref = refs[-1]
    bounds = {1: ((2, 14),), 3: ((-2, 2), (2, 14), (14, 18))}[n_y]
    y_parts = [(first, stop, ref) for (first, stop), ref in zip(bounds, y_refs)]
    u_parts = [(first, stop, ref) for (first, stop), ref in zip(parts, u_refs)]
    sources = sorted({s for first, stop in ranges for s in range(first - 2, stop + 2)})
    whole_y = ((-2, 18, y_ref),)

    def mend(var, half):
        pack = mend_y_ref[var, pl.ds(pl.multiple_of(half * WIDTH, WIDTH), WIDTH)]
        for row in sources:
            put(y_ref, row + 2, var, half, pick(y_parts, row, var, half) + unplace(pack, row))

    each_part(mend)

    def one(var, half):
        pack = mend_u_ref[var, pl.ds(pl.multiple_of(half * WIDTH, WIDTH), WIDTH)]

        def finish(row, total):
            for w in range(4):
                total = total + line_of(coef_ref, var, 25 + w, row) * pick(whole_y, row, w, half)
            total = total + unplace(pack, row)
            for (first, stop), ref in zip(parts, out_refs):
                if first <= row < stop:
                    put(ref, row - first, var, half, pick(u_parts, row, var, half) + total)

        for first, stop in ranges:
            sweep(
                first, stop, lambda s: pick(whole_y, s, var, half),
                lambda k, row: line_of(coef_ref, var, k, row), finish,
            )

    each_part(one)
    if sides:
        sort_sides(lax.axis_index("azim"), refs[0], refs[1], out_refs[0], out_refs[-1])


def call_second(ranges, parts, ys, mend_y, mend_u, coef, us, sides=False):
    outs = [((stop - first) * ROWS, 128) for first, stop in parts]
    outs += [outs[0]] * (2 * sides)
    return pl.pallas_call(
        functools.partial(second, ranges, parts, len(ys), sides),
        in_specs=whole(len(ys) + 3 + len(us)),
        out_specs=whole(len(outs)),
        out_shape=arrays(*outs),
        scratch_shapes=[pltpu.VMEM((20 * ROWS, 128), F32)],
        compiler_params=params(),
        cost_estimate=cost(8),
        name="second",
    )(*ys, mend_y, mend_u, coef, *us)


def gather(rows_ref, table_ref, out_ref, wide_ref, picked_ref):
    @pl.loop(0, 16)
    def _(k):
        at = pl.ds(pl.multiple_of(k * 256, 256), 256)
        wide_ref[at] = table_ref[at].astype(F32)

    @pl.loop(0, 32)
    def _(k):
        for t in range(32):
            slot = k * 32 + t
            picked_ref[pl.ds(slot, 1)] = wide_ref[pl.ds(rows_ref[slot], 1)]

    @pl.loop(0, 4)
    def _(k):
        at = pl.ds(pl.multiple_of(k * 256, 256), 256)
        out_ref[at] = picked_ref[at].astype(BF16)


def call_gather(rows, table):
    return pl.pallas_call(
        gather,
        in_specs=[pl.BlockSpec(memory_space=pltpu.SMEM)] + whole(1),
        out_specs=whole(1)[0],
        out_shape=jax.ShapeDtypeStruct((rows.shape[0], table.shape[1]), BF16),
        scratch_shapes=[pltpu.VMEM((4096, 512), F32), pltpu.VMEM((1024, 512), F32)],
        compiler_params=params(),
        name="gather",
    )(rows, table)


def spread(count_ref, cells_ref, weights_ref, high_ref, low_ref):
    step = pl.program_id(0)
    cell = lax.broadcasted_iota(jnp.int32, (256, 1024), 0) + step * 256
    live = lax.broadcasted_iota(jnp.int32, (1, 1024), 1) < count_ref[0]
    cells = jnp.where(live, cells_ref[...], -1)
    hit = jnp.where(cells == cell, 1.0, 0.0).astype(BF16)
    total = jnp.dot(hit, weights_ref[...], preferred_element_type=F32)
    high = total.astype(BF16)
    high_ref[...] = high
    low_ref[...] = (total - high.astype(F32)).astype(BF16)


def call_spread(count, cells, weights):
    return pl.pallas_call(
        spread,
        grid=(8,),
        in_specs=[pl.BlockSpec(memory_space=pltpu.SMEM)]
        + [spec((1, 1024), lambda s: (0, 0)), spec((1024, 512), lambda s: (0, 0))],
        out_specs=[spec((256, 512), lambda s: (s, 0))] * 2,
        out_shape=[jax.ShapeDtypeStruct((2048, 512), BF16)] * 2,
        compiler_params=params(1),
        cost_estimate=pl.CostEstimate(flops=2 << 30, bytes_accessed=6 << 20, transcendentals=0),
        name="spread",
    )(count, cells, weights)


def leave(low_ref, mid_ref, high_ref, w_high_ref, w_low_ref, out_ref, markov_ref, turned_ref, sems):
    copies = []
    rows = []
    for k, ((first, stop), ref) in enumerate(zip(PARTS, (low_ref, mid_ref, high_ref))):
        for row in range(first, stop):
            rows.append(ref.at[(row - first) * ROWS : (row - first + 1) * ROWS])
            turned_ref[row] = rows[-1][...].T
        at = pl.ds(first, stop - first)
        copies.append(pltpu.make_async_copy(turned_ref.at[at], out_ref.at[at], sems.at[k]))
        copies[-1].start()
    sums = jnp.zeros((256, 512), F32)
    for k in range(8):
        u = jnp.concatenate([rows[2 * k][...], rows[2 * k + 1][...]], axis=1)
        u_high = u.astype(BF16)
        u_low = (u - u_high.astype(F32)).astype(BF16)
        w_high = w_high_ref[256 * k : 256 * k + 256]
        w_low = w_low_ref[256 * k : 256 * k + 256]
        sums = sums + jnp.dot(u_high, w_high, preferred_element_type=F32)
        sums = sums + jnp.dot(u_low, w_high, preferred_element_type=F32)
        sums = sums + jnp.dot(u_high, w_low, preferred_element_type=F32)
    markov_ref[...] = sums.T
    for copy in copies:
        copy.wait()


def call_leave(low, mid, high, w_high, w_low):
    return pl.pallas_call(
        leave,
        in_specs=whole(5),
        out_specs=[pl.BlockSpec(memory_space=pltpu.HBM)] + whole(1),
        out_shape=arrays((16, 128, 256), (512, 256)),
        scratch_shapes=[pltpu.VMEM((16, 128, 256), F32), pltpu.SemaphoreType.DMA((3,))],
        compiler_params=params(),
        cost_estimate=pl.CostEstimate(flops=2 << 30, bytes_accessed=8 << 20, transcendentals=0),
        name="leave",
    )(low, mid, high, w_high, w_low)


def swaps(count, first, periodic):
    pairs = [(k, (k + 1) % count) for k in range(first, count, 2) if periodic or k + 1 < count]
    return pairs + [(target, source) for source, target in pairs]


def body(perturbation_in, coefficients, wall_cells, wall_count, mode_row, mode_table):
    n_azim, n_rad = lax.axis_size("azim"), lax.axis_size("rad")

    def swap(block, axis, odd):
        count = lax.axis_size(axis)
        return lax.ppermute(block, axis, swaps(count, odd, axis == "azim"))

    slots = wall_cells.shape[0]
    weights = call_gather(mode_row, mode_table)
    w_high, w_low = call_spread(wall_count, wall_cells.reshape(1, slots), weights)

    low, high, even, odd = call_enter_outer(perturbation_in, coefficients)
    mid = call_enter_inner(perturbation_in)
    coef_edge, coef = call_coef_edges(coefficients)
    for step in range(STEPS):
        even = swap(even, "azim", 0)
        odd = swap(odd, "azim", 1)
        extra = (coef_edge,) if step == 0 else ()
        own = call_edges(low, mid, high, *extra)
        sides = swap(own, "rad", 0), swap(own, "rad", 1)
        y_mid = call_inner_first(low, mid, high, coef)
        pack, fold_even, fold_odd = call_corner(*sides, own)
        fold_even = swap(fold_even, "azim", 0)
        fold_odd = swap(fold_odd, "azim", 1)
        if step == 0:
            pack, w_high = lax.optimization_barrier((pack, w_high))
        top, bot, pack, *rest = call_halo(even, odd, fold_even, fold_odd, pack, *extra)
        if step == 0:
            tails, lines = rest, call_strip_lines(pack)
        ys = call_outer_first(top, low, high, bot, coef, *tails)
        ys = ys[0], y_mid, ys[1]
        mends = call_strips(pack, lines)
        if step < STEPS - 1:
            (new_mid,) = call_second(((4, 12),), PARTS[1:2], ys[1:2], *mends, coef, (mid,))
            low, high, even, odd = call_second(
                (PARTS[0], PARTS[2]), (PARTS[0], PARTS[2]), ys, *mends, coef, (low, high), sides=True
            )
            mid = new_mid
        else:
            low, mid, high = call_second(((0, 16),), PARTS, ys, *mends, coef, (low, mid, high))
    out, term = call_leave(low, mid, high, w_high, w_low)
    count = n_azim * n_rad
    parts = lax.all_to_all(term.reshape(count, -1, term.shape[1]), ("azim", "rad"), 0, 0)
    return out, jnp.sum(parts, axis=0)


def solution(mesh):
    return jax.shard_map(
        body,
        mesh=mesh,
        in_specs=(
            P("azim", "rad", None),
            P(None, None, "azim", "rad"),
            P(("azim", "rad")),
            P(("azim", "rad")),
            P(("azim", "rad")),
            P(),
        ),
        out_specs=(P("azim", "rad", None), P(("azim", "rad"), None)),
        check_vma=False,
    )
```

```python
import functools

import jax
import jax.numpy as jnp
from jax import lax
from jax.experimental import pallas as pl
from jax.experimental.pallas import tpu as pltpu
from jax.sharding import PartitionSpec as P

STEPS = 2
VMEM_LIMIT = 32 * 1024 * 1024
ENTER_LIMIT = 58 * 1024 * 1024
F32 = jnp.float32
BF16 = jnp.bfloat16


def spec(block, index):
    return pl.BlockSpec(block, index)


def whole(n):
    return [pl.BlockSpec(memory_space=pltpu.VMEM)] * n


def params(n=0):
    order = ("arbitrary",) * n if n else None
    return pltpu.CompilerParams(vmem_limit_bytes=VMEM_LIMIT, dimension_semantics=order)


def cost(rows):
    return pl.CostEstimate(flops=2 * 29 * rows * 128 * 256, bytes_accessed=rows << 18, transcendentals=0)


def arrays(*shapes):
    return [jax.ShapeDtypeStruct(shape, F32) for shape in shapes]


def lanes(shape):
    return lax.broadcasted_iota(jnp.int32, shape, len(shape) - 1)


ROWS = 256
WIDTH = 32
UNROLL = 8
TAIL = 4 * ROWS
PARTS = ((0, 4), (4, 12), (12, 16))
COEF = 2 * ROWS


def window(ref, row, var, half):
    start = pl.multiple_of(row * ROWS + var * 64 + half * WIDTH, 8)
    return ref[pl.ds(start, WIDTH), :]


def put(ref, row, var, half, value):
    start = pl.multiple_of(row * ROWS + var * 64 + half * WIDTH, 8)
    ref[pl.ds(start, WIDTH), :] = value


def pick(parts, row, var, half):
    for first, stop, ref in parts:
        if first <= row < stop:
            return window(ref, row - first, var, half)
    raise IndexError(row)


def place(pack, row, value, cell):
    lane = lanes(value.shape)
    base = 4 * (row + 4)
    here = (lane >= base) & (lane < base + 4)
    return jnp.where(here, pltpu.roll(value, (base - cell) % 128, axis=1), pack)


def unplace(pack, row):
    lane = lanes(pack.shape)
    base = 4 * (row + 4)
    turned = pltpu.roll(pack, (126 - base) % 128, axis=1)
    return jnp.where((lane < 2) | (lane >= 126), turned, 0.0)


def each_part(body):
    halves = 64 // WIDTH

    @pl.loop(0, 4 * halves, unroll=UNROLL)
    def _(step):
        body(step // halves, step % halves)


def sweep(first, stop, source, weight, finish):
    for row in range(first, stop):
        sums = [None] * 5
        for i in range(5):
            u = source(row + i - 2)
            for j in range(5):
                term = weight(5 * i + j, row) * u
                sums[j] = term if i == 0 else sums[j] + term
        total = sums[2]
        for j in (0, 1, 3, 4):
            total = total + pltpu.roll(sums[j], (2 - j) % 128, axis=1)
        finish(row, total)


def turned(k, line):
    if k >= 25 or k % 5 == 2:
        return line
    lane = lanes(line.shape)
    keep = (lane < 126, lane < 127, None, lane >= 1, lane >= 2)[k % 5]
    return jnp.where(keep, pltpu.roll(line, (k % 5 - 2) % 128, axis=1), 0.0)


def line_of(coef_ref, var, k, row):
    return jnp.broadcast_to(coef_ref[var, k, row : row + 1], (WIDTH, 128))


def tail_line(ref, var, k, row):
    lines = ref.at[pl.ds(pl.multiple_of(row * 128 + var * 32, 32), 32)]
    return jnp.broadcast_to(lines[k : k + 1], (WIDTH, 128))


def sort_sides(index, even_ref, odd_ref, below_ref, above_ref):
    even_is_above = index % 2 == 0

    @pl.when(even_is_above)
    def _():
        odd_ref[...], even_ref[...] = below_ref[...], above_ref[...]

    @pl.when(jnp.logical_not(even_is_above))
    def _():
        even_ref[...], odd_ref[...] = below_ref[...], above_ref[...]


def ship(odd, x_ref, coef_ref, out_ref, coef_in, lines, sems):
    goes_up = lax.axis_index("azim") % 2 == odd
    row = jnp.where(goes_up, 12, 0)
    coef_row = pl.multiple_of(jnp.where(goes_up, 8, 0), 8)
    state = pltpu.make_async_copy(x_ref.at[pl.ds(row, 4)], out_ref.at[pl.ds(0, 4)], sems.at[0])
    state.start()
    load = pltpu.make_async_copy(coef_ref.at[:, pl.ds(coef_row, 8)], coef_in, sems.at[1])
    load.start()
    lines[...] = jnp.zeros_like(lines)
    load.wait()

    def fill(first):
        for var in range(4):
            for k in range(2):
                lines[32 * var : 32 * var + 29, 128 * k : 128 * k + 128] = coef_in[
                    29 * var : 29 * var + 29, first + k, :
                ]

    pl.when(goes_up)(lambda: fill(6))
    pl.when(jnp.logical_not(goes_up))(lambda: fill(0))
    store = pltpu.make_async_copy(lines, out_ref.at[4], sems.at[2])
    store.start()
    state.wait()
    store.wait()


def call_ship(odd, x, coef):
    hbm = pl.BlockSpec(memory_space=pltpu.HBM)
    return pl.pallas_call(
        functools.partial(ship, odd),
        in_specs=[hbm] * 2,
        out_specs=hbm,
        out_shape=arrays((5, 128, 256))[0],
        scratch_shapes=[
            pltpu.VMEM((116, 8, 128), F32),
            pltpu.VMEM((128, 256), F32),
            pltpu.SemaphoreType.DMA((3,)),
        ],
        compiler_params=pltpu.CompilerParams(vmem_limit_bytes=ENTER_LIMIT),
        name="ship",
    )(x, coef.reshape(116, 16, 128))


def enter(x_ref, low_ref, mid_ref, high_ref):
    for (first, stop), ref in zip(PARTS, (low_ref, mid_ref, high_ref)):

        @pl.loop(0, stop - first)
        def _(k):
            ref[pl.ds(pl.multiple_of(k * ROWS, ROWS), ROWS)] = x_ref[first + k].T


def call_enter(x):
    return pl.pallas_call(
        enter,
        in_specs=whole(1),
        out_specs=whole(3),
        out_shape=arrays((4 * ROWS, 128), (8 * ROWS, 128), (4 * ROWS, 128)),
        compiler_params=params(),
        name="enter",
    )(x)


def inner_first(low_ref, mid_ref, high_ref, coef_ref, y_ref, edge_ref):
    parts = ((0, 4, low_ref), (4, 12, mid_ref), (12, 16, high_ref))

    def one(var, half):
        def finish(row, total):
            for w in range(4):
                total = total + line_of(coef_ref, var, 25 + w, row) * pick(parts, row, w, half)
            put(y_ref, row - 2, var, half, pick(parts, row, var, half) + 0.5 * total)

        sweep(
            2, 14, lambda s: pick(parts, s, var, half),
            lambda k, row: line_of(coef_ref, var, k, row), finish,
        )
        tail = jnp.zeros((WIDTH, 128), F32)
        head = jnp.zeros((WIDTH, 128), F32)
        for row in range(16):
            value = pick(parts, row, var, half)
            tail, head = place(tail, row, value, 124), place(head, row, value, 0)
        put(edge_ref, 0, var, half, tail)
        put(edge_ref, 1, var, half, head)

    each_part(one)


def call_inner_first(low, mid, high, coef):
    return pl.pallas_call(
        inner_first,
        in_specs=whole(4),
        out_specs=whole(2),
        out_shape=arrays((12 * ROWS, 128), (2 * ROWS, 128)),
        compiler_params=params(),
        cost_estimate=cost(12),
        name="inner_first",
    )(low, mid, high, coef)


def coef_edges(coef_ref, out_ref, turned_ref):
    @pl.loop(0, 4)
    def _(var):
        for k in range(29):
            lines = pl.ds(pl.multiple_of(var * 464 + k * 16, 16), 16)
            turned_ref[var, k] = turned(k, coef_ref[lines, :])

    out_ref[...] = jnp.zeros_like(out_ref)
    for var in range(4):
        pack = jnp.zeros((29, 128), F32)
        for row in range(16):
            pack = place(pack, row, coef_ref[pl.ds(var * 464 + row, 29, stride=16), :], 126)
        out_ref[32 * var : 32 * var + 29] = pack


def call_coef_edges(coef):
    return pl.pallas_call(
        coef_edges,
        in_specs=whole(1),
        out_specs=whole(2),
        out_shape=arrays((128, 128), coef.shape),
        compiler_params=params(),
        name="coef_edges",
    )(coef.reshape(-1, 128))


def halo_edges(odd_ref, even_ref, edge_ref, *refs):
    top_ref, bot_ref, out_ref = refs[len(refs) > 3 :][:3]
    first_step = len(refs) > 3
    even_is_above = lax.axis_index("azim") % 2 == 0

    def sorted_sides(above):
        sides = (odd_ref, even_ref) if above else (even_ref, odd_ref)
        for side, ref in zip(sides, (top_ref, bot_ref)):
            if first_step:
                for k in range(4):
                    ref[ROWS * k : ROWS * k + ROWS] = side[k].T
            else:
                ref[...] = side[...]
        if first_step:
            for side, ref in zip(sides, refs[4:]):
                for k in range(2):
                    ref[128 * k : 128 * k + 128] = side[4, :, 128 * k : 128 * k + 128]

    pl.when(even_is_above)(lambda: sorted_sides(True))
    pl.when(jnp.logical_not(even_is_above))(lambda: sorted_sides(False))

    def one(var, half):
        tail = window(edge_ref, 0, var, half)
        head = window(edge_ref, 1, var, half)
        for k in range(4):
            for row, ref in ((k - 4, top_ref), (k + 16, bot_ref)):
                value = window(ref, k, var, half)
                tail, head = place(tail, row, value, 124), place(head, row, value, 0)
        put(out_ref, 0, var, half, tail)
        put(out_ref, 1, var, half, head)

    each_part(one)
    if first_step:
        coef_edge_ref, (ctop_ref, cbot_ref) = refs[0], refs[4:]
        number = lax.broadcasted_iota(jnp.int32, (32, 128), 0)
        for var in range(4):
            pack = coef_edge_ref[32 * var : 32 * var + 32]
            for k in range(2):
                at = slice(128 * k + 32 * var, 128 * k + 32 * var + 32)
                for ref, row in ((ctop_ref, k - 2), (cbot_ref, k + 16)):
                    lines = ref[at]
                    pack = place(pack, row, lines, 126)
                    result = lines
                    for j in (0, 1, 3, 4):
                        here = (number % 5 == j) & (number < 25)
                        result = jnp.where(here, turned(j, lines), result)
                    ref[at] = result
            out_ref[COEF + 32 * var : COEF + 32 * var + 32] = pack


def call_halo_edges(even, odd, edge, *coef_edge):
    return pl.pallas_call(
        halo_edges,
        in_specs=whole(3 + len(coef_edge)),
        out_specs=whole(3 + 2 * len(coef_edge)),
        out_shape=arrays(
            (TAIL, 128), (TAIL, 128), (COEF + 128 * len(coef_edge), 128),
            *[(256, 128)] * (2 * len(coef_edge)),
        ),
        compiler_params=params(),
        name="halo_edges",
    )(odd, even, edge, *coef_edge)


def outer_first(top_ref, low_ref, high_ref, bot_ref, coef_ref, ctop_ref, cbot_ref,
                y_low_ref, y_high_ref):
    parts = ((-4, 0, top_ref), (0, 4, low_ref), (12, 16, high_ref), (16, 20, bot_ref))

    def one(var, half):
        def weight(k, row):
            if row < 0:
                return tail_line(ctop_ref, var, k, row + 2)
            if row < 16:
                return line_of(coef_ref, var, k, row)
            return tail_line(cbot_ref, var, k, row - 16)

        def finish(row, total):
            for w in range(4):
                total = total + weight(25 + w, row) * pick(parts, row, w, half)
            value = pick(parts, row, var, half) + 0.5 * total
            if row < 2:
                put(y_low_ref, row + 2, var, half, value)
            else:
                put(y_high_ref, row - 14, var, half, value)

        for first in (-2, 14):
            sweep(first, first + 4, lambda s: pick(parts, s, var, half), weight, finish)

    each_part(one)


def call_outer_first(top, low, high, bot, coef, ctop, cbot):
    return pl.pallas_call(
        outer_first,
        in_specs=whole(7),
        out_specs=whole(2),
        out_shape=arrays((4 * ROWS, 128), (4 * ROWS, 128)),
        compiler_params=params(),
        cost_estimate=cost(8),
        name="outer_first",
    )(top, low, high, bot, coef, ctop, cbot)


def strip_lines(even_ref, odd_ref, own_ref, out_ref):
    entry = lanes((32, 128)) % 4
    even_is_right = lanes((32, 128)) * 0 + lax.axis_index("rad") % 2 == 0
    number = lax.broadcasted_iota(jnp.int32, (32, 128), 0)
    for var in range(4):
        at = slice(COEF + 32 * var, COEF + 32 * var + 32)
        even, odd = even_ref[at], odd_ref[at]
        right = jnp.where(even_is_right, even, odd)
        left = jnp.where(even_is_right, odd, even)
        lines = jnp.where(entry < 2, pltpu.roll(right, 126, axis=1), pltpu.roll(left, 2, axis=1))
        result = lines
        for i in (0, 1, 3, 4):
            here = (number >= 5 * i) & (number < 5 * i + 5)
            result = jnp.where(here, pltpu.roll(lines, (4 * (i - 2)) % 128, axis=1), result)
        out_ref[var, 0:32] = result
        own = own_ref.at[at]
        one_entry = entry[0:1]
        for i in range(5):
            k = 5 * i
            two = jnp.where(one_entry < 2, own[k + 4 : k + 5], own[k : k + 1])
            one = jnp.where(one_entry == 1, own[k + 3 : k + 4], 0.0)
            one = jnp.where(one_entry == 2, own[k + 1 : k + 2], one)
            turn = (4 * (i - 2)) % 128
            out_ref[var, 32 + i : 33 + i] = pltpu.roll(two, turn, axis=1) if turn else two
            out_ref[var, 37 + i : 38 + i] = pltpu.roll(one, turn, axis=1) if turn else one
        out_ref[var, 42:48] = jnp.zeros((6, 128), F32)


def call_strip_lines(even, odd, own):
    return pl.pallas_call(
        strip_lines,
        in_specs=whole(3),
        out_specs=whole(1)[0],
        out_shape=arrays((4, 48, 128))[0],
        compiler_params=params(),
        name="strip_lines",
    )(even, odd, own)


def strips(even_ref, odd_ref, own_ref, line_ref, mend_y_ref, mend_u_ref, shift_ref):
    entry = lanes((32, 128)) % 4
    even_is_right = lanes((32, 128)) * 0 + lax.axis_index("rad") % 2 == 0
    every = [(var, half) for var in range(4) for half in range(2)]

    def part(ref, kind, var, half):
        start = kind * ROWS + var * 64 + half * 32
        return ref[start : start + 32]

    def line(var, k):
        return jnp.broadcast_to(line_ref[var, k : k + 1], (32, 128))

    def turn(pack, by):
        return pltpu.roll(pack, by % 128, axis=1)

    def over_rows(sums):
        total = sums[2]
        for i in (0, 1, 3, 4):
            total = total + turn(sums[i], 4 * (2 - i))
        return total

    def beyond(var, rim, crossed):
        return over_rows([line(var, 32 + i) * rim + line(var, 37 + i) * crossed for i in range(5)])

    for var, half in every:
        at = slice(32 * half, 32 * half + 32)
        tail = jnp.where(even_is_right, part(odd_ref, 0, var, half), part(even_ref, 0, var, half))
        head = jnp.where(even_is_right, part(even_ref, 1, var, half), part(odd_ref, 1, var, half))
        rim = jnp.where(entry < 2, head, tail)
        outer = jnp.where(entry < 2, tail, head)
        own = jnp.where(entry < 2, part(own_ref, 1, var, half), part(own_ref, 0, var, half))
        up, down = turn(rim, 1), turn(rim, -1)
        shift_ref[0, var, at] = jnp.where(entry < 2, turn(own, -2), turn(outer, 2))
        shift_ref[1, var, at] = jnp.where(
            entry == 0, turn(own, -3), jnp.where(entry == 2, turn(outer, 1), up)
        )
        shift_ref[2, var, at] = rim
        shift_ref[3, var, at] = jnp.where(
            entry == 3, turn(own, 3), jnp.where(entry == 1, turn(outer, -1), down)
        )
        shift_ref[4, var, at] = jnp.where(entry < 2, turn(outer, -2), turn(own, 2))
        shift_ref[5, var, at] = jnp.where(entry == 1, up, down)
    for var, half in every:
        at = slice(32 * half, 32 * half + 32)
        mend_y_ref[var, at] = 0.5 * beyond(var, shift_ref[2, var, at], shift_ref[5, var, at])
    for var, half in every:
        at = slice(32 * half, 32 * half + 32)
        sums = []
        for i in range(5):
            total = line(var, 5 * i) * shift_ref[0, var, at]
            for j in range(1, 5):
                total = total + line(var, 5 * i + j) * shift_ref[j, var, at]
            sums.append(total)
        total = over_rows(sums)
        for w in range(4):
            total = total + line(var, 25 + w) * shift_ref[2, w, at]
        shift_ref[6, var, at] = shift_ref[2, var, at] + 0.5 * total
    for var, half in every:
        at = slice(32 * half, 32 * half + 32)
        rim = shift_ref[6, var, at]
        crossed = jnp.where(entry == 1, turn(rim, 1), turn(rim, -1))
        mend_u_ref[var, at] = beyond(var, rim, crossed)


def call_strips(even, odd, own, lines):
    return pl.pallas_call(
        strips,
        in_specs=whole(4),
        out_specs=whole(2),
        out_shape=arrays((4, 64, 128), (4, 64, 128)),
        scratch_shapes=[pltpu.VMEM((7, 4, 64, 128), F32)],
        compiler_params=params(),
        name="strips",
    )(even, odd, own, lines)


def second(ranges, parts, n_y, sides, *refs):
    y_refs, refs = refs[:n_y], refs[n_y:]
    mend_y_ref, mend_u_ref, coef_ref = refs[:3]
    u_refs, refs = refs[3 : 3 + len(parts)], refs[3 + len(parts) :]
    out_refs, refs = refs[: len(parts)], refs[len(parts) :]
    y_ref = refs[-1]
    bounds = {1: ((2, 14),), 3: ((-2, 2), (2, 14), (14, 18))}[n_y]
    y_parts = [(first, stop, ref) for (first, stop), ref in zip(bounds, y_refs)]
    u_parts = [(first, stop, ref) for (first, stop), ref in zip(parts, u_refs)]
    sources = sorted({s for first, stop in ranges for s in range(first - 2, stop + 2)})
    whole_y = ((-2, 18, y_ref),)

    def mend(var, half):
        pack = mend_y_ref[var, pl.ds(pl.multiple_of(half * WIDTH, WIDTH), WIDTH)]
        for row in sources:
            put(y_ref, row + 2, var, half, pick(y_parts, row, var, half) + unplace(pack, row))

    each_part(mend)

    def one(var, half):
        pack = mend_u_ref[var, pl.ds(pl.multiple_of(half * WIDTH, WIDTH), WIDTH)]

        def finish(row, total):
            for w in range(4):
                total = total + line_of(coef_ref, var, 25 + w, row) * pick(whole_y, row, w, half)
            total = total + unplace(pack, row)
            for (first, stop), ref in zip(parts, out_refs):
                if first <= row < stop:
                    put(ref, row - first, var, half, pick(u_parts, row, var, half) + total)

        for first, stop in ranges:
            sweep(
                first, stop, lambda s: pick(whole_y, s, var, half),
                lambda k, row: line_of(coef_ref, var, k, row), finish,
            )

    each_part(one)
    if sides:
        sort_sides(lax.axis_index("azim"), refs[0], refs[1], out_refs[0], out_refs[-1])


def call_second(ranges, parts, ys, mend_y, mend_u, coef, us, sides=False):
    outs = [((stop - first) * ROWS, 128) for first, stop in parts]
    outs += [outs[0]] * (2 * sides)
    return pl.pallas_call(
        functools.partial(second, ranges, parts, len(ys), sides),
        in_specs=whole(len(ys) + 3 + len(us)),
        out_specs=whole(len(outs)),
        out_shape=arrays(*outs),
        scratch_shapes=[pltpu.VMEM((20 * ROWS, 128), F32)],
        compiler_params=params(),
        cost_estimate=cost(8),
        name="second",
    )(*ys, mend_y, mend_u, coef, *us)


def gather(rows_ref, table_ref, out_ref, wide_ref, picked_ref):
    @pl.loop(0, 16)
    def _(k):
        at = pl.ds(pl.multiple_of(k * 256, 256), 256)
        wide_ref[at] = table_ref[at].astype(F32)

    @pl.loop(0, 32)
    def _(k):
        for t in range(32):
            slot = k * 32 + t
            picked_ref[pl.ds(slot, 1)] = wide_ref[pl.ds(rows_ref[slot], 1)]

    @pl.loop(0, 4)
    def _(k):
        at = pl.ds(pl.multiple_of(k * 256, 256), 256)
        out_ref[at] = picked_ref[at].astype(BF16)


def call_gather(rows, table):
    return pl.pallas_call(
        gather,
        in_specs=[pl.BlockSpec(memory_space=pltpu.SMEM)] + whole(1),
        out_specs=whole(1)[0],
        out_shape=jax.ShapeDtypeStruct((rows.shape[0], table.shape[1]), BF16),
        scratch_shapes=[pltpu.VMEM((4096, 512), F32), pltpu.VMEM((1024, 512), F32)],
        compiler_params=params(),
        name="gather",
    )(rows, table)


def spread(count_ref, cells_ref, weights_ref, high_ref, low_ref):
    step = pl.program_id(0)
    cell = lax.broadcasted_iota(jnp.int32, (256, 1024), 0) + step * 256
    live = lax.broadcasted_iota(jnp.int32, (1, 1024), 1) < count_ref[0]
    cells = jnp.where(live, cells_ref[...], -1)
    hit = jnp.where(cells == cell, 1.0, 0.0).astype(BF16)
    total = jnp.dot(hit, weights_ref[...], preferred_element_type=F32)
    high = total.astype(BF16)
    high_ref[...] = high
    low_ref[...] = (total - high.astype(F32)).astype(BF16)


def call_spread(count, cells, weights):
    return pl.pallas_call(
        spread,
        grid=(8,),
        in_specs=[pl.BlockSpec(memory_space=pltpu.SMEM)]
        + [spec((1, 1024), lambda s: (0, 0)), spec((1024, 512), lambda s: (0, 0))],
        out_specs=[spec((256, 512), lambda s: (s, 0))] * 2,
        out_shape=[jax.ShapeDtypeStruct((2048, 512), BF16)] * 2,
        compiler_params=params(1),
        cost_estimate=pl.CostEstimate(flops=2 << 30, bytes_accessed=6 << 20, transcendentals=0),
        name="spread",
    )(count, cells, weights)


def leave(low_ref, mid_ref, high_ref, w_high_ref, w_low_ref, out_ref, markov_ref, turned_ref, sems):
    copies = []
    rows = []
    for k, ((first, stop), ref) in enumerate(zip(PARTS, (low_ref, mid_ref, high_ref))):
        for row in range(first, stop):
            rows.append(ref.at[(row - first) * ROWS : (row - first + 1) * ROWS])
            turned_ref[row] = rows[-1][...].T
        at = pl.ds(first, stop - first)
        copies.append(pltpu.make_async_copy(turned_ref.at[at], out_ref.at[at], sems.at[k]))
        copies[-1].start()
    sums = jnp.zeros((256, 512), F32)
    for k in range(8):
        u = jnp.concatenate([rows[2 * k][...], rows[2 * k + 1][...]], axis=1)
        u_high = u.astype(BF16)
        u_low = (u - u_high.astype(F32)).astype(BF16)
        w_high = w_high_ref[256 * k : 256 * k + 256]
        w_low = w_low_ref[256 * k : 256 * k + 256]
        sums = sums + jnp.dot(u_high, w_high, preferred_element_type=F32)
        sums = sums + jnp.dot(u_low, w_high, preferred_element_type=F32)
        sums = sums + jnp.dot(u_high, w_low, preferred_element_type=F32)
    markov_ref[...] = sums.T
    for copy in copies:
        copy.wait()


def call_leave(low, mid, high, w_high, w_low):
    return pl.pallas_call(
        leave,
        in_specs=whole(5),
        out_specs=[pl.BlockSpec(memory_space=pltpu.HBM)] + whole(1),
        out_shape=arrays((16, 128, 256), (512, 256)),
        scratch_shapes=[pltpu.VMEM((16, 128, 256), F32), pltpu.SemaphoreType.DMA((3,))],
        compiler_params=params(),
        cost_estimate=pl.CostEstimate(flops=2 << 30, bytes_accessed=8 << 20, transcendentals=0),
        name="leave",
    )(low, mid, high, w_high, w_low)


def swaps(count, first, periodic):
    pairs = [(k, (k + 1) % count) for k in range(first, count, 2) if periodic or k + 1 < count]
    return pairs + [(target, source) for source, target in pairs]


def body(perturbation_in, coefficients, wall_cells, wall_count, mode_row, mode_table):
    n_azim, n_rad = lax.axis_size("azim"), lax.axis_size("rad")

    def swap(block, axis, odd):
        count = lax.axis_size(axis)
        return lax.ppermute(block, axis, swaps(count, odd, axis == "azim"))

    slots = wall_cells.shape[0]
    weights = call_gather(mode_row, mode_table)
    w_high, w_low = call_spread(wall_count, wall_cells.reshape(1, slots), weights)

    odd = call_ship(1, perturbation_in, coefficients)
    even = call_ship(0, perturbation_in, coefficients)
    low, mid, high = call_enter(perturbation_in)
    coef_edge, coef = call_coef_edges(coefficients)
    for step in range(STEPS):
        even = swap(even, "azim", 0)
        odd = swap(odd, "azim", 1)
        y_mid, edge = call_inner_first(low, mid, high, coef)
        if step == 0:
            edge, w_high = lax.optimization_barrier((edge, w_high))
            top, bot, own, *tails = call_halo_edges(even, odd, edge, coef_edge)
        else:
            top, bot, own = call_halo_edges(even, odd, edge)
        sides = swap(own, "rad", 0), swap(own, "rad", 1), own
        ys = call_outer_first(top, low, high, bot, coef, *tails)
        ys = ys[0], y_mid, ys[1]
        if step == 0:
            lines = call_strip_lines(*sides)
        mends = call_strips(*sides, lines)
        if step < STEPS - 1:
            (new_mid,) = call_second(((4, 12),), PARTS[1:2], ys[1:2], *mends, coef, (mid,))
            low, high, even, odd = call_second(
                (PARTS[0], PARTS[2]), (PARTS[0], PARTS[2]), ys, *mends, coef, (low, high), sides=True
            )
            mid = new_mid
        else:
            low, mid, high = call_second(((0, 16),), PARTS, ys, *mends, coef, (low, mid, high))
    out, term = call_leave(low, mid, high, w_high, w_low)
    count = n_azim * n_rad
    parts = lax.all_to_all(term.reshape(count, -1, term.shape[1]), ("azim", "rad"), 0, 0)
    return out, jnp.sum(parts, axis=0)


def solution(mesh):
    return jax.shard_map(
        body,
        mesh=mesh,
        in_specs=(
            P("azim", "rad", None),
            P(None, None, "azim", "rad"),
            P(("azim", "rad")),
            P(("azim", "rad")),
            P(("azim", "rad")),
            P(),
        ),
        out_specs=(P("azim", "rad", None), P(("azim", "rad"), None)),
        check_vma=False,
    )
```

```python
import functools

import jax
import jax.numpy as jnp
from jax import lax
from jax.experimental import pallas as pl
from jax.experimental.pallas import tpu as pltpu
from jax.sharding import PartitionSpec as P

STEPS = 2
VMEM_LIMIT = 32 * 1024 * 1024
ENTER_LIMIT = 58 * 1024 * 1024
F32 = jnp.float32
BF16 = jnp.bfloat16


def spec(block, index):
    return pl.BlockSpec(block, index)


def whole(n):
    return [pl.BlockSpec(memory_space=pltpu.VMEM)] * n


def params(n=0):
    order = ("arbitrary",) * n if n else None
    return pltpu.CompilerParams(vmem_limit_bytes=VMEM_LIMIT, dimension_semantics=order)


def cost(rows):
    return pl.CostEstimate(flops=2 * 29 * rows * 128 * 256, bytes_accessed=rows << 18, transcendentals=0)


def arrays(*shapes):
    return [jax.ShapeDtypeStruct(shape, F32) for shape in shapes]


def lanes(shape):
    return lax.broadcasted_iota(jnp.int32, shape, len(shape) - 1)


ROWS = 256
WIDTH = 32
UNROLL = 8
TAIL = 4 * ROWS
PARTS = ((0, 4), (4, 12), (12, 16))
COEF = 2 * ROWS


def window(ref, row, var, half):
    start = pl.multiple_of(row * ROWS + var * 64 + half * WIDTH, 8)
    return ref[pl.ds(start, WIDTH), :]


def put(ref, row, var, half, value):
    start = pl.multiple_of(row * ROWS + var * 64 + half * WIDTH, 8)
    ref[pl.ds(start, WIDTH), :] = value


def pick(parts, row, var, half):
    for first, stop, ref in parts:
        if first <= row < stop:
            return window(ref, row - first, var, half)
    raise IndexError(row)


def place(pack, row, value, cell):
    lane = lanes(value.shape)
    base = 4 * (row + 4)
    here = (lane >= base) & (lane < base + 4)
    return jnp.where(here, pltpu.roll(value, (base - cell) % 128, axis=1), pack)


def unplace(pack, row):
    lane = lanes(pack.shape)
    base = 4 * (row + 4)
    turned = pltpu.roll(pack, (126 - base) % 128, axis=1)
    return jnp.where((lane < 2) | (lane >= 126), turned, 0.0)


def each_part(body):
    halves = 64 // WIDTH

    @pl.loop(0, 4 * halves, unroll=UNROLL)
    def _(step):
        body(step // halves, step % halves)


def sweep(first, stop, source, weight, finish):
    for row in range(first, stop):
        sums = [None] * 5
        for i in range(5):
            u = source(row + i - 2)
            for j in range(5):
                term = weight(5 * i + j, row) * u
                sums[j] = term if i == 0 else sums[j] + term
        total = sums[2]
        for j in (0, 1, 3, 4):
            total = total + pltpu.roll(sums[j], (2 - j) % 128, axis=1)
        finish(row, total)


def turned(k, line):
    if k >= 25 or k % 5 == 2:
        return line
    lane = lanes(line.shape)
    keep = (lane < 126, lane < 127, None, lane >= 1, lane >= 2)[k % 5]
    return jnp.where(keep, pltpu.roll(line, (k % 5 - 2) % 128, axis=1), 0.0)


def line_of(coef_ref, var, k, row):
    return jnp.broadcast_to(coef_ref[var, k, row : row + 1], (WIDTH, 128))


def tail_line(ref, var, k, row):
    lines = ref.at[pl.ds(pl.multiple_of(row * 128 + var * 32, 32), 32)]
    return jnp.broadcast_to(lines[k : k + 1], (WIDTH, 128))


def sort_sides(index, even_ref, odd_ref, below_ref, above_ref):
    even_is_above = index % 2 == 0

    @pl.when(even_is_above)
    def _():
        odd_ref[...], even_ref[...] = below_ref[...], above_ref[...]

    @pl.when(jnp.logical_not(even_is_above))
    def _():
        even_ref[...], odd_ref[...] = below_ref[...], above_ref[...]


def ship(odd, x_ref, coef_ref, out_ref, coef_in, sems):
    goes_up = lax.axis_index("azim") % 2 == odd
    row = jnp.where(goes_up, 12, 0)
    coef_row = pl.multiple_of(jnp.where(goes_up, 8, 0), 8)
    state = pltpu.make_async_copy(x_ref.at[pl.ds(row, 4)], out_ref.at[pl.ds(0, 4)], sems.at[0])
    state.start()
    load = pltpu.make_async_copy(coef_ref.at[:, pl.ds(coef_row, 8)], coef_in, sems.at[1])
    load.start()
    out_ref[4] = jnp.zeros((128, 256), F32)
    load.wait()

    def fill(first):
        for var in range(4):
            for k in range(2):
                out_ref[4, 32 * var : 32 * var + 29, 128 * k : 128 * k + 128] = coef_in[
                    29 * var : 29 * var + 29, first + k, :
                ]

    pl.when(goes_up)(lambda: fill(6))
    pl.when(jnp.logical_not(goes_up))(lambda: fill(0))
    state.wait()


def call_ship(odd, x, coef):
    hbm = pl.BlockSpec(memory_space=pltpu.HBM)
    return pl.pallas_call(
        functools.partial(ship, odd),
        in_specs=[hbm] * 2,
        out_specs=whole(1)[0],
        out_shape=arrays((5, 128, 256))[0],
        scratch_shapes=[pltpu.VMEM((116, 8, 128), F32), pltpu.SemaphoreType.DMA((2,))],
        compiler_params=pltpu.CompilerParams(vmem_limit_bytes=ENTER_LIMIT),
        name="ship",
    )(x, coef.reshape(116, 16, 128))


def enter(x_ref, low_ref, mid_ref, high_ref):
    for (first, stop), ref in zip(PARTS, (low_ref, mid_ref, high_ref)):

        @pl.loop(0, stop - first)
        def _(k):
            ref[pl.ds(pl.multiple_of(k * ROWS, ROWS), ROWS)] = x_ref[first + k].T


def call_enter(x):
    return pl.pallas_call(
        enter,
        in_specs=whole(1),
        out_specs=whole(3),
        out_shape=arrays((4 * ROWS, 128), (8 * ROWS, 128), (4 * ROWS, 128)),
        compiler_params=params(),
        name="enter",
    )(x)


def inner_first(low_ref, mid_ref, high_ref, coef_ref, y_ref, edge_ref):
    parts = ((0, 4, low_ref), (4, 12, mid_ref), (12, 16, high_ref))

    def one(var, half):
        def finish(row, total):
            for w in range(4):
                total = total + line_of(coef_ref, var, 25 + w, row) * pick(parts, row, w, half)
            put(y_ref, row - 2, var, half, pick(parts, row, var, half) + 0.5 * total)

        sweep(
            2, 14, lambda s: pick(parts, s, var, half),
            lambda k, row: line_of(coef_ref, var, k, row), finish,
        )
        tail = jnp.zeros((WIDTH, 128), F32)
        head = jnp.zeros((WIDTH, 128), F32)
        for row in range(16):
            value = pick(parts, row, var, half)
            tail, head = place(tail, row, value, 124), place(head, row, value, 0)
        put(edge_ref, 0, var, half, tail)
        put(edge_ref, 1, var, half, head)

    each_part(one)


def call_inner_first(low, mid, high, coef):
    return pl.pallas_call(
        inner_first,
        in_specs=whole(4),
        out_specs=whole(2),
        out_shape=arrays((12 * ROWS, 128), (2 * ROWS, 128)),
        compiler_params=params(),
        cost_estimate=cost(12),
        name="inner_first",
    )(low, mid, high, coef)


def coef_edges(coef_ref, out_ref, turned_ref):
    @pl.loop(0, 4)
    def _(var):
        for k in range(29):
            lines = pl.ds(pl.multiple_of(var * 464 + k * 16, 16), 16)
            turned_ref[var, k] = turned(k, coef_ref[lines, :])

    out_ref[...] = jnp.zeros_like(out_ref)
    for var in range(4):
        pack = jnp.zeros((29, 128), F32)
        for row in range(16):
            pack = place(pack, row, coef_ref[pl.ds(var * 464 + row, 29, stride=16), :], 126)
        out_ref[32 * var : 32 * var + 29] = pack


def call_coef_edges(coef):
    return pl.pallas_call(
        coef_edges,
        in_specs=whole(1),
        out_specs=whole(2),
        out_shape=arrays((128, 128), coef.shape),
        compiler_params=params(),
        name="coef_edges",
    )(coef.reshape(-1, 128))


def halo_edges(odd_ref, even_ref, edge_ref, *refs):
    first_step = len(refs) > 5
    top_ref, bot_ref, out_ref = refs[first_step:][:3]
    rad_even_ref, rad_odd_ref = refs[-2:]
    even_is_above = lax.axis_index("azim") % 2 == 0

    def sorted_sides(above):
        sides = (odd_ref, even_ref) if above else (even_ref, odd_ref)
        for side, ref in zip(sides, (top_ref, bot_ref)):
            if first_step:
                for k in range(4):
                    ref[ROWS * k : ROWS * k + ROWS] = side[k].T
            else:
                ref[...] = side[...]
        if first_step:
            for side, ref in zip(sides, refs[4:6]):
                for k in range(2):
                    ref[128 * k : 128 * k + 128] = side[4, :, 128 * k : 128 * k + 128]

    pl.when(even_is_above)(lambda: sorted_sides(True))
    pl.when(jnp.logical_not(even_is_above))(lambda: sorted_sides(False))

    def one(var, half):
        tail = window(edge_ref, 0, var, half)
        head = window(edge_ref, 1, var, half)
        for k in range(4):
            for row, ref in ((k - 4, top_ref), (k + 16, bot_ref)):
                value = window(ref, k, var, half)
                tail, head = place(tail, row, value, 124), place(head, row, value, 0)
        put(out_ref, 0, var, half, tail)
        put(out_ref, 1, var, half, head)

    each_part(one)
    if first_step:
        coef_edge_ref, ctop_ref, cbot_ref = refs[0], refs[4], refs[5]
        number = lax.broadcasted_iota(jnp.int32, (32, 128), 0)
        for var in range(4):
            pack = coef_edge_ref[32 * var : 32 * var + 32]
            for k in range(2):
                at = slice(128 * k + 32 * var, 128 * k + 32 * var + 32)
                for ref, row in ((ctop_ref, k - 2), (cbot_ref, k + 16)):
                    lines = ref[at]
                    pack = place(pack, row, lines, 126)
                    result = lines
                    for j in (0, 1, 3, 4):
                        here = (number % 5 == j) & (number < 25)
                        result = jnp.where(here, turned(j, lines), result)
                    ref[at] = result
            out_ref[COEF + 32 * var : COEF + 32 * var + 32] = pack
        rad_even_ref[ROWS:] = out_ref[COEF:]
        rad_odd_ref[ROWS:] = out_ref[COEF:]
    even_is_right = lax.axis_index("rad") % 2 == 0

    @pl.when(even_is_right)
    def _():
        rad_even_ref[:ROWS], rad_odd_ref[:ROWS] = out_ref[:ROWS], out_ref[ROWS:COEF]

    @pl.when(jnp.logical_not(even_is_right))
    def _():
        rad_odd_ref[:ROWS], rad_even_ref[:ROWS] = out_ref[:ROWS], out_ref[ROWS:COEF]


def call_halo_edges(even, odd, edge, *coef_edge):
    return pl.pallas_call(
        halo_edges,
        in_specs=whole(3 + len(coef_edge)),
        out_specs=whole(5 + 2 * len(coef_edge)),
        out_shape=arrays(
            (TAIL, 128), (TAIL, 128), (COEF + 128 * len(coef_edge), 128),
            *[(256, 128)] * (2 * len(coef_edge)),
            *[(ROWS + 128 * len(coef_edge), 128)] * 2,
        ),
        compiler_params=params(),
        name="halo_edges",
    )(odd, even, edge, *coef_edge)


def outer_first(top_ref, low_ref, high_ref, bot_ref, coef_ref, ctop_ref, cbot_ref,
                y_low_ref, y_high_ref):
    parts = ((-4, 0, top_ref), (0, 4, low_ref), (12, 16, high_ref), (16, 20, bot_ref))

    def one(var, half):
        def weight(k, row):
            if row < 0:
                return tail_line(ctop_ref, var, k, row + 2)
            if row < 16:
                return line_of(coef_ref, var, k, row)
            return tail_line(cbot_ref, var, k, row - 16)

        def finish(row, total):
            for w in range(4):
                total = total + weight(25 + w, row) * pick(parts, row, w, half)
            value = pick(parts, row, var, half) + 0.5 * total
            if row < 2:
                put(y_low_ref, row + 2, var, half, value)
            else:
                put(y_high_ref, row - 14, var, half, value)

        for first in (-2, 14):
            sweep(first, first + 4, lambda s: pick(parts, s, var, half), weight, finish)

    each_part(one)


def call_outer_first(top, low, high, bot, coef, ctop, cbot):
    return pl.pallas_call(
        outer_first,
        in_specs=whole(7),
        out_specs=whole(2),
        out_shape=arrays((4 * ROWS, 128), (4 * ROWS, 128)),
        compiler_params=params(),
        cost_estimate=cost(8),
        name="outer_first",
    )(top, low, high, bot, coef, ctop, cbot)


def strip_lines(even_ref, odd_ref, own_ref, out_ref):
    entry = lanes((32, 128)) % 4
    even_is_right = lanes((32, 128)) * 0 + lax.axis_index("rad") % 2 == 0
    number = lax.broadcasted_iota(jnp.int32, (32, 128), 0)
    for var in range(4):
        at = slice(COEF + 32 * var, COEF + 32 * var + 32)
        there = slice(ROWS + 32 * var, ROWS + 32 * var + 32)
        even, odd = even_ref[there], odd_ref[there]
        right = jnp.where(even_is_right, even, odd)
        left = jnp.where(even_is_right, odd, even)
        lines = jnp.where(entry < 2, pltpu.roll(right, 126, axis=1), pltpu.roll(left, 2, axis=1))
        result = lines
        for i in (0, 1, 3, 4):
            here = (number >= 5 * i) & (number < 5 * i + 5)
            result = jnp.where(here, pltpu.roll(lines, (4 * (i - 2)) % 128, axis=1), result)
        out_ref[var, 0:32] = result
        own = own_ref.at[at]
        one_entry = entry[0:1]
        for i in range(5):
            k = 5 * i
            two = jnp.where(one_entry < 2, own[k + 4 : k + 5], own[k : k + 1])
            one = jnp.where(one_entry == 1, own[k + 3 : k + 4], 0.0)
            one = jnp.where(one_entry == 2, own[k + 1 : k + 2], one)
            turn = (4 * (i - 2)) % 128
            out_ref[var, 32 + i : 33 + i] = pltpu.roll(two, turn, axis=1) if turn else two
            out_ref[var, 37 + i : 38 + i] = pltpu.roll(one, turn, axis=1) if turn else one
        out_ref[var, 42:48] = jnp.zeros((6, 128), F32)


def call_strip_lines(even, odd, own):
    return pl.pallas_call(
        strip_lines,
        in_specs=whole(3),
        out_specs=whole(1)[0],
        out_shape=arrays((4, 48, 128))[0],
        compiler_params=params(),
        name="strip_lines",
    )(even, odd, own)


def strips(even_ref, odd_ref, own_ref, line_ref, mend_y_ref, mend_u_ref, shift_ref):
    entry = lanes((32, 128)) % 4
    even_is_right = lanes((32, 128)) * 0 + lax.axis_index("rad") % 2 == 0
    every = [(var, half) for var in range(4) for half in range(2)]

    def part(ref, kind, var, half):
        start = kind * ROWS + var * 64 + half * 32
        return ref[start : start + 32]

    def line(var, k):
        return jnp.broadcast_to(line_ref[var, k : k + 1], (32, 128))

    def turn(pack, by):
        return pltpu.roll(pack, by % 128, axis=1)

    def over_rows(sums):
        total = sums[2]
        for i in (0, 1, 3, 4):
            total = total + turn(sums[i], 4 * (2 - i))
        return total

    def beyond(var, rim, crossed):
        return over_rows([line(var, 32 + i) * rim + line(var, 37 + i) * crossed for i in range(5)])

    for var, half in every:
        at = slice(32 * half, 32 * half + 32)
        tail = jnp.where(even_is_right, part(odd_ref, 0, var, half), part(even_ref, 0, var, half))
        head = jnp.where(even_is_right, part(even_ref, 0, var, half), part(odd_ref, 0, var, half))
        rim = jnp.where(entry < 2, head, tail)
        outer = jnp.where(entry < 2, tail, head)
        own = jnp.where(entry < 2, part(own_ref, 1, var, half), part(own_ref, 0, var, half))
        up, down = turn(rim, 1), turn(rim, -1)
        shift_ref[0, var, at] = jnp.where(entry < 2, turn(own, -2), turn(outer, 2))
        shift_ref[1, var, at] = jnp.where(
            entry == 0, turn(own, -3), jnp.where(entry == 2, turn(outer, 1), up)
        )
        shift_ref[2, var, at] = rim
        shift_ref[3, var, at] = jnp.where(
            entry == 3, turn(own, 3), jnp.where(entry == 1, turn(outer, -1), down)
        )
        shift_ref[4, var, at] = jnp.where(entry < 2, turn(outer, -2), turn(own, 2))
        shift_ref[5, var, at] = jnp.where(entry == 1, up, down)
    for var, half in every:
        at = slice(32 * half, 32 * half + 32)
        mend_y_ref[var, at] = 0.5 * beyond(var, shift_ref[2, var, at], shift_ref[5, var, at])
    for var, half in every:
        at = slice(32 * half, 32 * half + 32)
        sums = []
        for i in range(5):
            total = line(var, 5 * i) * shift_ref[0, var, at]
            for j in range(1, 5):
                total = total + line(var, 5 * i + j) * shift_ref[j, var, at]
            sums.append(total)
        total = over_rows(sums)
        for w in range(4):
            total = total + line(var, 25 + w) * shift_ref[2, w, at]
        shift_ref[6, var, at] = shift_ref[2, var, at] + 0.5 * total
    for var, half in every:
        at = slice(32 * half, 32 * half + 32)
        rim = shift_ref[6, var, at]
        crossed = jnp.where(entry == 1, turn(rim, 1), turn(rim, -1))
        mend_u_ref[var, at] = beyond(var, rim, crossed)


def call_strips(even, odd, own, lines):
    return pl.pallas_call(
        strips,
        in_specs=whole(4),
        out_specs=whole(2),
        out_shape=arrays((4, 64, 128), (4, 64, 128)),
        scratch_shapes=[pltpu.VMEM((7, 4, 64, 128), F32)],
        compiler_params=params(),
        name="strips",
    )(even, odd, own, lines)


def second(ranges, parts, n_y, sides, *refs):
    y_refs, refs = refs[:n_y], refs[n_y:]
    mend_y_ref, mend_u_ref, coef_ref = refs[:3]
    u_refs, refs = refs[3 : 3 + len(parts)], refs[3 + len(parts) :]
    out_refs, refs = refs[: len(parts)], refs[len(parts) :]
    y_ref = refs[-1]
    bounds = {1: ((2, 14),), 3: ((-2, 2), (2, 14), (14, 18))}[n_y]
    y_parts = [(first, stop, ref) for (first, stop), ref in zip(bounds, y_refs)]
    u_parts = [(first, stop, ref) for (first, stop), ref in zip(parts, u_refs)]
    sources = sorted({s for first, stop in ranges for s in range(first - 2, stop + 2)})
    whole_y = ((-2, 18, y_ref),)

    def mend(var, half):
        pack = mend_y_ref[var, pl.ds(pl.multiple_of(half * WIDTH, WIDTH), WIDTH)]
        for row in sources:
            put(y_ref, row + 2, var, half, pick(y_parts, row, var, half) + unplace(pack, row))

    each_part(mend)

    def one(var, half):
        pack = mend_u_ref[var, pl.ds(pl.multiple_of(half * WIDTH, WIDTH), WIDTH)]

        def finish(row, total):
            for w in range(4):
                total = total + line_of(coef_ref, var, 25 + w, row) * pick(whole_y, row, w, half)
            total = total + unplace(pack, row)
            for (first, stop), ref in zip(parts, out_refs):
                if first <= row < stop:
                    put(ref, row - first, var, half, pick(u_parts, row, var, half) + total)

        for first, stop in ranges:
            sweep(
                first, stop, lambda s: pick(whole_y, s, var, half),
                lambda k, row: line_of(coef_ref, var, k, row), finish,
            )

    each_part(one)
    if sides:
        sort_sides(lax.axis_index("azim"), refs[0], refs[1], out_refs[0], out_refs[-1])


def call_second(ranges, parts, ys, mend_y, mend_u, coef, us, sides=False):
    outs = [((stop - first) * ROWS, 128) for first, stop in parts]
    outs += [outs[0]] * (2 * sides)
    return pl.pallas_call(
        functools.partial(second, ranges, parts, len(ys), sides),
        in_specs=whole(len(ys) + 3 + len(us)),
        out_specs=whole(len(outs)),
        out_shape=arrays(*outs),
        scratch_shapes=[pltpu.VMEM((20 * ROWS, 128), F32)],
        compiler_params=params(),
        cost_estimate=cost(8),
        name="second",
    )(*ys, mend_y, mend_u, coef, *us)


def gather(rows_ref, table_ref, out_ref, wide_ref, picked_ref):
    @pl.loop(0, 16)
    def _(k):
        at = pl.ds(pl.multiple_of(k * 256, 256), 256)
        wide_ref[at] = table_ref[at].astype(F32)

    @pl.loop(0, 32)
    def _(k):
        for t in range(32):
            slot = k * 32 + t
            picked_ref[pl.ds(slot, 1)] = wide_ref[pl.ds(rows_ref[slot], 1)]

    @pl.loop(0, 4)
    def _(k):
        at = pl.ds(pl.multiple_of(k * 256, 256), 256)
        out_ref[at] = picked_ref[at].astype(BF16)


def call_gather(rows, table):
    return pl.pallas_call(
        gather,
        in_specs=[pl.BlockSpec(memory_space=pltpu.SMEM)] + whole(1),
        out_specs=whole(1)[0],
        out_shape=jax.ShapeDtypeStruct((rows.shape[0], table.shape[1]), BF16),
        scratch_shapes=[pltpu.VMEM((4096, 512), F32), pltpu.VMEM((1024, 512), F32)],
        compiler_params=params(),
        name="gather",
    )(rows, table)


def spread(count_ref, cells_ref, weights_ref, high_ref, low_ref):
    step = pl.program_id(0)
    cell = lax.broadcasted_iota(jnp.int32, (256, 1024), 0) + step * 256
    live = lax.broadcasted_iota(jnp.int32, (1, 1024), 1) < count_ref[0]
    cells = jnp.where(live, cells_ref[...], -1)
    hit = jnp.where(cells == cell, 1.0, 0.0).astype(BF16)
    total = jnp.dot(hit, weights_ref[...], preferred_element_type=F32)
    high = total.astype(BF16)
    high_ref[...] = high
    low_ref[...] = (total - high.astype(F32)).astype(BF16)


def call_spread(count, cells, weights):
    return pl.pallas_call(
        spread,
        grid=(8,),
        in_specs=[pl.BlockSpec(memory_space=pltpu.SMEM)]
        + [spec((1, 1024), lambda s: (0, 0)), spec((1024, 512), lambda s: (0, 0))],
        out_specs=[spec((256, 512), lambda s: (s, 0))] * 2,
        out_shape=[jax.ShapeDtypeStruct((2048, 512), BF16)] * 2,
        compiler_params=params(1),
        cost_estimate=pl.CostEstimate(flops=2 << 30, bytes_accessed=6 << 20, transcendentals=0),
        name="spread",
    )(count, cells, weights)


def leave(low_ref, mid_ref, high_ref, w_high_ref, w_low_ref, out_ref, markov_ref, turned_ref, sems):
    copies = []
    rows = []
    for k, ((first, stop), ref) in enumerate(zip(PARTS, (low_ref, mid_ref, high_ref))):
        for row in range(first, stop):
            rows.append(ref.at[(row - first) * ROWS : (row - first + 1) * ROWS])
            turned_ref[row] = rows[-1][...].T
        at = pl.ds(first, stop - first)
        copies.append(pltpu.make_async_copy(turned_ref.at[at], out_ref.at[at], sems.at[k]))
        copies[-1].start()
    sums = jnp.zeros((256, 512), F32)
    for k in range(8):
        u = jnp.concatenate([rows[2 * k][...], rows[2 * k + 1][...]], axis=1)
        u_high = u.astype(BF16)
        u_low = (u - u_high.astype(F32)).astype(BF16)
        w_high = w_high_ref[256 * k : 256 * k + 256]
        w_low = w_low_ref[256 * k : 256 * k + 256]
        sums = sums + jnp.dot(u_high, w_high, preferred_element_type=F32)
        sums = sums + jnp.dot(u_low, w_high, preferred_element_type=F32)
        sums = sums + jnp.dot(u_high, w_low, preferred_element_type=F32)
    markov_ref[...] = sums.T
    for copy in copies:
        copy.wait()


def call_leave(low, mid, high, w_high, w_low):
    return pl.pallas_call(
        leave,
        in_specs=whole(5),
        out_specs=[pl.BlockSpec(memory_space=pltpu.HBM)] + whole(1),
        out_shape=arrays((16, 128, 256), (512, 256)),
        scratch_shapes=[pltpu.VMEM((16, 128, 256), F32), pltpu.SemaphoreType.DMA((3,))],
        compiler_params=params(),
        cost_estimate=pl.CostEstimate(flops=2 << 30, bytes_accessed=8 << 20, transcendentals=0),
        name="leave",
    )(low, mid, high, w_high, w_low)


def swaps(count, first, periodic):
    pairs = [(k, (k + 1) % count) for k in range(first, count, 2) if periodic or k + 1 < count]
    return pairs + [(target, source) for source, target in pairs]


def body(perturbation_in, coefficients, wall_cells, wall_count, mode_row, mode_table):
    n_azim, n_rad = lax.axis_size("azim"), lax.axis_size("rad")

    def swap(block, axis, odd):
        count = lax.axis_size(axis)
        return lax.ppermute(block, axis, swaps(count, odd, axis == "azim"))

    slots = wall_cells.shape[0]
    weights = call_gather(mode_row, mode_table)
    w_high, w_low = call_spread(wall_count, wall_cells.reshape(1, slots), weights)

    odd = call_ship(1, perturbation_in, coefficients)
    even = call_ship(0, perturbation_in, coefficients)
    low, mid, high = call_enter(perturbation_in)
    coef_edge, coef = call_coef_edges(coefficients)
    for step in range(STEPS):
        even = swap(even, "azim", 0)
        odd = swap(odd, "azim", 1)
        y_mid, edge = call_inner_first(low, mid, high, coef)
        if step == 0:
            edge, w_high = lax.optimization_barrier((edge, w_high))
            top, bot, own, *tails, rad_even, rad_odd = call_halo_edges(even, odd, edge, coef_edge)
        else:
            top, bot, own, rad_even, rad_odd = call_halo_edges(even, odd, edge)
        sides = swap(rad_even, "rad", 0), swap(rad_odd, "rad", 1), own
        ys = call_outer_first(top, low, high, bot, coef, *tails)
        ys = ys[0], y_mid, ys[1]
        if step == 0:
            lines = call_strip_lines(*sides)
        mends = call_strips(*sides, lines)
        if step < STEPS - 1:
            (new_mid,) = call_second(((4, 12),), PARTS[1:2], ys[1:2], *mends, coef, (mid,))
            low, high, even, odd = call_second(
                (PARTS[0], PARTS[2]), (PARTS[0], PARTS[2]), ys, *mends, coef, (low, high), sides=True
            )
            mid = new_mid
        else:
            low, mid, high = call_second(((0, 16),), PARTS, ys, *mends, coef, (low, mid, high))
    out, term = call_leave(low, mid, high, w_high, w_low)
    count = n_azim * n_rad
    parts = lax.all_to_all(term.reshape(count, -1, term.shape[1]), ("azim", "rad"), 0, 0)
    return out, jnp.sum(parts, axis=0)


def solution(mesh):
    return jax.shard_map(
        body,
        mesh=mesh,
        in_specs=(
            P("azim", "rad", None),
            P(None, None, "azim", "rad"),
            P(("azim", "rad")),
            P(("azim", "rad")),
            P(("azim", "rad")),
            P(),
        ),
        out_specs=(P("azim", "rad", None), P(("azim", "rad"), None)),
        check_vma=False,
    )
```

```python
import functools

import jax
import jax.numpy as jnp
from jax import lax
from jax.experimental import pallas as pl
from jax.experimental.pallas import tpu as pltpu
from jax.sharding import PartitionSpec as P

STEPS = 2
VMEM_LIMIT = 32 * 1024 * 1024
ENTER_LIMIT = 58 * 1024 * 1024
F32 = jnp.float32
BF16 = jnp.bfloat16


def spec(block, index):
    return pl.BlockSpec(block, index)


def whole(n):
    return [pl.BlockSpec(memory_space=pltpu.VMEM)] * n


def params(n=0):
    order = ("arbitrary",) * n if n else None
    return pltpu.CompilerParams(vmem_limit_bytes=VMEM_LIMIT, dimension_semantics=order)


def cost(rows):
    return pl.CostEstimate(flops=2 * 29 * rows * 128 * 256, bytes_accessed=rows << 18, transcendentals=0)


SMALL = pl.CostEstimate(flops=1, bytes_accessed=1, transcendentals=0)


def arrays(*shapes):
    return [jax.ShapeDtypeStruct(shape, F32) for shape in shapes]


def lanes(shape):
    return lax.broadcasted_iota(jnp.int32, shape, len(shape) - 1)


ROWS = 256
WIDTH = 32
UNROLL = 8
TAIL = 4 * ROWS
PARTS = ((0, 4), (4, 12), (12, 16))
COEF = 2 * ROWS


def window(ref, row, var, half):
    start = pl.multiple_of(row * ROWS + var * 64 + half * WIDTH, 8)
    return ref[pl.ds(start, WIDTH), :]


def put(ref, row, var, half, value):
    start = pl.multiple_of(row * ROWS + var * 64 + half * WIDTH, 8)
    ref[pl.ds(start, WIDTH), :] = value


def pick(parts, row, var, half):
    for first, stop, ref in parts:
        if first <= row < stop:
            return window(ref, row - first, var, half)
    raise IndexError(row)


def place(pack, row, value, cell):
    lane = lanes(value.shape)
    base = 4 * (row + 4)
    here = (lane >= base) & (lane < base + 4)
    return jnp.where(here, pltpu.roll(value, (base - cell) % 128, axis=1), pack)


def unplace(pack, row):
    lane = lanes(pack.shape)
    base = 4 * (row + 4)
    turned = pltpu.roll(pack, (126 - base) % 128, axis=1)
    return jnp.where((lane < 2) | (lane >= 126), turned, 0.0)


def each_part(body):
    halves = 64 // WIDTH

    @pl.loop(0, 4 * halves, unroll=UNROLL)
    def _(step):
        body(step // halves, step % halves)


def sweep(first, stop, source, weight, finish):
    for row in range(first, stop):
        sums = [None] * 5
        for i in range(5):
            u = source(row + i - 2)
            for j in range(5):
                term = weight(5 * i + j, row) * u
                sums[j] = term if i == 0 else sums[j] + term
        total = sums[2]
        for j in (0, 1, 3, 4):
            total = total + pltpu.roll(sums[j], (2 - j) % 128, axis=1)
        finish(row, total)


def turned(k, line):
    if k >= 25 or k % 5 == 2:
        return line
    lane = lanes(line.shape)
    keep = (lane < 126, lane < 127, None, lane >= 1, lane >= 2)[k % 5]
    return jnp.where(keep, pltpu.roll(line, (k % 5 - 2) % 128, axis=1), 0.0)


def line_of(coef_ref, var, k, row):
    return jnp.broadcast_to(coef_ref[var, k, row : row + 1], (WIDTH, 128))


def tail_line(ref, var, k, row):
    lines = ref.at[pl.ds(pl.multiple_of(row * 128 + var * 32, 32), 32)]
    return jnp.broadcast_to(lines[k : k + 1], (WIDTH, 128))


def sort_sides(index, even_ref, odd_ref, below_ref, above_ref):
    even_is_above = index % 2 == 0

    @pl.when(even_is_above)
    def _():
        odd_ref[...], even_ref[...] = below_ref[...], above_ref[...]

    @pl.when(jnp.logical_not(even_is_above))
    def _():
        even_ref[...], odd_ref[...] = below_ref[...], above_ref[...]


def ship(odd, x_ref, coef_ref, out_ref, coef_in, sems):
    goes_up = lax.axis_index("azim") % 2 == odd
    row = jnp.where(goes_up, 12, 0)
    coef_row = pl.multiple_of(jnp.where(goes_up, 8, 0), 8)
    state = pltpu.make_async_copy(x_ref.at[pl.ds(row, 4)], out_ref.at[pl.ds(0, 4)], sems.at[0])
    state.start()
    load = pltpu.make_async_copy(coef_ref.at[:, pl.ds(coef_row, 8)], coef_in, sems.at[1])
    load.start()
    out_ref[4] = jnp.zeros((128, 256), F32)
    load.wait()

    def fill(first):
        for var in range(4):
            for k in range(2):
                out_ref[4, 32 * var : 32 * var + 29, 128 * k : 128 * k + 128] = coef_in[
                    29 * var : 29 * var + 29, first + k, :
                ]

    pl.when(goes_up)(lambda: fill(6))
    pl.when(jnp.logical_not(goes_up))(lambda: fill(0))
    state.wait()


def call_ship(odd, x, coef):
    hbm = pl.BlockSpec(memory_space=pltpu.HBM)
    return pl.pallas_call(
        functools.partial(ship, odd),
        in_specs=[hbm] * 2,
        out_specs=whole(1)[0],
        out_shape=arrays((5, 128, 256))[0],
        scratch_shapes=[pltpu.VMEM((116, 8, 128), F32), pltpu.SemaphoreType.DMA((2,))],
        compiler_params=pltpu.CompilerParams(vmem_limit_bytes=ENTER_LIMIT),
        name="ship",
    )(x, coef.reshape(116, 16, 128))


def enter(x_ref, low_ref, mid_ref, high_ref):
    for (first, stop), ref in zip(PARTS, (low_ref, mid_ref, high_ref)):

        @pl.loop(0, stop - first)
        def _(k):
            ref[pl.ds(pl.multiple_of(k * ROWS, ROWS), ROWS)] = x_ref[first + k].T


def call_enter(x):
    return pl.pallas_call(
        enter,
        in_specs=whole(1),
        out_specs=whole(3),
        out_shape=arrays((4 * ROWS, 128), (8 * ROWS, 128), (4 * ROWS, 128)),
        compiler_params=params(),
        name="enter",
    )(x)


def inner_first(low_ref, mid_ref, high_ref, coef_ref, y_ref, edge_ref):
    parts = ((0, 4, low_ref), (4, 12, mid_ref), (12, 16, high_ref))

    def one(var, half):
        def finish(row, total):
            for w in range(4):
                total = total + line_of(coef_ref, var, 25 + w, row) * pick(parts, row, w, half)
            put(y_ref, row - 2, var, half, pick(parts, row, var, half) + 0.5 * total)

        sweep(
            2, 14, lambda s: pick(parts, s, var, half),
            lambda k, row: line_of(coef_ref, var, k, row), finish,
        )
        tail = jnp.zeros((WIDTH, 128), F32)
        head = jnp.zeros((WIDTH, 128), F32)
        for row in range(16):
            value = pick(parts, row, var, half)
            tail, head = place(tail, row, value, 124), place(head, row, value, 0)
        put(edge_ref, 0, var, half, tail)
        put(edge_ref, 1, var, half, head)

    each_part(one)


def call_inner_first(low, mid, high, coef):
    return pl.pallas_call(
        inner_first,
        in_specs=whole(4),
        out_specs=whole(2),
        out_shape=arrays((12 * ROWS, 128), (2 * ROWS, 128)),
        compiler_params=params(),
        cost_estimate=SMALL,
        name="inner_first",
    )(low, mid, high, coef)


def coef_edges(coef_ref, out_ref, turned_ref):
    @pl.loop(0, 4)
    def _(var):
        for k in range(29):
            lines = pl.ds(pl.multiple_of(var * 464 + k * 16, 16), 16)
            turned_ref[var, k] = turned(k, coef_ref[lines, :])

    out_ref[...] = jnp.zeros_like(out_ref)
    for var in range(4):
        pack = jnp.zeros((29, 128), F32)
        for row in range(16):
            pack = place(pack, row, coef_ref[pl.ds(var * 464 + row, 29, stride=16), :], 126)
        out_ref[32 * var : 32 * var + 29] = pack


def call_coef_edges(coef):
    return pl.pallas_call(
        coef_edges,
        in_specs=whole(1),
        out_specs=whole(2),
        out_shape=arrays((128, 128), coef.shape),
        compiler_params=params(),
        name="coef_edges",
    )(coef.reshape(-1, 128))


def halo_edges(odd_ref, even_ref, edge_ref, *refs):
    first_step = len(refs) > 5
    top_ref, bot_ref, out_ref = refs[first_step:][:3]
    rad_even_ref, rad_odd_ref = refs[-2:]
    even_is_above = lax.axis_index("azim") % 2 == 0

    def sorted_sides(above):
        sides = (odd_ref, even_ref) if above else (even_ref, odd_ref)
        for side, ref in zip(sides, (top_ref, bot_ref)):
            if first_step:
                for k in range(4):
                    ref[ROWS * k : ROWS * k + ROWS] = side[k].T
            else:
                ref[...] = side[...]
        if first_step:
            for side, ref in zip(sides, refs[4:6]):
                for k in range(2):
                    ref[128 * k : 128 * k + 128] = side[4, :, 128 * k : 128 * k + 128]

    pl.when(even_is_above)(lambda: sorted_sides(True))
    pl.when(jnp.logical_not(even_is_above))(lambda: sorted_sides(False))

    def one(var, half):
        tail = window(edge_ref, 0, var, half)
        head = window(edge_ref, 1, var, half)
        for k in range(4):
            for row, ref in ((k - 4, top_ref), (k + 16, bot_ref)):
                value = window(ref, k, var, half)
                tail, head = place(tail, row, value, 124), place(head, row, value, 0)
        put(out_ref, 0, var, half, tail)
        put(out_ref, 1, var, half, head)

    each_part(one)
    if first_step:
        coef_edge_ref, ctop_ref, cbot_ref = refs[0], refs[4], refs[5]
        number = lax.broadcasted_iota(jnp.int32, (32, 128), 0)
        for var in range(4):
            pack = coef_edge_ref[32 * var : 32 * var + 32]
            for k in range(2):
                at = slice(128 * k + 32 * var, 128 * k + 32 * var + 32)
                for ref, row in ((ctop_ref, k - 2), (cbot_ref, k + 16)):
                    lines = ref[at]
                    pack = place(pack, row, lines, 126)
                    result = lines
                    for j in (0, 1, 3, 4):
                        here = (number % 5 == j) & (number < 25)
                        result = jnp.where(here, turned(j, lines), result)
                    ref[at] = result
            out_ref[COEF + 32 * var : COEF + 32 * var + 32] = pack
        rad_even_ref[ROWS:] = out_ref[COEF:]
        rad_odd_ref[ROWS:] = out_ref[COEF:]
    even_is_right = lax.axis_index("rad") % 2 == 0

    @pl.when(even_is_right)
    def _():
        rad_even_ref[:ROWS], rad_odd_ref[:ROWS] = out_ref[:ROWS], out_ref[ROWS:COEF]

    @pl.when(jnp.logical_not(even_is_right))
    def _():
        rad_odd_ref[:ROWS], rad_even_ref[:ROWS] = out_ref[:ROWS], out_ref[ROWS:COEF]


def call_halo_edges(even, odd, edge, *coef_edge):
    return pl.pallas_call(
        halo_edges,
        in_specs=whole(3 + len(coef_edge)),
        out_specs=whole(5 + 2 * len(coef_edge)),
        out_shape=arrays(
            (TAIL, 128), (TAIL, 128), (COEF + 128 * len(coef_edge), 128),
            *[(256, 128)] * (2 * len(coef_edge)),
            *[(ROWS + 128 * len(coef_edge), 128)] * 2,
        ),
        compiler_params=params(),
        name="halo_edges",
    )(odd, even, edge, *coef_edge)


def outer_first(top_ref, low_ref, high_ref, bot_ref, coef_ref, ctop_ref, cbot_ref,
                y_low_ref, y_high_ref):
    parts = ((-4, 0, top_ref), (0, 4, low_ref), (12, 16, high_ref), (16, 20, bot_ref))

    def one(var, half):
        def weight(k, row):
            if row < 0:
                return tail_line(ctop_ref, var, k, row + 2)
            if row < 16:
                return line_of(coef_ref, var, k, row)
            return tail_line(cbot_ref, var, k, row - 16)

        def finish(row, total):
            for w in range(4):
                total = total + weight(25 + w, row) * pick(parts, row, w, half)
            value = pick(parts, row, var, half) + 0.5 * total
            if row < 2:
                put(y_low_ref, row + 2, var, half, value)
            else:
                put(y_high_ref, row - 14, var, half, value)

        for first in (-2, 14):
            sweep(first, first + 4, lambda s: pick(parts, s, var, half), weight, finish)

    each_part(one)


def call_outer_first(top, low, high, bot, coef, ctop, cbot):
    return pl.pallas_call(
        outer_first,
        in_specs=whole(7),
        out_specs=whole(2),
        out_shape=arrays((4 * ROWS, 128), (4 * ROWS, 128)),
        compiler_params=params(),
        cost_estimate=cost(8),
        name="outer_first",
    )(top, low, high, bot, coef, ctop, cbot)


def strip_lines(even_ref, odd_ref, own_ref, out_ref):
    entry = lanes((32, 128)) % 4
    even_is_right = lanes((32, 128)) * 0 + lax.axis_index("rad") % 2 == 0
    number = lax.broadcasted_iota(jnp.int32, (32, 128), 0)
    for var in range(4):
        at = slice(COEF + 32 * var, COEF + 32 * var + 32)
        there = slice(ROWS + 32 * var, ROWS + 32 * var + 32)
        even, odd = even_ref[there], odd_ref[there]
        right = jnp.where(even_is_right, even, odd)
        left = jnp.where(even_is_right, odd, even)
        lines = jnp.where(entry < 2, pltpu.roll(right, 126, axis=1), pltpu.roll(left, 2, axis=1))
        result = lines
        for i in (0, 1, 3, 4):
            here = (number >= 5 * i) & (number < 5 * i + 5)
            result = jnp.where(here, pltpu.roll(lines, (4 * (i - 2)) % 128, axis=1), result)
        out_ref[var, 0:32] = result
        own = own_ref.at[at]
        one_entry = entry[0:1]
        for i in range(5):
            k = 5 * i
            two = jnp.where(one_entry < 2, own[k + 4 : k + 5], own[k : k + 1])
            one = jnp.where(one_entry == 1, own[k + 3 : k + 4], 0.0)
            one = jnp.where(one_entry == 2, own[k + 1 : k + 2], one)
            turn = (4 * (i - 2)) % 128
            out_ref[var, 32 + i : 33 + i] = pltpu.roll(two, turn, axis=1) if turn else two
            out_ref[var, 37 + i : 38 + i] = pltpu.roll(one, turn, axis=1) if turn else one
        out_ref[var, 42:48] = jnp.zeros((6, 128), F32)


def call_strip_lines(even, odd, own):
    return pl.pallas_call(
        strip_lines,
        in_specs=whole(3),
        out_specs=whole(1)[0],
        out_shape=arrays((4, 48, 128))[0],
        compiler_params=params(),
        name="strip_lines",
    )(even, odd, own)


def strips(even_ref, odd_ref, own_ref, line_ref, mend_y_ref, mend_u_ref, shift_ref):
    entry = lanes((32, 128)) % 4
    even_is_right = lanes((32, 128)) * 0 + lax.axis_index("rad") % 2 == 0
    every = [(var, half) for var in range(4) for half in range(2)]

    def part(ref, kind, var, half):
        start = kind * ROWS + var * 64 + half * 32
        return ref[start : start + 32]

    def line(var, k):
        return jnp.broadcast_to(line_ref[var, k : k + 1], (32, 128))

    def turn(pack, by):
        return pltpu.roll(pack, by % 128, axis=1)

    def over_rows(sums):
        total = sums[2]
        for i in (0, 1, 3, 4):
            total = total + turn(sums[i], 4 * (2 - i))
        return total

    def beyond(var, rim, crossed):
        return over_rows([line(var, 32 + i) * rim + line(var, 37 + i) * crossed for i in range(5)])

    for var, half in every:
        at = slice(32 * half, 32 * half + 32)
        tail = jnp.where(even_is_right, part(odd_ref, 0, var, half), part(even_ref, 0, var, half))
        head = jnp.where(even_is_right, part(even_ref, 0, var, half), part(odd_ref, 0, var, half))
        rim = jnp.where(entry < 2, head, tail)
        outer = jnp.where(entry < 2, tail, head)
        own = jnp.where(entry < 2, part(own_ref, 1, var, half), part(own_ref, 0, var, half))
        up, down = turn(rim, 1), turn(rim, -1)
        shift_ref[0, var, at] = jnp.where(entry < 2, turn(own, -2), turn(outer, 2))
        shift_ref[1, var, at] = jnp.where(
            entry == 0, turn(own, -3), jnp.where(entry == 2, turn(outer, 1), up)
        )
        shift_ref[2, var, at] = rim
        shift_ref[3, var, at] = jnp.where(
            entry == 3, turn(own, 3), jnp.where(entry == 1, turn(outer, -1), down)
        )
        shift_ref[4, var, at] = jnp.where(entry < 2, turn(outer, -2), turn(own, 2))
        shift_ref[5, var, at] = jnp.where(entry == 1, up, down)
    for var, half in every:
        at = slice(32 * half, 32 * half + 32)
        mend_y_ref[var, at] = 0.5 * beyond(var, shift_ref[2, var, at], shift_ref[5, var, at])
    for var, half in every:
        at = slice(32 * half, 32 * half + 32)
        sums = []
        for i in range(5):
            total = line(var, 5 * i) * shift_ref[0, var, at]
            for j in range(1, 5):
                total = total + line(var, 5 * i + j) * shift_ref[j, var, at]
            sums.append(total)
        total = over_rows(sums)
        for w in range(4):
            total = total + line(var, 25 + w) * shift_ref[2, w, at]
        shift_ref[6, var, at] = shift_ref[2, var, at] + 0.5 * total
    for var, half in every:
        at = slice(32 * half, 32 * half + 32)
        rim = shift_ref[6, var, at]
        crossed = jnp.where(entry == 1, turn(rim, 1), turn(rim, -1))
        mend_u_ref[var, at] = beyond(var, rim, crossed)


def call_strips(even, odd, own, lines):
    return pl.pallas_call(
        strips,
        in_specs=whole(4),
        out_specs=whole(2),
        out_shape=arrays((4, 64, 128), (4, 64, 128)),
        scratch_shapes=[pltpu.VMEM((7, 4, 64, 128), F32)],
        compiler_params=params(),
        name="strips",
    )(even, odd, own, lines)


def second(ranges, parts, n_y, sides, *refs):
    y_refs, refs = refs[:n_y], refs[n_y:]
    mend_y_ref, mend_u_ref, coef_ref = refs[:3]
    u_refs, refs = refs[3 : 3 + len(parts)], refs[3 + len(parts) :]
    out_refs, refs = refs[: len(parts)], refs[len(parts) :]
    y_ref = refs[-1]
    bounds = {1: ((2, 14),), 3: ((-2, 2), (2, 14), (14, 18))}[n_y]
    y_parts = [(first, stop, ref) for (first, stop), ref in zip(bounds, y_refs)]
    u_parts = [(first, stop, ref) for (first, stop), ref in zip(parts, u_refs)]
    sources = sorted({s for first, stop in ranges for s in range(first - 2, stop + 2)})
    whole_y = ((-2, 18, y_ref),)

    def mend(var, half):
        pack = mend_y_ref[var, pl.ds(pl.multiple_of(half * WIDTH, WIDTH), WIDTH)]
        for row in sources:
            put(y_ref, row + 2, var, half, pick(y_parts, row, var, half) + unplace(pack, row))

    each_part(mend)

    def one(var, half):
        pack = mend_u_ref[var, pl.ds(pl.multiple_of(half * WIDTH, WIDTH), WIDTH)]

        def finish(row, total):
            for w in range(4):
                total = total + line_of(coef_ref, var, 25 + w, row) * pick(whole_y, row, w, half)
            total = total + unplace(pack, row)
            for (first, stop), ref in zip(parts, out_refs):
                if first <= row < stop:
                    put(ref, row - first, var, half, pick(u_parts, row, var, half) + total)

        for first, stop in ranges:
            sweep(
                first, stop, lambda s: pick(whole_y, s, var, half),
                lambda k, row: line_of(coef_ref, var, k, row), finish,
            )

    each_part(one)
    if sides:
        sort_sides(lax.axis_index("azim"), refs[0], refs[1], out_refs[0], out_refs[-1])


def call_second(ranges, parts, ys, mend_y, mend_u, coef, us, sides=False):
    outs = [((stop - first) * ROWS, 128) for first, stop in parts]
    outs += [outs[0]] * (2 * sides)
    return pl.pallas_call(
        functools.partial(second, ranges, parts, len(ys), sides),
        in_specs=whole(len(ys) + 3 + len(us)),
        out_specs=whole(len(outs)),
        out_shape=arrays(*outs),
        scratch_shapes=[pltpu.VMEM((20 * ROWS, 128), F32)],
        compiler_params=params(),
        cost_estimate=cost(8),
        name="second",
    )(*ys, mend_y, mend_u, coef, *us)


def gather(rows_ref, table_ref, out_ref, wide_ref, picked_ref):
    @pl.loop(0, 16)
    def _(k):
        at = pl.ds(pl.multiple_of(k * 256, 256), 256)
        wide_ref[at] = table_ref[at].astype(F32)

    @pl.loop(0, 32)
    def _(k):
        for t in range(32):
            slot = k * 32 + t
            picked_ref[pl.ds(slot, 1)] = wide_ref[pl.ds(rows_ref[slot], 1)]

    mode = lax.broadcasted_iota(jnp.int32, (512, 512), 0)
    place_of = (mode // 4 % 2) * 256 + mode // 8 * 4 + mode % 4
    order = jnp.where(place_of == lanes((512, 512)), 1.0, 0.0).astype(BF16)
    for k in range(4):
        at = slice(256 * k, 256 * k + 256)
        picked = picked_ref[at].astype(BF16)
        out_ref[at] = jnp.dot(picked, order, preferred_element_type=F32).astype(BF16)


def call_gather(rows, table):
    return pl.pallas_call(
        gather,
        in_specs=[pl.BlockSpec(memory_space=pltpu.SMEM)] + whole(1),
        out_specs=whole(1)[0],
        out_shape=jax.ShapeDtypeStruct((rows.shape[0], table.shape[1]), BF16),
        scratch_shapes=[pltpu.VMEM((4096, 512), F32), pltpu.VMEM((1024, 512), F32)],
        compiler_params=params(),
        name="gather",
    )(rows, table)


def spread(count_ref, cells_ref, weights_ref, high_ref, low_ref):
    step = pl.program_id(0)
    cell = lax.broadcasted_iota(jnp.int32, (256, 1024), 0) + step * 256
    live = lax.broadcasted_iota(jnp.int32, (1, 1024), 1) < count_ref[0]
    cells = jnp.where(live, cells_ref[...], -1)
    hit = jnp.where(cells == cell, 1.0, 0.0).astype(BF16)
    total = jnp.dot(hit, weights_ref[...], preferred_element_type=F32)
    high = total.astype(BF16)
    high_ref[...] = high
    low_ref[...] = (total - high.astype(F32)).astype(BF16)


def call_spread(count, cells, weights):
    return pl.pallas_call(
        spread,
        grid=(8,),
        in_specs=[pl.BlockSpec(memory_space=pltpu.SMEM)]
        + [spec((1, 1024), lambda s: (0, 0)), spec((1024, 512), lambda s: (0, 0))],
        out_specs=[spec((256, 512), lambda s: (s, 0))] * 2,
        out_shape=[jax.ShapeDtypeStruct((2048, 512), BF16)] * 2,
        compiler_params=params(1),
        cost_estimate=pl.CostEstimate(flops=2 << 30, bytes_accessed=6 << 20, transcendentals=0),
        name="spread",
    )(count, cells, weights)


def loads(rows, w_high_ref, w_low_ref, core):
    half = pl.ds(pl.multiple_of(core * 256, 256), 256)
    sums = jnp.zeros((256, 256), F32)
    for k in range(8):
        u = jnp.concatenate([rows[2 * k][...], rows[2 * k + 1][...]], axis=1)
        u_high = u.astype(BF16)
        u_low = (u - u_high.astype(F32)).astype(BF16)
        w_high = w_high_ref[256 * k : 256 * k + 256, half]
        w_low = w_low_ref[256 * k : 256 * k + 256, half]
        sums = sums + jnp.dot(u_high, w_high, preferred_element_type=F32)
        sums = sums + jnp.dot(u_low, w_high, preferred_element_type=F32)
        sums = sums + jnp.dot(u_high, w_low, preferred_element_type=F32)
    return sums.T


def rows_of(refs):
    rows = []
    for (first, stop), ref in zip(PARTS, refs):
        rows += [ref.at[k * ROWS : (k + 1) * ROWS] for k in range(stop - first)]
    return rows


def other_loads(low_ref, mid_ref, high_ref, w_high_ref, w_low_ref, out_ref):
    core = 1 - lax.axis_index("rad") % 2
    out_ref[...] = loads(rows_of((low_ref, mid_ref, high_ref)), w_high_ref, w_low_ref, core)


def call_other_loads(low, mid, high, w_high, w_low):
    return pl.pallas_call(
        other_loads,
        in_specs=whole(5),
        out_specs=whole(1)[0],
        out_shape=arrays((256, 256))[0],
        compiler_params=params(),
        cost_estimate=pl.CostEstimate(flops=1 << 29, bytes_accessed=1 << 20, transcendentals=0),
        name="other_loads",
    )(low, mid, high, w_high, w_low)


def leave(low_ref, mid_ref, high_ref, w_high_ref, w_low_ref, out_ref, loads_ref, turned_ref, sems):
    rows = rows_of((low_ref, mid_ref, high_ref))
    copies = []
    for k, (first, stop) in enumerate(PARTS):
        for row in range(first, stop):
            turned_ref[row] = rows[row][...].T
        at = pl.ds(first, stop - first)
        copies.append(pltpu.make_async_copy(turned_ref.at[at], out_ref.at[at], sems.at[k]))
        copies[-1].start()
    loads_ref[...] = loads(rows, w_high_ref, w_low_ref, lax.axis_index("rad") % 2)
    for copy in copies:
        copy.wait()


def call_leave(low, mid, high, w_high, w_low):
    return pl.pallas_call(
        leave,
        in_specs=whole(5),
        out_specs=[pl.BlockSpec(memory_space=pltpu.HBM)] + whole(1),
        out_shape=arrays((16, 128, 256), (256, 256)),
        scratch_shapes=[pltpu.VMEM((16, 128, 256), F32), pltpu.SemaphoreType.DMA((3,))],
        compiler_params=params(),
        cost_estimate=pl.CostEstimate(flops=1 << 30, bytes_accessed=4 << 20, transcendentals=0),
        name="leave",
    )(low, mid, high, w_high, w_low)


def swaps(count, first, periodic):
    pairs = [(k, (k + 1) % count) for k in range(first, count, 2) if periodic or k + 1 < count]
    return pairs + [(target, source) for source, target in pairs]


def body(perturbation_in, coefficients, wall_cells, wall_count, mode_row, mode_table):
    n_azim, n_rad = lax.axis_size("azim"), lax.axis_size("rad")

    def swap(block, axis, odd):
        count = lax.axis_size(axis)
        return lax.ppermute(block, axis, swaps(count, odd, axis == "azim"))

    slots = wall_cells.shape[0]
    weights = call_gather(mode_row, mode_table)
    w_high, w_low = call_spread(wall_count, wall_cells.reshape(1, slots), weights)

    odd = call_ship(1, perturbation_in, coefficients)
    even = call_ship(0, perturbation_in, coefficients)
    low, mid, high = call_enter(perturbation_in)
    coef_edge, coef = call_coef_edges(coefficients)
    for step in range(STEPS):
        even = swap(even, "azim", 0)
        odd = swap(odd, "azim", 1)
        y_mid, edge = call_inner_first(low, mid, high, coef)
        if step == 0:
            edge, w_high = lax.optimization_barrier((edge, w_high))
            top, bot, own, *tails, rad_even, rad_odd = call_halo_edges(even, odd, edge, coef_edge)
        else:
            top, bot, own, rad_even, rad_odd = call_halo_edges(even, odd, edge)
        sides = swap(rad_even, "rad", 0), swap(rad_odd, "rad", 1), own
        ys = call_outer_first(top, low, high, bot, coef, *tails)
        ys = ys[0], y_mid, ys[1]
        if step == 0:
            lines = call_strip_lines(*sides)
        mends = call_strips(*sides, lines)
        if step < STEPS - 1:
            (new_mid,) = call_second(((4, 12),), PARTS[1:2], ys[1:2], *mends, coef, (mid,))
            low, high, even, odd = call_second(
                (PARTS[0], PARTS[2]), (PARTS[0], PARTS[2]), ys, *mends, coef, (low, high), sides=True
            )
            mid = new_mid
        else:
            low, mid, high = call_second(((0, 16),), PARTS, ys, *mends, coef, (low, mid, high))
    others = swap(call_other_loads(low, mid, high, w_high, w_low), "rad", 0)
    out, term = call_leave(low, mid, high, w_high, w_low)
    groups = [[k for k in range(n_azim * n_rad) if k % 2 == core] for core in range(2)]
    term = (term + others).reshape(len(groups[0]), -1, term.shape[1])
    parts = lax.all_to_all(term, ("azim", "rad"), 0, 0, axis_index_groups=groups)
    return out, jnp.sum(parts, axis=0)


def solution(mesh):
    return jax.shard_map(
        body,
        mesh=mesh,
        in_specs=(
            P("azim", "rad", None),
            P(None, None, "azim", "rad"),
            P(("azim", "rad")),
            P(("azim", "rad")),
            P(("azim", "rad")),
            P(),
        ),
        out_specs=(P("azim", "rad", None), P(("azim", "rad"), None)),
        check_vma=False,
    )
```

```python
import functools

import jax
import jax.numpy as jnp
from jax import lax
from jax.experimental import pallas as pl
from jax.experimental.pallas import tpu as pltpu
from jax.sharding import PartitionSpec as P

STEPS = 2
VMEM_LIMIT = 32 * 1024 * 1024
ENTER_LIMIT = 58 * 1024 * 1024
F32 = jnp.float32
BF16 = jnp.bfloat16


def spec(block, index):
    return pl.BlockSpec(block, index)


def whole(n):
    return [pl.BlockSpec(memory_space=pltpu.VMEM)] * n


def params(n=0):
    order = ("arbitrary",) * n if n else None
    return pltpu.CompilerParams(vmem_limit_bytes=VMEM_LIMIT, dimension_semantics=order)


def cost(rows):
    return pl.CostEstimate(flops=2 * 29 * rows * 128 * 256, bytes_accessed=rows << 18, transcendentals=0)


SMALL = pl.CostEstimate(flops=1, bytes_accessed=1, transcendentals=0)


def arrays(*shapes):
    return [jax.ShapeDtypeStruct(shape, F32) for shape in shapes]


def lanes(shape):
    return lax.broadcasted_iota(jnp.int32, shape, len(shape) - 1)


ROWS = 256
WIDTH = 32
UNROLL = 8
TAIL = 4 * ROWS
PARTS = ((0, 4), (4, 12), (12, 16))
COEF = 2 * ROWS


def window(ref, row, var, half):
    start = pl.multiple_of(row * ROWS + var * 64 + half * WIDTH, 8)
    return ref[pl.ds(start, WIDTH), :]


def put(ref, row, var, half, value):
    start = pl.multiple_of(row * ROWS + var * 64 + half * WIDTH, 8)
    ref[pl.ds(start, WIDTH), :] = value


def pick(parts, row, var, half):
    for first, stop, ref in parts:
        if first <= row < stop:
            return window(ref, row - first, var, half)
    raise IndexError(row)


def place(pack, row, value, cell):
    lane = lanes(value.shape)
    base = 4 * (row + 4)
    here = (lane >= base) & (lane < base + 4)
    return jnp.where(here, pltpu.roll(value, (base - cell) % 128, axis=1), pack)


def unplace(pack, row):
    lane = lanes(pack.shape)
    base = 4 * (row + 4)
    turned = pltpu.roll(pack, (126 - base) % 128, axis=1)
    return jnp.where((lane < 2) | (lane >= 126), turned, 0.0)


def each_part(body):
    halves = 64 // WIDTH

    @pl.loop(0, 4 * halves, unroll=UNROLL)
    def _(step):
        body(step // halves, step % halves)


def sweep(first, stop, source, weight, finish):
    for row in range(first, stop):
        sums = [None] * 5
        for i in range(5):
            u = source(row + i - 2)
            for j in range(5):
                term = weight(5 * i + j, row) * u
                sums[j] = term if i == 0 else sums[j] + term
        total = sums[2]
        for j in (0, 1, 3, 4):
            total = total + pltpu.roll(sums[j], (2 - j) % 128, axis=1)
        finish(row, total)


def turned(k, line):
    if k >= 25 or k % 5 == 2:
        return line
    lane = lanes(line.shape)
    keep = (lane < 126, lane < 127, None, lane >= 1, lane >= 2)[k % 5]
    return jnp.where(keep, pltpu.roll(line, (k % 5 - 2) % 128, axis=1), 0.0)


def line_of(coef_ref, var, k, row):
    return jnp.broadcast_to(coef_ref[var, k, row : row + 1], (WIDTH, 128))


def tail_line(ref, var, k, row):
    lines = ref.at[pl.ds(pl.multiple_of(row * 128 + var * 32, 32), 32)]
    return jnp.broadcast_to(lines[k : k + 1], (WIDTH, 128))


def sort_sides(index, even_ref, odd_ref, below_ref, above_ref):
    even_is_above = index % 2 == 0

    @pl.when(even_is_above)
    def _():
        odd_ref[...], even_ref[...] = below_ref[...], above_ref[...]

    @pl.when(jnp.logical_not(even_is_above))
    def _():
        even_ref[...], odd_ref[...] = below_ref[...], above_ref[...]


def ship(odd, x_ref, coef_ref, out_ref, coef_in, sems):
    goes_up = lax.axis_index("azim") % 2 == odd
    row = jnp.where(goes_up, 12, 0)
    coef_row = pl.multiple_of(jnp.where(goes_up, 8, 0), 8)
    state = pltpu.make_async_copy(x_ref.at[pl.ds(row, 4)], out_ref.at[pl.ds(0, 4)], sems.at[0])
    state.start()
    load = pltpu.make_async_copy(coef_ref.at[:, pl.ds(coef_row, 8)], coef_in, sems.at[1])
    load.start()
    out_ref[4] = jnp.zeros((128, 256), F32)
    load.wait()

    def fill(first):
        for var in range(4):
            for k in range(2):
                out_ref[4, 32 * var : 32 * var + 29, 128 * k : 128 * k + 128] = coef_in[
                    29 * var : 29 * var + 29, first + k, :
                ]

    pl.when(goes_up)(lambda: fill(6))
    pl.when(jnp.logical_not(goes_up))(lambda: fill(0))
    state.wait()


def call_ship(odd, x, coef):
    hbm = pl.BlockSpec(memory_space=pltpu.HBM)
    return pl.pallas_call(
        functools.partial(ship, odd),
        in_specs=[hbm] * 2,
        out_specs=whole(1)[0],
        out_shape=arrays((5, 128, 256))[0],
        scratch_shapes=[pltpu.VMEM((116, 8, 128), F32), pltpu.SemaphoreType.DMA((2,))],
        compiler_params=pltpu.CompilerParams(vmem_limit_bytes=ENTER_LIMIT),
        name="ship",
    )(x, coef.reshape(116, 16, 128))


def enter(x_ref, low_ref, mid_ref, high_ref):
    for (first, stop), ref in zip(PARTS, (low_ref, mid_ref, high_ref)):

        @pl.loop(0, stop - first)
        def _(k):
            ref[pl.ds(pl.multiple_of(k * ROWS, ROWS), ROWS)] = x_ref[first + k].T


def call_enter(x):
    return pl.pallas_call(
        enter,
        in_specs=whole(1),
        out_specs=whole(3),
        out_shape=arrays((4 * ROWS, 128), (8 * ROWS, 128), (4 * ROWS, 128)),
        compiler_params=params(),
        name="enter",
    )(x)


def inner_first(low_ref, mid_ref, high_ref, coef_ref, y_ref, edge_ref):
    parts = ((0, 4, low_ref), (4, 12, mid_ref), (12, 16, high_ref))

    def one(var, half):
        def finish(row, total):
            for w in range(4):
                total = total + line_of(coef_ref, var, 25 + w, row) * pick(parts, row, w, half)
            put(y_ref, row - 2, var, half, pick(parts, row, var, half) + 0.5 * total)

        sweep(
            2, 14, lambda s: pick(parts, s, var, half),
            lambda k, row: line_of(coef_ref, var, k, row), finish,
        )
        tail = jnp.zeros((WIDTH, 128), F32)
        head = jnp.zeros((WIDTH, 128), F32)
        for row in range(16):
            value = pick(parts, row, var, half)
            tail, head = place(tail, row, value, 124), place(head, row, value, 0)
        put(edge_ref, 0, var, half, tail)
        put(edge_ref, 1, var, half, head)

    each_part(one)


def call_inner_first(low, mid, high, coef):
    return pl.pallas_call(
        inner_first,
        in_specs=whole(4),
        out_specs=whole(2),
        out_shape=arrays((12 * ROWS, 128), (2 * ROWS, 128)),
        compiler_params=params(),
        cost_estimate=SMALL,
        name="inner_first",
    )(low, mid, high, coef)


def coef_edges(coef_ref, out_ref, turned_ref):
    @pl.loop(0, 4)
    def _(var):
        for k in range(29):
            lines = pl.ds(pl.multiple_of(var * 464 + k * 16, 16), 16)
            turned_ref[var, k] = turned(k, coef_ref[lines, :])

    out_ref[...] = jnp.zeros_like(out_ref)
    for var in range(4):
        pack = jnp.zeros((29, 128), F32)
        for row in range(16):
            pack = place(pack, row, coef_ref[pl.ds(var * 464 + row, 29, stride=16), :], 126)
        out_ref[32 * var : 32 * var + 29] = pack


def call_coef_edges(coef):
    return pl.pallas_call(
        coef_edges,
        in_specs=whole(1),
        out_specs=whole(2),
        out_shape=arrays((128, 128), coef.shape),
        compiler_params=params(),
        name="coef_edges",
    )(coef.reshape(-1, 128))


def halo_edges(odd_ref, even_ref, edge_ref, *refs):
    first_step = len(refs) > 5
    top_ref, bot_ref, out_ref = refs[first_step:][:3]
    rad_even_ref, rad_odd_ref = refs[-2:]
    even_is_above = lax.axis_index("azim") % 2 == 0

    def sorted_sides(above):
        sides = (odd_ref, even_ref) if above else (even_ref, odd_ref)
        for side, ref in zip(sides, (top_ref, bot_ref)):
            if first_step:
                for k in range(4):
                    ref[ROWS * k : ROWS * k + ROWS] = side[k].T
            else:
                ref[...] = side[...]
        if first_step:
            for side, ref in zip(sides, refs[4:6]):
                for k in range(2):
                    ref[128 * k : 128 * k + 128] = side[4, :, 128 * k : 128 * k + 128]

    pl.when(even_is_above)(lambda: sorted_sides(True))
    pl.when(jnp.logical_not(even_is_above))(lambda: sorted_sides(False))

    def one(var, half):
        tail = window(edge_ref, 0, var, half)
        head = window(edge_ref, 1, var, half)
        for k in range(4):
            for row, ref in ((k - 4, top_ref), (k + 16, bot_ref)):
                value = window(ref, k, var, half)
                tail, head = place(tail, row, value, 124), place(head, row, value, 0)
        put(out_ref, 0, var, half, tail)
        put(out_ref, 1, var, half, head)

    each_part(one)
    if first_step:
        coef_edge_ref, ctop_ref, cbot_ref = refs[0], refs[4], refs[5]
        number = lax.broadcasted_iota(jnp.int32, (32, 128), 0)
        for var in range(4):
            pack = coef_edge_ref[32 * var : 32 * var + 32]
            for k in range(2):
                at = slice(128 * k + 32 * var, 128 * k + 32 * var + 32)
                for ref, row in ((ctop_ref, k - 2), (cbot_ref, k + 16)):
                    lines = ref[at]
                    pack = place(pack, row, lines, 126)
                    result = lines
                    for j in (0, 1, 3, 4):
                        here = (number % 5 == j) & (number < 25)
                        result = jnp.where(here, turned(j, lines), result)
                    ref[at] = result
            out_ref[COEF + 32 * var : COEF + 32 * var + 32] = pack
        rad_even_ref[ROWS:] = out_ref[COEF:]
        rad_odd_ref[ROWS:] = out_ref[COEF:]
    even_is_right = lax.axis_index("rad") % 2 == 0

    @pl.when(even_is_right)
    def _():
        rad_even_ref[:ROWS], rad_odd_ref[:ROWS] = out_ref[:ROWS], out_ref[ROWS:COEF]

    @pl.when(jnp.logical_not(even_is_right))
    def _():
        rad_odd_ref[:ROWS], rad_even_ref[:ROWS] = out_ref[:ROWS], out_ref[ROWS:COEF]


def call_halo_edges(even, odd, edge, *coef_edge):
    return pl.pallas_call(
        halo_edges,
        in_specs=whole(3 + len(coef_edge)),
        out_specs=whole(5 + 2 * len(coef_edge)),
        out_shape=arrays(
            (TAIL, 128), (TAIL, 128), (COEF + 128 * len(coef_edge), 128),
            *[(256, 128)] * (2 * len(coef_edge)),
            *[(ROWS + 128 * len(coef_edge), 128)] * 2,
        ),
        compiler_params=params(),
        name="halo_edges",
    )(odd, even, edge, *coef_edge)


def outer_first(top_ref, low_ref, high_ref, bot_ref, coef_ref, ctop_ref, cbot_ref,
                y_low_ref, y_high_ref):
    parts = ((-4, 0, top_ref), (0, 4, low_ref), (12, 16, high_ref), (16, 20, bot_ref))

    def one(var, half):
        def weight(k, row):
            if row < 0:
                return tail_line(ctop_ref, var, k, row + 2)
            if row < 16:
                return line_of(coef_ref, var, k, row)
            return tail_line(cbot_ref, var, k, row - 16)

        def finish(row, total):
            for w in range(4):
                total = total + weight(25 + w, row) * pick(parts, row, w, half)
            value = pick(parts, row, var, half) + 0.5 * total
            if row < 2:
                put(y_low_ref, row + 2, var, half, value)
            else:
                put(y_high_ref, row - 14, var, half, value)

        for first in (-2, 14):
            sweep(first, first + 4, lambda s: pick(parts, s, var, half), weight, finish)

    each_part(one)


def call_outer_first(top, low, high, bot, coef, ctop, cbot):
    return pl.pallas_call(
        outer_first,
        in_specs=whole(7),
        out_specs=whole(2),
        out_shape=arrays((4 * ROWS, 128), (4 * ROWS, 128)),
        compiler_params=params(),
        cost_estimate=cost(8),
        name="outer_first",
    )(top, low, high, bot, coef, ctop, cbot)


def strip_lines(odd_ref, even_ref, own_ref, out_ref):
    entry = lanes((32, 128)) % 4
    even_is_right = lanes((32, 128)) * 0 + lax.axis_index("rad") % 2 == 0
    number = lax.broadcasted_iota(jnp.int32, (32, 128), 0)
    for var in range(4):
        at = slice(COEF + 32 * var, COEF + 32 * var + 32)
        there = slice(ROWS + 32 * var, ROWS + 32 * var + 32)
        even, odd = even_ref[there], odd_ref[there]
        right = jnp.where(even_is_right, even, odd)
        left = jnp.where(even_is_right, odd, even)
        lines = jnp.where(entry < 2, pltpu.roll(right, 126, axis=1), pltpu.roll(left, 2, axis=1))
        result = lines
        for i in (0, 1, 3, 4):
            here = (number >= 5 * i) & (number < 5 * i + 5)
            result = jnp.where(here, pltpu.roll(lines, (4 * (i - 2)) % 128, axis=1), result)
        out_ref[var, 0:32] = result
        own = own_ref.at[at]
        one_entry = entry[0:1]
        for i in range(5):
            k = 5 * i
            two = jnp.where(one_entry < 2, own[k + 4 : k + 5], own[k : k + 1])
            one = jnp.where(one_entry == 1, own[k + 3 : k + 4], 0.0)
            one = jnp.where(one_entry == 2, own[k + 1 : k + 2], one)
            turn = (4 * (i - 2)) % 128
            out_ref[var, 32 + i : 33 + i] = pltpu.roll(two, turn, axis=1) if turn else two
            out_ref[var, 37 + i : 38 + i] = pltpu.roll(one, turn, axis=1) if turn else one
        out_ref[var, 42:48] = jnp.zeros((6, 128), F32)


def call_strip_lines(even, odd, own):
    return pl.pallas_call(
        strip_lines,
        in_specs=whole(3),
        out_specs=whole(1)[0],
        out_shape=arrays((4, 48, 128))[0],
        compiler_params=params(),
        name="strip_lines",
    )(odd, even, own)


def strips(odd_ref, even_ref, own_ref, line_ref, mend_y_ref, mend_u_ref, shift_ref):
    entry = lanes((32, 128)) % 4
    even_is_right = lanes((32, 128)) * 0 + lax.axis_index("rad") % 2 == 0
    every = [(var, half) for var in range(4) for half in range(2)]

    def part(ref, kind, var, half):
        start = kind * ROWS + var * 64 + half * 32
        return ref[start : start + 32]

    def line(var, k):
        return jnp.broadcast_to(line_ref[var, k : k + 1], (32, 128))

    def turn(pack, by):
        return pltpu.roll(pack, by % 128, axis=1)

    def over_rows(sums):
        total = sums[2]
        for i in (0, 1, 3, 4):
            total = total + turn(sums[i], 4 * (2 - i))
        return total

    def beyond(var, rim, crossed):
        return over_rows([line(var, 32 + i) * rim + line(var, 37 + i) * crossed for i in range(5)])

    for var, half in every:
        at = slice(32 * half, 32 * half + 32)
        tail = jnp.where(even_is_right, part(odd_ref, 0, var, half), part(even_ref, 0, var, half))
        head = jnp.where(even_is_right, part(even_ref, 0, var, half), part(odd_ref, 0, var, half))
        rim = jnp.where(entry < 2, head, tail)
        outer = jnp.where(entry < 2, tail, head)
        own = jnp.where(entry < 2, part(own_ref, 1, var, half), part(own_ref, 0, var, half))
        up, down = turn(rim, 1), turn(rim, -1)
        shift_ref[0, var, at] = jnp.where(entry < 2, turn(own, -2), turn(outer, 2))
        shift_ref[1, var, at] = jnp.where(
            entry == 0, turn(own, -3), jnp.where(entry == 2, turn(outer, 1), up)
        )
        shift_ref[2, var, at] = rim
        shift_ref[3, var, at] = jnp.where(
            entry == 3, turn(own, 3), jnp.where(entry == 1, turn(outer, -1), down)
        )
        shift_ref[4, var, at] = jnp.where(entry < 2, turn(outer, -2), turn(own, 2))
        shift_ref[5, var, at] = jnp.where(entry == 1, up, down)
    for var, half in every:
        at = slice(32 * half, 32 * half + 32)
        mend_y_ref[var, at] = 0.5 * beyond(var, shift_ref[2, var, at], shift_ref[5, var, at])
    for var, half in every:
        at = slice(32 * half, 32 * half + 32)
        sums = []
        for i in range(5):
            total = line(var, 5 * i) * shift_ref[0, var, at]
            for j in range(1, 5):
                total = total + line(var, 5 * i + j) * shift_ref[j, var, at]
            sums.append(total)
        total = over_rows(sums)
        for w in range(4):
            total = total + line(var, 25 + w) * shift_ref[2, w, at]
        shift_ref[6, var, at] = shift_ref[2, var, at] + 0.5 * total
    for var, half in every:
        at = slice(32 * half, 32 * half + 32)
        rim = shift_ref[6, var, at]
        crossed = jnp.where(entry == 1, turn(rim, 1), turn(rim, -1))
        mend_u_ref[var, at] = beyond(var, rim, crossed)


def call_strips(even, odd, own, lines):
    return pl.pallas_call(
        strips,
        in_specs=whole(4),
        out_specs=whole(2),
        out_shape=arrays((4, 64, 128), (4, 64, 128)),
        scratch_shapes=[pltpu.VMEM((7, 4, 64, 128), F32)],
        compiler_params=params(),
        name="strips",
    )(odd, even, own, lines)


def second(ranges, parts, n_y, sides, *refs):
    y_refs, refs = refs[:n_y], refs[n_y:]
    mend_y_ref, mend_u_ref, coef_ref = refs[:3]
    u_refs, refs = refs[3 : 3 + len(parts)], refs[3 + len(parts) :]
    out_refs, refs = refs[: len(parts)], refs[len(parts) :]
    y_ref = refs[-1]
    bounds = {1: ((2, 14),), 3: ((-2, 2), (2, 14), (14, 18))}[n_y]
    y_parts = [(first, stop, ref) for (first, stop), ref in zip(bounds, y_refs)]
    u_parts = [(first, stop, ref) for (first, stop), ref in zip(parts, u_refs)]
    sources = sorted({s for first, stop in ranges for s in range(first - 2, stop + 2)})
    whole_y = ((-2, 18, y_ref),)

    def mend(var, half):
        pack = mend_y_ref[var, pl.ds(pl.multiple_of(half * WIDTH, WIDTH), WIDTH)]
        for row in sources:
            put(y_ref, row + 2, var, half, pick(y_parts, row, var, half) + unplace(pack, row))

    each_part(mend)

    def one(var, half):
        pack = mend_u_ref[var, pl.ds(pl.multiple_of(half * WIDTH, WIDTH), WIDTH)]

        def finish(row, total):
            for w in range(4):
                total = total + line_of(coef_ref, var, 25 + w, row) * pick(whole_y, row, w, half)
            total = total + unplace(pack, row)
            for (first, stop), ref in zip(parts, out_refs):
                if first <= row < stop:
                    put(ref, row - first, var, half, pick(u_parts, row, var, half) + total)

        for first, stop in ranges:
            sweep(
                first, stop, lambda s: pick(whole_y, s, var, half),
                lambda k, row: line_of(coef_ref, var, k, row), finish,
            )

    each_part(one)
    if sides:
        sort_sides(lax.axis_index("azim"), refs[0], refs[1], out_refs[0], out_refs[-1])


def call_second(ranges, parts, ys, mend_y, mend_u, coef, us, sides=False):
    outs = [((stop - first) * ROWS, 128) for first, stop in parts]
    outs += [outs[0]] * (2 * sides)
    return pl.pallas_call(
        functools.partial(second, ranges, parts, len(ys), sides),
        in_specs=whole(len(ys) + 3 + len(us)),
        out_specs=whole(len(outs)),
        out_shape=arrays(*outs),
        scratch_shapes=[pltpu.VMEM((20 * ROWS, 128), F32)],
        compiler_params=params(),
        cost_estimate=cost(8),
        name="second",
    )(*ys, mend_y, mend_u, coef, *us)


def gather(rows_ref, table_ref, out_ref, wide_ref, picked_ref):
    @pl.loop(0, 16)
    def _(k):
        at = pl.ds(pl.multiple_of(k * 256, 256), 256)
        wide_ref[at] = table_ref[at].astype(F32)

    @pl.loop(0, 32)
    def _(k):
        for t in range(32):
            slot = k * 32 + t
            picked_ref[pl.ds(slot, 1)] = wide_ref[pl.ds(rows_ref[slot], 1)]

    mode = lax.broadcasted_iota(jnp.int32, (512, 512), 0)
    place_of = (mode // 4 % 2) * 256 + mode // 8 * 4 + mode % 4
    order = jnp.where(place_of == lanes((512, 512)), 1.0, 0.0).astype(BF16)
    for k in range(4):
        at = slice(256 * k, 256 * k + 256)
        picked = picked_ref[at].astype(BF16)
        out_ref[at] = jnp.dot(picked, order, preferred_element_type=F32).astype(BF16)


def call_gather(rows, table):
    return pl.pallas_call(
        gather,
        in_specs=[pl.BlockSpec(memory_space=pltpu.SMEM)] + whole(1),
        out_specs=whole(1)[0],
        out_shape=jax.ShapeDtypeStruct((rows.shape[0], table.shape[1]), BF16),
        scratch_shapes=[pltpu.VMEM((4096, 512), F32), pltpu.VMEM((1024, 512), F32)],
        compiler_params=params(),
        name="gather",
    )(rows, table)


def spread(count_ref, cells_ref, weights_ref, high_ref, low_ref):
    step = pl.program_id(0)
    cell = lax.broadcasted_iota(jnp.int32, (256, 1024), 0) + step * 256
    live = lax.broadcasted_iota(jnp.int32, (1, 1024), 1) < count_ref[0]
    cells = jnp.where(live, cells_ref[...], -1)
    hit = jnp.where(cells == cell, 1.0, 0.0).astype(BF16)
    total = jnp.dot(hit, weights_ref[...], preferred_element_type=F32)
    high = total.astype(BF16)
    high_ref[...] = high
    low_ref[...] = (total - high.astype(F32)).astype(BF16)


def call_spread(count, cells, weights):
    return pl.pallas_call(
        spread,
        grid=(8,),
        in_specs=[pl.BlockSpec(memory_space=pltpu.SMEM)]
        + [spec((1, 1024), lambda s: (0, 0)), spec((1024, 512), lambda s: (0, 0))],
        out_specs=[spec((256, 512), lambda s: (s, 0))] * 2,
        out_shape=[jax.ShapeDtypeStruct((2048, 512), BF16)] * 2,
        compiler_params=params(1),
        cost_estimate=pl.CostEstimate(flops=2 << 30, bytes_accessed=6 << 20, transcendentals=0),
        name="spread",
    )(count, cells, weights)


def loads(rows, w_high_ref, w_low_ref, core):
    half = pl.ds(pl.multiple_of(core * 256, 256), 256)
    sums = jnp.zeros((256, 256), F32)
    for k in range(8):
        u = jnp.concatenate([rows[2 * k][...], rows[2 * k + 1][...]], axis=1)
        u_high = u.astype(BF16)
        u_low = (u - u_high.astype(F32)).astype(BF16)
        w_high = w_high_ref[256 * k : 256 * k + 256, half]
        w_low = w_low_ref[256 * k : 256 * k + 256, half]
        sums = sums + jnp.dot(u_high, w_high, preferred_element_type=F32)
        sums = sums + jnp.dot(u_low, w_high, preferred_element_type=F32)
        sums = sums + jnp.dot(u_high, w_low, preferred_element_type=F32)
    return sums.T


def rows_of(refs):
    rows = []
    for (first, stop), ref in zip(PARTS, refs):
        rows += [ref.at[k * ROWS : (k + 1) * ROWS] for k in range(stop - first)]
    return rows


def other_loads(low_ref, mid_ref, high_ref, w_high_ref, w_low_ref, out_ref):
    core = 1 - lax.axis_index("rad") % 2
    out_ref[...] = loads(rows_of((low_ref, mid_ref, high_ref)), w_high_ref, w_low_ref, core)


def call_other_loads(low, mid, high, w_high, w_low):
    return pl.pallas_call(
        other_loads,
        in_specs=whole(5),
        out_specs=whole(1)[0],
        out_shape=arrays((256, 256))[0],
        compiler_params=params(),
        cost_estimate=pl.CostEstimate(flops=1 << 29, bytes_accessed=1 << 20, transcendentals=0),
        name="other_loads",
    )(low, mid, high, w_high, w_low)


def leave(low_ref, mid_ref, high_ref, w_high_ref, w_low_ref, out_ref, loads_ref, turned_ref, sems):
    rows = rows_of((low_ref, mid_ref, high_ref))
    copies = []
    for k, (first, stop) in enumerate(PARTS):
        for row in range(first, stop):
            turned_ref[row] = rows[row][...].T
        at = pl.ds(first, stop - first)
        copies.append(pltpu.make_async_copy(turned_ref.at[at], out_ref.at[at], sems.at[k]))
        copies[-1].start()
    loads_ref[...] = loads(rows, w_high_ref, w_low_ref, lax.axis_index("rad") % 2)
    for copy in copies:
        copy.wait()


def call_leave(low, mid, high, w_high, w_low):
    return pl.pallas_call(
        leave,
        in_specs=whole(5),
        out_specs=[pl.BlockSpec(memory_space=pltpu.HBM)] + whole(1),
        out_shape=arrays((16, 128, 256), (256, 256)),
        scratch_shapes=[pltpu.VMEM((16, 128, 256), F32), pltpu.SemaphoreType.DMA((3,))],
        compiler_params=params(),
        cost_estimate=pl.CostEstimate(flops=1 << 30, bytes_accessed=4 << 20, transcendentals=0),
        name="leave",
    )(low, mid, high, w_high, w_low)


def swaps(count, first, periodic):
    pairs = [(k, (k + 1) % count) for k in range(first, count, 2) if periodic or k + 1 < count]
    return pairs + [(target, source) for source, target in pairs]


def body(perturbation_in, coefficients, wall_cells, wall_count, mode_row, mode_table):
    n_azim, n_rad = lax.axis_size("azim"), lax.axis_size("rad")

    def swap(block, axis, odd):
        count = lax.axis_size(axis)
        return lax.ppermute(block, axis, swaps(count, odd, axis == "azim"))

    slots = wall_cells.shape[0]
    weights = call_gather(mode_row, mode_table)
    w_high, w_low = call_spread(wall_count, wall_cells.reshape(1, slots), weights)

    odd = call_ship(1, perturbation_in, coefficients)
    even = call_ship(0, perturbation_in, coefficients)
    low, mid, high = call_enter(perturbation_in)
    coef_edge, coef = call_coef_edges(coefficients)
    for step in range(STEPS):
        even = swap(even, "azim", 0)
        odd = swap(odd, "azim", 1)
        y_mid, edge = call_inner_first(low, mid, high, coef)
        if step == 0:
            edge, w_high = lax.optimization_barrier((edge, w_high))
            top, bot, own, *tails, rad_even, rad_odd = call_halo_edges(even, odd, edge, coef_edge)
        else:
            top, bot, own, rad_even, rad_odd = call_halo_edges(even, odd, edge)
        sides = swap(rad_even, "rad", 0), swap(rad_odd, "rad", 1), own
        ys = call_outer_first(top, low, high, bot, coef, *tails)
        ys = ys[0], y_mid, ys[1]
        if step == 0:
            lines = call_strip_lines(*sides)
        mends = call_strips(*sides, lines)
        if step < STEPS - 1:
            (new_mid,) = call_second(((4, 12),), PARTS[1:2], ys[1:2], *mends, coef, (mid,))
            low, high, even, odd = call_second(
                (PARTS[0], PARTS[2]), (PARTS[0], PARTS[2]), ys, *mends, coef, (low, high), sides=True
            )
            mid = new_mid
        else:
            low, mid, high = call_second(((0, 16),), PARTS, ys, *mends, coef, (low, mid, high))
    others = swap(call_other_loads(low, mid, high, w_high, w_low), "rad", 0)
    out, term = call_leave(low, mid, high, w_high, w_low)
    groups = [[k for k in range(n_azim * n_rad) if k % 2 == core] for core in range(2)]
    term = (term + others).reshape(len(groups[0]), -1, term.shape[1])
    parts = lax.all_to_all(term, ("azim", "rad"), 0, 0, axis_index_groups=groups)
    return out, jnp.sum(parts, axis=0)


def solution(mesh):
    return jax.shard_map(
        body,
        mesh=mesh,
        in_specs=(
            P("azim", "rad", None),
            P(None, None, "azim", "rad"),
            P(("azim", "rad")),
            P(("azim", "rad")),
            P(("azim", "rad")),
            P(),
        ),
        out_specs=(P("azim", "rad", None), P(("azim", "rad"), None)),
        check_vma=False,
    )
```

```python
import functools

import jax
import jax.numpy as jnp
from jax import lax
from jax.experimental import pallas as pl
from jax.experimental.pallas import tpu as pltpu
from jax.sharding import PartitionSpec as P

STEPS = 2
VMEM_LIMIT = 32 * 1024 * 1024
ENTER_LIMIT = 58 * 1024 * 1024
F32 = jnp.float32
BF16 = jnp.bfloat16


def spec(block, index):
    return pl.BlockSpec(block, index)


def whole(n):
    return [pl.BlockSpec(memory_space=pltpu.VMEM)] * n


def params(n=0):
    order = ("arbitrary",) * n if n else None
    return pltpu.CompilerParams(vmem_limit_bytes=VMEM_LIMIT, dimension_semantics=order)


def cost(rows):
    return pl.CostEstimate(flops=2 * 29 * rows * 128 * 256, bytes_accessed=rows << 18, transcendentals=0)


SMALL = pl.CostEstimate(flops=1, bytes_accessed=1, transcendentals=0)


def arrays(*shapes):
    return [jax.ShapeDtypeStruct(shape, F32) for shape in shapes]


def lanes(shape):
    return lax.broadcasted_iota(jnp.int32, shape, len(shape) - 1)


ROWS = 256
WIDTH = 32
UNROLL = 8
TAIL = 4 * ROWS
PARTS = ((0, 4), (4, 12), (12, 16))
COEF = 2 * ROWS


def window(ref, row, var, half):
    start = pl.multiple_of(row * ROWS + var * 64 + half * WIDTH, 8)
    return ref[pl.ds(start, WIDTH), :]


def put(ref, row, var, half, value):
    start = pl.multiple_of(row * ROWS + var * 64 + half * WIDTH, 8)
    ref[pl.ds(start, WIDTH), :] = value


def pick(parts, row, var, half):
    for first, stop, ref in parts:
        if first <= row < stop:
            return window(ref, row - first, var, half)
    raise IndexError(row)


def place(pack, row, value, cell):
    lane = lanes(value.shape)
    base = 4 * (row + 4)
    here = (lane >= base) & (lane < base + 4)
    return jnp.where(here, pltpu.roll(value, (base - cell) % 128, axis=1), pack)


def unplace(pack, row):
    lane = lanes(pack.shape)
    base = 4 * (row + 4)
    turned = pltpu.roll(pack, (126 - base) % 128, axis=1)
    return jnp.where((lane < 2) | (lane >= 126), turned, 0.0)


def each_part(body):
    halves = 64 // WIDTH

    @pl.loop(0, 4 * halves, unroll=UNROLL)
    def _(step):
        body(step // halves, step % halves)


def sweep(first, stop, source, weight, finish):
    for row in range(first, stop):
        sums = [None] * 5
        for i in range(5):
            u = source(row + i - 2)
            for j in range(5):
                term = weight(5 * i + j, row) * u
                sums[j] = term if i == 0 else sums[j] + term
        total = sums[2]
        for j in (0, 1, 3, 4):
            total = total + pltpu.roll(sums[j], (2 - j) % 128, axis=1)
        finish(row, total)


def turned(k, line):
    if k >= 25 or k % 5 == 2:
        return line
    lane = lanes(line.shape)
    keep = (lane < 126, lane < 127, None, lane >= 1, lane >= 2)[k % 5]
    return jnp.where(keep, pltpu.roll(line, (k % 5 - 2) % 128, axis=1), 0.0)


def line_of(coef_ref, var, k, row):
    return jnp.broadcast_to(coef_ref[var, k, row : row + 1], (WIDTH, 128))


def tail_line(ref, var, k, row):
    lines = ref.at[pl.ds(pl.multiple_of(row * 128 + var * 32, 32), 32)]
    return jnp.broadcast_to(lines[k : k + 1], (WIDTH, 128))


def sort_sides(index, even_ref, odd_ref, below_ref, above_ref):
    even_is_above = index % 2 == 0

    @pl.when(even_is_above)
    def _():
        odd_ref[...], even_ref[...] = below_ref[...], above_ref[...]

    @pl.when(jnp.logical_not(even_is_above))
    def _():
        even_ref[...], odd_ref[...] = below_ref[...], above_ref[...]


def ship(odd, x_ref, coef_ref, out_ref, coef_in, sems):
    goes_up = lax.axis_index("azim") % 2 == odd
    row = jnp.where(goes_up, 12, 0)
    coef_row = pl.multiple_of(jnp.where(goes_up, 8, 0), 8)
    state = pltpu.make_async_copy(x_ref.at[pl.ds(row, 4)], out_ref.at[pl.ds(0, 4)], sems.at[0])
    state.start()
    load = pltpu.make_async_copy(coef_ref.at[:, pl.ds(coef_row, 8)], coef_in, sems.at[1])
    load.start()
    out_ref[4] = jnp.zeros((128, 256), F32)
    load.wait()

    def fill(first):
        for var in range(4):
            for k in range(2):
                out_ref[4, 32 * var : 32 * var + 29, 128 * k : 128 * k + 128] = coef_in[
                    29 * var : 29 * var + 29, first + k, :
                ]

    pl.when(goes_up)(lambda: fill(6))
    pl.when(jnp.logical_not(goes_up))(lambda: fill(0))
    state.wait()


def call_ship(odd, x, coef):
    hbm = pl.BlockSpec(memory_space=pltpu.HBM)
    return pl.pallas_call(
        functools.partial(ship, odd),
        in_specs=[hbm] * 2,
        out_specs=whole(1)[0],
        out_shape=arrays((5, 128, 256))[0],
        scratch_shapes=[pltpu.VMEM((116, 8, 128), F32), pltpu.SemaphoreType.DMA((2,))],
        compiler_params=pltpu.CompilerParams(vmem_limit_bytes=ENTER_LIMIT),
        name="ship",
    )(x, coef.reshape(116, 16, 128))


def enter(x_ref, low_ref, mid_ref, high_ref):
    for (first, stop), ref in zip(PARTS, (low_ref, mid_ref, high_ref)):

        @pl.loop(0, stop - first)
        def _(k):
            ref[pl.ds(pl.multiple_of(k * ROWS, ROWS), ROWS)] = x_ref[first + k].T


def call_enter(x):
    return pl.pallas_call(
        enter,
        in_specs=whole(1),
        out_specs=whole(3),
        out_shape=arrays((4 * ROWS, 128), (8 * ROWS, 128), (4 * ROWS, 128)),
        compiler_params=params(),
        name="enter",
    )(x)


def inner_first(low_ref, mid_ref, high_ref, coef_ref, y_ref, edge_ref):
    parts = ((0, 4, low_ref), (4, 12, mid_ref), (12, 16, high_ref))

    def one(var, half):
        def finish(row, total):
            for w in range(4):
                total = total + line_of(coef_ref, var, 25 + w, row) * pick(parts, row, w, half)
            put(y_ref, row - 2, var, half, pick(parts, row, var, half) + 0.5 * total)

        sweep(
            2, 14, lambda s: pick(parts, s, var, half),
            lambda k, row: line_of(coef_ref, var, k, row), finish,
        )
        tail = jnp.zeros((WIDTH, 128), F32)
        head = jnp.zeros((WIDTH, 128), F32)
        for row in range(16):
            value = pick(parts, row, var, half)
            tail, head = place(tail, row, value, 124), place(head, row, value, 0)
        put(edge_ref, 0, var, half, tail)
        put(edge_ref, 1, var, half, head)

    each_part(one)


def call_inner_first(low, mid, high, coef):
    return pl.pallas_call(
        inner_first,
        in_specs=whole(4),
        out_specs=whole(2),
        out_shape=arrays((12 * ROWS, 128), (2 * ROWS, 128)),
        compiler_params=params(),
        cost_estimate=SMALL,
        name="inner_first",
    )(low, mid, high, coef)


def coef_edges(coef_ref, out_ref, turned_ref):
    @pl.loop(0, 4)
    def _(var):
        for k in range(29):
            lines = pl.ds(pl.multiple_of(var * 464 + k * 16, 16), 16)
            turned_ref[var, k] = turned(k, coef_ref[lines, :])

    out_ref[...] = jnp.zeros_like(out_ref)
    for var in range(4):
        pack = jnp.zeros((29, 128), F32)
        for row in range(16):
            pack = place(pack, row, coef_ref[pl.ds(var * 464 + row, 29, stride=16), :], 126)
        out_ref[32 * var : 32 * var + 29] = pack


def call_coef_edges(coef):
    return pl.pallas_call(
        coef_edges,
        in_specs=whole(1),
        out_specs=whole(2),
        out_shape=arrays((128, 128), coef.shape),
        compiler_params=params(),
        name="coef_edges",
    )(coef.reshape(-1, 128))


def halo_edges(odd_ref, even_ref, edge_ref, *refs):
    first_step = len(refs) > 5
    top_ref, bot_ref, out_ref = refs[first_step:][:3]
    rad_even_ref, rad_odd_ref = refs[-2:]
    even_is_above = lax.axis_index("azim") % 2 == 0

    def sorted_sides(above):
        sides = (odd_ref, even_ref) if above else (even_ref, odd_ref)
        for side, ref in zip(sides, (top_ref, bot_ref)):
            if first_step:
                for k in range(4):
                    ref[ROWS * k : ROWS * k + ROWS] = side[k].T
            else:
                ref[...] = side[...]
        if first_step:
            for side, ref in zip(sides, refs[4:6]):
                for k in range(2):
                    ref[128 * k : 128 * k + 128] = side[4, :, 128 * k : 128 * k + 128]

    pl.when(even_is_above)(lambda: sorted_sides(True))
    pl.when(jnp.logical_not(even_is_above))(lambda: sorted_sides(False))

    def one(var, half):
        tail = window(edge_ref, 0, var, half)
        head = window(edge_ref, 1, var, half)
        for k in range(4):
            for row, ref in ((k - 4, top_ref), (k + 16, bot_ref)):
                value = window(ref, k, var, half)
                tail, head = place(tail, row, value, 124), place(head, row, value, 0)
        put(out_ref, 0, var, half, tail)
        put(out_ref, 1, var, half, head)

    each_part(one)
    if first_step:
        coef_edge_ref, ctop_ref, cbot_ref = refs[0], refs[4], refs[5]
        number = lax.broadcasted_iota(jnp.int32, (32, 128), 0)
        for var in range(4):
            pack = coef_edge_ref[32 * var : 32 * var + 32]
            for k in range(2):
                at = slice(128 * k + 32 * var, 128 * k + 32 * var + 32)
                for ref, row in ((ctop_ref, k - 2), (cbot_ref, k + 16)):
                    lines = ref[at]
                    pack = place(pack, row, lines, 126)
                    result = lines
                    for j in (0, 1, 3, 4):
                        here = (number % 5 == j) & (number < 25)
                        result = jnp.where(here, turned(j, lines), result)
                    ref[at] = result
            out_ref[COEF + 32 * var : COEF + 32 * var + 32] = pack
        rad_even_ref[ROWS:] = out_ref[COEF:]
        rad_odd_ref[ROWS:] = out_ref[COEF:]
    even_is_right = lax.axis_index("rad") % 2 == 0

    @pl.when(even_is_right)
    def _():
        rad_even_ref[:ROWS], rad_odd_ref[:ROWS] = out_ref[:ROWS], out_ref[ROWS:COEF]

    @pl.when(jnp.logical_not(even_is_right))
    def _():
        rad_odd_ref[:ROWS], rad_even_ref[:ROWS] = out_ref[:ROWS], out_ref[ROWS:COEF]


def call_halo_edges(even, odd, edge, *coef_edge):
    return pl.pallas_call(
        halo_edges,
        in_specs=whole(3 + len(coef_edge)),
        out_specs=whole(5 + 2 * len(coef_edge)),
        out_shape=arrays(
            (TAIL, 128), (TAIL, 128), (COEF + 128 * len(coef_edge), 128),
            *[(256, 128)] * (2 * len(coef_edge)),
            *[(ROWS + 128 * len(coef_edge), 128)] * 2,
        ),
        compiler_params=params(),
        name="halo_edges",
    )(odd, even, edge, *coef_edge)


def outer_first(top_ref, low_ref, high_ref, bot_ref, coef_ref, ctop_ref, cbot_ref,
                y_low_ref, y_high_ref):
    parts = ((-4, 0, top_ref), (0, 4, low_ref), (12, 16, high_ref), (16, 20, bot_ref))

    def one(var, half):
        def weight(k, row):
            if row < 0:
                return tail_line(ctop_ref, var, k, row + 2)
            if row < 16:
                return line_of(coef_ref, var, k, row)
            return tail_line(cbot_ref, var, k, row - 16)

        def finish(row, total):
            for w in range(4):
                total = total + weight(25 + w, row) * pick(parts, row, w, half)
            value = pick(parts, row, var, half) + 0.5 * total
            if row < 2:
                put(y_low_ref, row + 2, var, half, value)
            else:
                put(y_high_ref, row - 14, var, half, value)

        for first in (-2, 14):
            sweep(first, first + 4, lambda s: pick(parts, s, var, half), weight, finish)

    each_part(one)


def call_outer_first(top, low, high, bot, coef, ctop, cbot):
    return pl.pallas_call(
        outer_first,
        in_specs=whole(7),
        out_specs=whole(2),
        out_shape=arrays((4 * ROWS, 128), (4 * ROWS, 128)),
        compiler_params=params(),
        cost_estimate=cost(8),
        name="outer_first",
    )(top, low, high, bot, coef, ctop, cbot)


def strip_lines(even_ref, odd_ref, own_ref, out_ref):
    entry = lanes((32, 128)) % 4
    even_is_right = lanes((32, 128)) * 0 + lax.axis_index("rad") % 2 == 0
    number = lax.broadcasted_iota(jnp.int32, (32, 128), 0)
    for var in range(4):
        at = slice(COEF + 32 * var, COEF + 32 * var + 32)
        there = slice(ROWS + 32 * var, ROWS + 32 * var + 32)
        even, odd = even_ref[there], odd_ref[there]
        right = jnp.where(even_is_right, even, odd)
        left = jnp.where(even_is_right, odd, even)
        lines = jnp.where(entry < 2, pltpu.roll(right, 126, axis=1), pltpu.roll(left, 2, axis=1))
        result = lines
        for i in (0, 1, 3, 4):
            here = (number >= 5 * i) & (number < 5 * i + 5)
            result = jnp.where(here, pltpu.roll(lines, (4 * (i - 2)) % 128, axis=1), result)
        out_ref[var, 0:32] = result
        own = own_ref.at[at]
        one_entry = entry[0:1]
        for i in range(5):
            k = 5 * i
            two = jnp.where(one_entry < 2, own[k + 4 : k + 5], own[k : k + 1])
            one = jnp.where(one_entry == 1, own[k + 3 : k + 4], 0.0)
            one = jnp.where(one_entry == 2, own[k + 1 : k + 2], one)
            turn = (4 * (i - 2)) % 128
            out_ref[var, 32 + i : 33 + i] = pltpu.roll(two, turn, axis=1) if turn else two
            out_ref[var, 37 + i : 38 + i] = pltpu.roll(one, turn, axis=1) if turn else one
        out_ref[var, 42:48] = jnp.zeros((6, 128), F32)


def call_strip_lines(even, odd, own):
    return pl.pallas_call(
        strip_lines,
        in_specs=whole(3),
        out_specs=whole(1)[0],
        out_shape=arrays((4, 48, 128))[0],
        compiler_params=params(),
        name="strip_lines",
    )(even, odd, own)


def strips(even_ref, odd_ref, own_ref, line_ref, mend_y_ref, mend_u_ref, shift_ref):
    entry = lanes((32, 128)) % 4
    even_is_right = lanes((32, 128)) * 0 + lax.axis_index("rad") % 2 == 0
    every = [(var, half) for var in range(4) for half in range(2)]

    def part(ref, kind, var, half):
        start = kind * ROWS + var * 64 + half * 32
        return ref[start : start + 32]

    def line(var, k):
        return jnp.broadcast_to(line_ref[var, k : k + 1], (32, 128))

    def turn(pack, by):
        return pltpu.roll(pack, by % 128, axis=1)

    def over_rows(sums):
        total = sums[2]
        for i in (0, 1, 3, 4):
            total = total + turn(sums[i], 4 * (2 - i))
        return total

    def beyond(var, rim, crossed):
        return over_rows([line(var, 32 + i) * rim + line(var, 37 + i) * crossed for i in range(5)])

    for var, half in every:
        at = slice(32 * half, 32 * half + 32)
        tail = jnp.where(even_is_right, part(odd_ref, 0, var, half), part(even_ref, 0, var, half))
        head = jnp.where(even_is_right, part(even_ref, 0, var, half), part(odd_ref, 0, var, half))
        rim = jnp.where(entry < 2, head, tail)
        outer = jnp.where(entry < 2, tail, head)
        own = jnp.where(entry < 2, part(own_ref, 1, var, half), part(own_ref, 0, var, half))
        up, down = turn(rim, 1), turn(rim, -1)
        shift_ref[0, var, at] = jnp.where(entry < 2, turn(own, -2), turn(outer, 2))
        shift_ref[1, var, at] = jnp.where(
            entry == 0, turn(own, -3), jnp.where(entry == 2, turn(outer, 1), up)
        )
        shift_ref[2, var, at] = rim
        shift_ref[3, var, at] = jnp.where(
            entry == 3, turn(own, 3), jnp.where(entry == 1, turn(outer, -1), down)
        )
        shift_ref[4, var, at] = jnp.where(entry < 2, turn(outer, -2), turn(own, 2))
        shift_ref[5, var, at] = jnp.where(entry == 1, up, down)
    for var, half in every:
        at = slice(32 * half, 32 * half + 32)
        mend_y_ref[var, at] = 0.5 * beyond(var, shift_ref[2, var, at], shift_ref[5, var, at])
    for var, half in every:
        at = slice(32 * half, 32 * half + 32)
        sums = []
        for i in range(5):
            total = line(var, 5 * i) * shift_ref[0, var, at]
            for j in range(1, 5):
                total = total + line(var, 5 * i + j) * shift_ref[j, var, at]
            sums.append(total)
        total = over_rows(sums)
        for w in range(4):
            total = total + line(var, 25 + w) * shift_ref[2, w, at]
        shift_ref[6, var, at] = shift_ref[2, var, at] + 0.5 * total
    for var, half in every:
        at = slice(32 * half, 32 * half + 32)
        rim = shift_ref[6, var, at]
        crossed = jnp.where(entry == 1, turn(rim, 1), turn(rim, -1))
        mend_u_ref[var, at] = beyond(var, rim, crossed)


def call_strips(even, odd, own, lines):
    return pl.pallas_call(
        strips,
        in_specs=whole(4),
        out_specs=whole(2),
        out_shape=arrays((4, 64, 128), (4, 64, 128)),
        scratch_shapes=[pltpu.VMEM((7, 4, 64, 128), F32)],
        compiler_params=params(),
        name="strips",
    )(even, odd, own, lines)


def second(ranges, parts, n_y, sides, *refs):
    y_refs, refs = refs[:n_y], refs[n_y:]
    mend_y_ref, mend_u_ref, coef_ref = refs[:3]
    u_refs, refs = refs[3 : 3 + len(parts)], refs[3 + len(parts) :]
    out_refs, refs = refs[: len(parts)], refs[len(parts) :]
    y_ref = refs[-1]
    bounds = {1: ((2, 14),), 3: ((-2, 2), (2, 14), (14, 18))}[n_y]
    y_parts = [(first, stop, ref) for (first, stop), ref in zip(bounds, y_refs)]
    u_parts = [(first, stop, ref) for (first, stop), ref in zip(parts, u_refs)]
    sources = sorted({s for first, stop in ranges for s in range(first - 2, stop + 2)})
    whole_y = ((-2, 18, y_ref),)

    def mend(var, half):
        pack = mend_y_ref[var, pl.ds(pl.multiple_of(half * WIDTH, WIDTH), WIDTH)]
        for row in sources:
            put(y_ref, row + 2, var, half, pick(y_parts, row, var, half) + unplace(pack, row))

    each_part(mend)

    def one(var, half):
        pack = mend_u_ref[var, pl.ds(pl.multiple_of(half * WIDTH, WIDTH), WIDTH)]

        def finish(row, total):
            for w in range(4):
                total = total + line_of(coef_ref, var, 25 + w, row) * pick(whole_y, row, w, half)
            total = total + unplace(pack, row)
            for (first, stop), ref in zip(parts, out_refs):
                if first <= row < stop:
                    put(ref, row - first, var, half, pick(u_parts, row, var, half) + total)

        for first, stop in ranges:
            sweep(
                first, stop, lambda s: pick(whole_y, s, var, half),
                lambda k, row: line_of(coef_ref, var, k, row), finish,
            )

    each_part(one)
    if sides:
        sort_sides(lax.axis_index("azim"), refs[0], refs[1], out_refs[0], out_refs[-1])


def call_second(ranges, parts, ys, mend_y, mend_u, coef, us, sides=False):
    outs = [((stop - first) * ROWS, 128) for first, stop in parts]
    outs += [outs[0]] * (2 * sides)
    return pl.pallas_call(
        functools.partial(second, ranges, parts, len(ys), sides),
        in_specs=whole(len(ys) + 3 + len(us)),
        out_specs=whole(len(outs)),
        out_shape=arrays(*outs),
        scratch_shapes=[pltpu.VMEM((20 * ROWS, 128), F32)],
        compiler_params=params(),
        cost_estimate=cost(8),
        name="second",
    )(*ys, mend_y, mend_u, coef, *us)


def gather(rows_ref, table_ref, out_ref, wide_ref, picked_ref):
    @pl.loop(0, 16)
    def _(k):
        at = pl.ds(pl.multiple_of(k * 256, 256), 256)
        wide_ref[at] = table_ref[at].astype(F32)

    @pl.loop(0, 32)
    def _(k):
        for t in range(32):
            slot = k * 32 + t
            picked_ref[pl.ds(slot, 1)] = wide_ref[pl.ds(rows_ref[slot], 1)]

    mode = lax.broadcasted_iota(jnp.int32, (512, 512), 0)
    place_of = (mode // 4 % 2) * 256 + mode // 8 * 4 + mode % 4
    order = jnp.where(place_of == lanes((512, 512)), 1.0, 0.0).astype(BF16)
    for k in range(4):
        at = slice(256 * k, 256 * k + 256)
        picked = picked_ref[at].astype(BF16)
        out_ref[at] = jnp.dot(picked, order, preferred_element_type=F32).astype(BF16)


def call_gather(rows, table):
    return pl.pallas_call(
        gather,
        in_specs=[pl.BlockSpec(memory_space=pltpu.SMEM)] + whole(1),
        out_specs=whole(1)[0],
        out_shape=jax.ShapeDtypeStruct((rows.shape[0], table.shape[1]), BF16),
        scratch_shapes=[pltpu.VMEM((4096, 512), F32), pltpu.VMEM((1024, 512), F32)],
        compiler_params=params(),
        name="gather",
    )(rows, table)


def spread(count_ref, cells_ref, weights_ref, high_ref, low_ref):
    step = pl.program_id(0)
    cell = lax.broadcasted_iota(jnp.int32, (256, 1024), 0) + step * 256
    live = lax.broadcasted_iota(jnp.int32, (1, 1024), 1) < count_ref[0]
    cells = jnp.where(live, cells_ref[...], -1)
    hit = jnp.where(cells == cell, 1.0, 0.0).astype(BF16)
    total = jnp.dot(hit, weights_ref[...], preferred_element_type=F32)
    high = total.astype(BF16)
    high_ref[...] = high
    low_ref[...] = (total - high.astype(F32)).astype(BF16)


def call_spread(count, cells, weights):
    return pl.pallas_call(
        spread,
        grid=(8,),
        in_specs=[pl.BlockSpec(memory_space=pltpu.SMEM)]
        + [spec((1, 1024), lambda s: (0, 0)), spec((1024, 512), lambda s: (0, 0))],
        out_specs=[spec((256, 512), lambda s: (s, 0))] * 2,
        out_shape=[jax.ShapeDtypeStruct((2048, 512), BF16)] * 2,
        compiler_params=params(1),
        cost_estimate=pl.CostEstimate(flops=2 << 30, bytes_accessed=6 << 20, transcendentals=0),
        name="spread",
    )(count, cells, weights)


def loads(rows, w_high_ref, w_low_ref, core):
    half = pl.ds(pl.multiple_of(core * 256, 256), 256)
    sums = jnp.zeros((256, 256), F32)
    for k in range(8):
        u = jnp.concatenate([rows[2 * k][...], rows[2 * k + 1][...]], axis=1)
        u_high = u.astype(BF16)
        u_low = (u - u_high.astype(F32)).astype(BF16)
        w_high = w_high_ref[256 * k : 256 * k + 256, half]
        w_low = w_low_ref[256 * k : 256 * k + 256, half]
        sums = sums + jnp.dot(u_high, w_high, preferred_element_type=F32)
        sums = sums + jnp.dot(u_low, w_high, preferred_element_type=F32)
        sums = sums + jnp.dot(u_high, w_low, preferred_element_type=F32)
    return sums.T


def rows_of(refs):
    rows = []
    for (first, stop), ref in zip(PARTS, refs):
        rows += [ref.at[k * ROWS : (k + 1) * ROWS] for k in range(stop - first)]
    return rows


def other_loads(low_ref, mid_ref, high_ref, w_high_ref, w_low_ref, out_ref):
    core = 1 - lax.axis_index("rad") % 2
    out_ref[...] = loads(rows_of((low_ref, mid_ref, high_ref)), w_high_ref, w_low_ref, core)


def call_other_loads(low, mid, high, w_high, w_low):
    return pl.pallas_call(
        other_loads,
        in_specs=whole(5),
        out_specs=whole(1)[0],
        out_shape=arrays((256, 256))[0],
        compiler_params=params(),
        cost_estimate=pl.CostEstimate(flops=1 << 29, bytes_accessed=1 << 20, transcendentals=0),
        name="other_loads",
    )(low, mid, high, w_high, w_low)


def leave(low_ref, mid_ref, high_ref, w_high_ref, w_low_ref, out_ref, loads_ref, turned_ref, sems):
    rows = rows_of((low_ref, mid_ref, high_ref))
    copies = []
    for k, (first, stop) in enumerate(PARTS):
        for row in range(first, stop):
            turned_ref[row] = rows[row][...].T
        at = pl.ds(first, stop - first)
        copies.append(pltpu.make_async_copy(turned_ref.at[at], out_ref.at[at], sems.at[k]))
        copies[-1].start()
    loads_ref[...] = loads(rows, w_high_ref, w_low_ref, lax.axis_index("rad") % 2)
    for copy in copies:
        copy.wait()


def call_leave(low, mid, high, w_high, w_low):
    return pl.pallas_call(
        leave,
        in_specs=whole(5),
        out_specs=[pl.BlockSpec(memory_space=pltpu.HBM)] + whole(1),
        out_shape=arrays((16, 128, 256), (256, 256)),
        scratch_shapes=[pltpu.VMEM((16, 128, 256), F32), pltpu.SemaphoreType.DMA((3,))],
        compiler_params=params(),
        cost_estimate=pl.CostEstimate(flops=1 << 30, bytes_accessed=4 << 20, transcendentals=0),
        name="leave",
    )(low, mid, high, w_high, w_low)


def swaps(count, first, periodic):
    pairs = [(k, (k + 1) % count) for k in range(first, count, 2) if periodic or k + 1 < count]
    return pairs + [(target, source) for source, target in pairs]


def body(perturbation_in, coefficients, wall_cells, wall_count, mode_row, mode_table):
    n_azim, n_rad = lax.axis_size("azim"), lax.axis_size("rad")

    def swap(block, axis, odd):
        count = lax.axis_size(axis)
        return lax.ppermute(block, axis, swaps(count, odd, axis == "azim"))

    slots = wall_cells.shape[0]
    weights = call_gather(mode_row, mode_table)
    w_high, w_low = call_spread(wall_count, wall_cells.reshape(1, slots), weights)

    odd = call_ship(1, perturbation_in, coefficients)
    even = call_ship(0, perturbation_in, coefficients)
    low, mid, high = call_enter(perturbation_in)
    coef_edge, coef = call_coef_edges(coefficients)
    for step in range(STEPS):
        even = swap(even, "azim", 0)
        odd = swap(odd, "azim", 1)
        y_mid, edge = call_inner_first(low, mid, high, coef)
        if step == 0:
            edge, w_high = lax.optimization_barrier((edge, w_high))
            top, bot, own, *tails, rad_even, rad_odd = call_halo_edges(even, odd, edge, coef_edge)
        else:
            top, bot, own, rad_even, rad_odd = call_halo_edges(even, odd, edge)
        sides = swap(rad_even, "rad", 0), swap(rad_odd, "rad", 1), own
        ys = call_outer_first(top, low, high, bot, coef, *tails)
        ys = ys[0], y_mid, ys[1]
        if step == 0:
            lines = call_strip_lines(*sides)
        mends = call_strips(*sides, lines)
        if step < STEPS - 1:
            (new_mid,) = call_second(((4, 12),), PARTS[1:2], ys[1:2], *mends, coef, (mid,))
            low, high, even, odd = call_second(
                (PARTS[0], PARTS[2]), (PARTS[0], PARTS[2]), ys, *mends, coef, (low, high), sides=True
            )
            mid = new_mid
        else:
            low, mid, high = call_second(((0, 16),), PARTS, ys, *mends, coef, (low, mid, high))
    others = swap(call_other_loads(low, mid, high, w_high, w_low), "rad", 0)
    out, term = call_leave(low, mid, high, w_high, w_low)
    groups = [[k for k in range(n_azim * n_rad) if k % 2 == core] for core in range(2)]
    columns = term.shape[1]
    term = (term + others).reshape(len(groups[0]), -1, 128)
    parts = lax.all_to_all(term, ("azim", "rad"), 0, 0, axis_index_groups=groups)
    return out, jnp.sum(parts, axis=0).reshape(-1, columns)


def solution(mesh):
    return jax.shard_map(
        body,
        mesh=mesh,
        in_specs=(
            P("azim", "rad", None),
            P(None, None, "azim", "rad"),
            P(("azim", "rad")),
            P(("azim", "rad")),
            P(("azim", "rad")),
            P(),
        ),
        out_specs=(P("azim", "rad", None), P(("azim", "rad"), None)),
        check_vma=False,
    )
```
